32 devices in a mesh: groups: 2 (over y), dp: 4 (over z), layer: 2 (over x), sub: 2 (over core).
Axes of the slice: x: 2, y: 2, z: 4, core: 2. Of those that a mesh axis runs over, the one named last changes fastest.
Arguments:
- acts: bfloat16 [2, 2048, 4096], P('layer', ('groups', 'dp')), parts along dimension 1, may hold values from -6 to 6
- kv_grad: bfloat16 [2, 2048, 2048], P('layer', ('groups', 'dp'), 'sub'), parts along dimension 1, may hold values from -6 to 6
- kv_weight: bfloat16 [2, 4096, 2048], P('layer', 'dp', 'sub'), may hold values from -0.125 to 0.125
- proj_in: bfloat16 [4096, 64], replicated, may hold values from -0.09375 to 0.09375
- proj_out: bfloat16 [4096, 64], replicated, may hold values from -0.09375 to 0.09375
- codebook: bfloat16 [512, 256, 8], P('sub'), may hold values from -5 to 5
- codes: int32 [2048, 2, 512], P(('groups', 'dp'), 'layer', 'sub'), parts along dimension 0, may hold values from 0 to 255
- counts: int32 [8], P(('groups', 'dp')), parts along dimension 0, may hold values from 1 to 256, 512 in all
Outputs:
- scores: float32 [2048, 16], P(('groups', 'dp')), parts along dimension 0
The draws below stay inside these ranges and needn't reach their ends.
There are 2 independent parts, one for each index of `groups`. The reference program is written for one: setup_inputs(seed, part) draws one part's arguments, and reference() takes and returns one part's arrays. A program takes and returns all parts, laid end to end along the dimension named above; an argument that names none is the same for every part. Nothing has to cross between parts.
Inputs may be any that keep to these rules, and one draw needn't show every extreme that they name: `counts`: one block of 256 slots is full in every draw.
All inputs are finite; a program needn't handle non-finite values.
Results may differ from the reference program's by a relative error of at most 0.003.
Values may be sent and summed in bfloat16 or wider, within the bound.
No kernel may reach another device: no remote copies, remote signals or barrier semaphores. Data moves between devices by JAX's collectives and lax.ppermute only.
A program may use at most 128 MiB of HBM per device.

```python
import math
import jax
import jax.numpy as jnp
import numpy as np
from jax import lax

D = 4096
KV2 = 2048
RANK = 64
SUBDIM = 8
CODES = 256
M = 512
SEQ = 64
TRAIN_DEV = 256
LAYERS = 2
TOKENS = 1024
NTRAIN = 1024
N_DP = 4


def plant(entries, key, least, high):
    extent = entries.shape
    spot = [jax.random.randint(jax.random.fold_in(key, axis), (), 0, extent[axis]) for axis in range(len(extent))]
    entries = entries.at[tuple(spot)].set(least)
    longest = extent.index(max(extent))
    spot[longest] = (spot[longest] + 1) % extent[longest]
    return entries.at[tuple(spot)].set(high)


def block_scale(key, dims, pieces, smallest, top_value):
    factor_of, own = 1.0, jax.random.fold_in(key, 6)
    for axis_at, shards_of in pieces:
        draws = jnp.exp(jax.random.uniform(jax.random.fold_in(own, axis_at), (shards_of,), jnp.float32, smallest / len(pieces), top_value / len(pieces)))
        factor_of = factor_of * jnp.repeat(draws, dims[axis_at] // shards_of).reshape([-1 if axis == axis_at else 1 for axis in range(len(dims))])
    return factor_of


def split_up(count, total, bound, lean):
    weights = [(1 << 20) // math.isqrt(rank ** lean) + 1 for rank in range(2, count + 1)]
    surplus, given = total - bound - (count - 1), [1] * (count - 1)
    while surplus > 0:
        candidates = [i for i in range(count - 1) if given[i] < bound]
        pool, budget = sum([weights[i] for i in candidates]), surplus
        for i in candidates:
            extra = min(bound - given[i], max(1, budget * weights[i] // pool), surplus)
            given[i] = given[i] + extra
            surplus = surplus - extra
    return np.array([bound] + given)


def ragged(stream_key, count, total, most, lean):
    if count == 2:
        one = jax.random.randint(stream_key, (), max(1, total - most), min(most, total - 1) + 1)
        return jnp.stack([one, total - one])
    tallies = jnp.asarray(split_up(count, total, most, lean), jnp.int32)
    twos = (count - 1) // 2
    source_of, taker = tallies[1:1 + 2 * twos:2], tallies[2:2 + 2 * twos:2]
    slack = jnp.minimum(source_of - 1, most - taker)
    shifted = jax.random.randint(jax.random.fold_in(stream_key, 1), (twos,), 0, 1 << 20) % (slack + 1)
    tallies = tallies.at[1:1 + 2 * twos:2].set(source_of - shifted).at[2:2 + 2 * twos:2].set(taker + shifted)
    return tallies[jax.random.permutation(jax.random.fold_in(stream_key, 2), count)]


def noise(key, extent, deviation, most, cuts=(), held_as=jnp.bfloat16):
    drawn = deviation * jax.random.normal(key, extent, jnp.float32)
    if cuts:
        drawn = drawn * block_scale(key, extent, cuts, -0.22, 0.18)
    return jnp.clip(drawn, -most, most).astype(held_as)


def setup_inputs(seed: int = 0, part: int = 0) -> dict:
    key_list = jax.random.split(jax.random.key(seed), 9)
    part_splits = jax.random.split(jax.random.fold_in(key_list[8], part), 9)
    return {
        "acts": noise(part_splits[0], (LAYERS, TOKENS, D), 1.0, 6.0, ((0, 2), (1, 4))),
        "kv_grad": noise(part_splits[1], (LAYERS, TOKENS, KV2), 1.0, 6.0, ((0, 2), (1, 4), (2, 2))),
        "kv_weight": noise(key_list[2], (LAYERS, D, KV2), KV2 ** -0.5, 0.125, ((0, 2), (1, 4), (2, 2))),
        "proj_in": noise(key_list[3], (D, RANK), D ** -0.5, 0.09375),
        "proj_out": noise(key_list[4], (D, RANK), D ** -0.5, 0.09375),
        "codebook": noise(key_list[5], (M, CODES, SUBDIM), 1.0, 5.0, ((0, 2),)),
        "codes": plant(jax.random.randint(part_splits[6], (NTRAIN, LAYERS, M), 0, CODES), jax.random.fold_in(part_splits[6], 1), 0, CODES - 1).astype(jnp.int32),
        "counts": ragged(part_splits[7], N_DP, N_DP * TRAIN_DEV // 2, TRAIN_DEV, 2).astype(jnp.int32),
    }


def reference(acts, kv_grad, kv_weight, proj_in, proj_out, codebook, codes, counts):
    num_layers, num_tokens, model_width = acts.shape
    rank_dim = proj_in.shape[1]
    num_tests = num_tokens // SEQ
    sub_count, code_count, sub_width = codebook.shape
    train_rows = codes.shape[0]
    per_block = train_rows // counts.shape[0]
    row_ids = jnp.arange(train_rows, dtype=jnp.int32)
    block_ids = row_ids // per_block
    live_rows = row_ids % per_block < counts[block_ids]
    score_total = jnp.zeros((train_rows, num_tests), jnp.float32)
    book_f = codebook.astype(jnp.float32)
    for layer_idx in range(num_layers):
        input_grad = jnp.dot(kv_grad[layer_idx], kv_weight[layer_idx].T, preferred_element_type=jnp.float32)
        out_side = jnp.dot(input_grad, proj_out.astype(jnp.float32), precision=lax.Precision.HIGHEST)
        in_side = jnp.dot(acts[layer_idx], proj_in, preferred_element_type=jnp.float32)
        grads = jnp.einsum('esi,esj->eij', in_side.reshape(num_tests, SEQ, rank_dim), out_side.reshape(num_tests, SEQ, rank_dim), precision=lax.Precision.HIGHEST).reshape(num_tests, rank_dim * rank_dim)
        vectors = grads * lax.rsqrt(lax.optimization_barrier(jnp.mean(grads * grads, axis=1, keepdims=True)) + 1e-06) / rank_dim
        tables = jnp.einsum('emd,mkd->emk', vectors.reshape(num_tests, sub_count, sub_width), book_f, precision=lax.Precision.HIGHEST).astype(jnp.bfloat16)
        table_t = jnp.transpose(tables, (1, 2, 0)).astype(jnp.float32)
        picked = table_t[jnp.arange(sub_count, dtype=jnp.int32)[None, :], codes[:, layer_idx, :]]
        score_total = score_total + lax.optimization_barrier(jnp.sum(picked, axis=1))
    return jnp.where(live_rows[:, None], score_total, jnp.float32(0.0))
```

```python
import jax
import jax.numpy as jnp
from jax import lax
from jax.experimental import pallas as pl
from jax.experimental.pallas import tpu as pltpu
from jax.sharding import PartitionSpec as P

SEQ = 64
LANES = 128
LINK_SCALE = 1024.0


def decode_kernel(codes_ref, book_ref, out_ref):
    subs, width, code_count = book_ref.shape
    slots = codes_ref.shape[1]

    def eight(step, carry):
        first = pl.multiple_of(step * 8, 8)
        ids = codes_ref[pl.ds(first, 8), :]
        low = ids & (LANES - 1)
        for pair in range(0, 8, 2):
            halves = []
            for sub in (pair, pair + 1):
                table = book_ref[first + sub].astype(jnp.float32)
                columns = []
                for left in range(0, slots, LANES):
                    own = jnp.broadcast_to(ids[sub : sub + 1, left : left + LANES], (width, LANES))
                    spot = jnp.broadcast_to(low[sub : sub + 1, left : left + LANES], (width, LANES))
                    picked = None
                    for part in range(0, code_count, LANES):
                        found = jnp.take_along_axis(
                            table[:, part : part + LANES], spot, axis=1, mode="promise_in_bounds"
                        )
                        picked = found if picked is None else jnp.where(own >= part, found, picked)
                    columns.append(picked)
                halves.append(jnp.concatenate(columns, axis=1))
            rows = pl.multiple_of((first + pair) * width, 2 * width)
            out_ref[pl.ds(rows, 2 * width), :] = jnp.concatenate(halves, axis=0).astype(jnp.bfloat16)
        return carry

    lax.fori_loop(0, subs // 8, eight, 0)


def decode(codes_t, book_t):
    subs, width, _ = book_t.shape
    slots = codes_t.shape[1]
    return pl.pallas_call(
        decode_kernel,
        out_shape=jax.ShapeDtypeStruct((subs * width, slots), jnp.bfloat16),
        in_specs=[pl.BlockSpec(memory_space=pltpu.VMEM)] * 2,
        out_specs=pl.BlockSpec(memory_space=pltpu.VMEM),
        compiler_params=pltpu.CompilerParams(vmem_limit_bytes=16 * 1024 * 1024),
        cost_estimate=pl.CostEstimate(flops=0, bytes_accessed=2 * 1024 * 1024, transcendentals=0),
        name="decode",
    )(codes_t, book_t)


def split_high_low(x):
    high = lax.reduce_precision(x, 8, 7)
    return high.astype(jnp.bfloat16), (x - high).astype(jnp.bfloat16)


def partners(size, step):
    return [(i, i ^ step) for i in range(size)]


def is_power_of_two(n):
    return n & (n - 1) == 0


def sum_over_dp(x):
    size = lax.axis_size("dp")
    if not is_power_of_two(size):
        return lax.psum(x, "dp")
    step = 1
    while step < size:
        sent = (x * LINK_SCALE).astype(jnp.float16)
        x = x + lax.ppermute(sent, "dp", partners(size, step)).astype(jnp.float32) * (1.0 / LINK_SCALE)
        step *= 2
    return x


def gather_over_dp(x):
    size = lax.axis_size("dp")
    if size > 4 or not is_power_of_two(size):
        return lax.all_gather(x, "dp", axis=0)
    own = lax.axis_index("dp")
    got = jnp.zeros((size,) + x.shape, x.dtype)
    got = lax.dynamic_update_index_in_dim(got, x, own, 0)
    for step in range(1, size):
        block = lax.ppermute(x, "dp", partners(size, step))
        got = lax.dynamic_update_index_in_dim(got, block, own ^ step, 0)
    return got


def sum_over_layer_sub(x):
    if lax.axis_size("layer") != 2 or lax.axis_size("sub") != 2:
        return lax.psum(x, ("layer", "sub"))
    by_sub = lax.ppermute(x, "sub", partners(2, 1))
    by_layer = lax.ppermute(x, "layer", partners(2, 1))
    by_both = lax.ppermute(x, ("layer", "sub"), partners(4, 3))
    return (x + by_sub) + (by_layer + by_both)


def per_device(acts, kv_grad, kv_weight, proj_in, proj_out, codebook, codes, counts):
    tok_local = acts.shape[1]
    rank_dim = proj_in.shape[1]
    sub_local, code_count, sub_width = codebook.shape
    train_local = codes.shape[0]
    tests_local = tok_local // SEQ
    rows_local = kv_weight.shape[1]
    dims_local = sub_local * sub_width
    live_rows = jnp.arange(train_local, dtype=jnp.int32) < counts[0]

    own_rows = lax.dynamic_slice_in_dim(proj_out, lax.axis_index("dp") * rows_local, rows_local, 0)
    folded = lax.dot_general(
        own_rows, kv_weight[0], (((0,), (0,)), ((), ())), preferred_element_type=jnp.float32
    )
    folded = sum_over_dp(folded)
    out_side = lax.dot_general(
        jnp.concatenate(split_high_low(folded), axis=0),
        kv_grad[0],
        (((1,), (1,)), ((), ())),
        preferred_element_type=jnp.float32,
    )
    out_side = out_side[:rank_dim] + out_side[rank_dim:]
    out_side = lax.psum(out_side, "sub") if lax.axis_size("sub") != 2 else (
        out_side + lax.ppermute(out_side, "sub", partners(2, 1))
    )
    in_side = lax.dot_general(
        proj_in, acts[0], (((0,), (1,)), ((), ())), preferred_element_type=jnp.float32
    )
    grads = jnp.einsum(
        "ies,jes->eij",
        in_side.reshape(rank_dim, tests_local, SEQ),
        out_side.reshape(rank_dim, tests_local, SEQ),
        precision=lax.Precision.HIGHEST,
    ).reshape(tests_local, rank_dim * rank_dim)
    vectors = grads * lax.rsqrt(jnp.mean(grads * grads, axis=1, keepdims=True) + 1e-06) / rank_dim
    own_part = lax.dynamic_slice_in_dim(vectors, lax.axis_index("sub") * dims_local, dims_local, 1)
    every = gather_over_dp(own_part).reshape(-1, dims_local)
    tests_all = every.shape[0]

    decoded = decode(jnp.transpose(codes[:, 0, :]), jnp.transpose(codebook, (0, 2, 1)))
    layer_scores = jnp.dot(
        jnp.concatenate(split_high_low(every), axis=0), decoded, preferred_element_type=jnp.float32
    )
    layer_scores = layer_scores[:tests_all] + layer_scores[tests_all:]
    total = sum_over_layer_sub(layer_scores)
    return jnp.transpose(jnp.where(live_rows[None, :], total, jnp.float32(0.0)))


def solution(mesh):
    return jax.shard_map(
        per_device,
        mesh=mesh,
        in_specs=(
            P("layer", ("groups", "dp"), None),
            P("layer", ("groups", "dp"), "sub"),
            P("layer", "dp", "sub"),
            P(),
            P(),
            P("sub", None, None),
            P(("groups", "dp"), "layer", "sub"),
            P(("groups", "dp")),
        ),
        out_specs=P(("groups", "dp"), None),
        check_vma=False,
    )
```

```python
import jax
import jax.numpy as jnp
from jax import lax
from jax.experimental import pallas as pl
from jax.experimental.pallas import tpu as pltpu
from jax.sharding import PartitionSpec as P

SEQ = 64
LANES = 128
LINK_SCALE = 1024.0


def decode_kernel(codes_ref, book_ref, out_ref):
    subs, width, code_count = book_ref.shape
    slots = codes_ref.shape[1]

    def eight(step, carry):
        first = pl.multiple_of(step * 8, 8)
        ids = codes_ref[pl.ds(first, 8), :]
        low = ids & (LANES - 1)
        for pair in range(0, 8, 2):
            halves = []
            for sub in (pair, pair + 1):
                table = book_ref[first + sub].astype(jnp.float32)
                columns = []
                for left in range(0, slots, LANES):
                    own = jnp.broadcast_to(ids[sub : sub + 1, left : left + LANES], (width, LANES))
                    spot = jnp.broadcast_to(low[sub : sub + 1, left : left + LANES], (width, LANES))
                    picked = None
                    for part in range(0, code_count, LANES):
                        found = jnp.take_along_axis(
                            table[:, part : part + LANES], spot, axis=1, mode="promise_in_bounds"
                        )
                        picked = found if picked is None else jnp.where(own >= part, found, picked)
                    columns.append(picked)
                halves.append(jnp.concatenate(columns, axis=1))
            rows = pl.multiple_of((first + pair) * width, 2 * width)
            out_ref[pl.ds(rows, 2 * width), :] = jnp.concatenate(halves, axis=0).astype(jnp.bfloat16)
        return carry

    lax.fori_loop(0, subs // 8, eight, 0)


def decode(codes_t, book_t):
    subs, width, _ = book_t.shape
    slots = codes_t.shape[1]
    return pl.pallas_call(
        decode_kernel,
        out_shape=jax.ShapeDtypeStruct((subs * width, slots), jnp.bfloat16),
        in_specs=[pl.BlockSpec(memory_space=pltpu.VMEM)] * 2,
        out_specs=pl.BlockSpec(memory_space=pltpu.VMEM),
        compiler_params=pltpu.CompilerParams(vmem_limit_bytes=16 * 1024 * 1024),
        cost_estimate=pl.CostEstimate(flops=0, bytes_accessed=2 * 1024 * 1024, transcendentals=0),
        name="decode",
    )(codes_t, book_t)


def split_high_low(x):
    high = lax.reduce_precision(x, 8, 7)
    return high.astype(jnp.bfloat16), (x - high).astype(jnp.bfloat16)


def partners(size, step):
    return [(i, i ^ step) for i in range(size)]


def is_power_of_two(n):
    return n & (n - 1) == 0


def sum_over_dp(x, beside):
    size = lax.axis_size("dp")
    beside = list(beside)
    made = []
    if not is_power_of_two(size):
        return lax.psum(x, "dp"), [work() for work in beside]
    step = 1
    while step < size:
        got = lax.ppermute((x * LINK_SCALE).astype(jnp.float16), "dp", partners(size, step))
        if beside:
            got, done = lax.optimization_barrier((got, beside.pop(0)()))
            made.append(done)
        x = x + got.astype(jnp.float32) * (1.0 / LINK_SCALE)
        step *= 2
    return x, made + [work() for work in beside]


def gather_over_dp(x):
    size = lax.axis_size("dp")
    if size > 4 or not is_power_of_two(size):
        return lax.all_gather(x, "dp", axis=0)
    own = lax.axis_index("dp")
    got = jnp.zeros((size,) + x.shape, x.dtype)
    got = lax.dynamic_update_index_in_dim(got, x, own, 0)
    for step in range(1, size):
        block = lax.ppermute(x, "dp", partners(size, step))
        got = lax.dynamic_update_index_in_dim(got, block, own ^ step, 0)
    return got


def sum_over_layer_sub(x):
    if lax.axis_size("layer") != 2 or lax.axis_size("sub") != 2:
        return lax.psum(x, ("layer", "sub"))
    by_sub = lax.ppermute(x, "sub", partners(2, 1))
    by_layer = lax.ppermute(x, "layer", partners(2, 1))
    by_both = lax.ppermute(x, ("layer", "sub"), partners(4, 3))
    return (x + by_sub) + (by_layer + by_both)


def per_device(acts, kv_grad, kv_weight, proj_in, proj_out, codebook, codes, counts):
    tok_local = acts.shape[1]
    rank_dim = proj_in.shape[1]
    sub_local, code_count, sub_width = codebook.shape
    train_local = codes.shape[0]
    tests_local = tok_local // SEQ
    rows_local = kv_weight.shape[1]
    dims_local = sub_local * sub_width
    live_rows = jnp.arange(train_local, dtype=jnp.int32) < counts[0]

    own_rows = lax.dynamic_slice_in_dim(proj_out, lax.axis_index("dp") * rows_local, rows_local, 0)
    folded = lax.dot_general(
        own_rows, kv_weight[0], (((0,), (0,)), ((), ())), preferred_element_type=jnp.float32
    )
    folded, (in_side, decoded) = sum_over_dp(
        folded,
        [
            lambda: lax.dot_general(
                proj_in, acts[0], (((0,), (1,)), ((), ())), preferred_element_type=jnp.float32
            ),
            lambda: decode(jnp.transpose(codes[:, 0, :]), jnp.transpose(codebook, (0, 2, 1))),
        ],
    )
    out_side = lax.dot_general(
        jnp.concatenate(split_high_low(folded), axis=0),
        kv_grad[0],
        (((1,), (1,)), ((), ())),
        preferred_element_type=jnp.float32,
    )
    out_side = out_side[:rank_dim] + out_side[rank_dim:]
    out_side = lax.psum(out_side, "sub") if lax.axis_size("sub") != 2 else (
        out_side + lax.ppermute(out_side, "sub", partners(2, 1))
    )
    grads = jnp.einsum(
        "ies,jes->eij",
        in_side.reshape(rank_dim, tests_local, SEQ),
        out_side.reshape(rank_dim, tests_local, SEQ),
        precision=lax.Precision.HIGHEST,
    ).reshape(tests_local, rank_dim * rank_dim)
    vectors = grads * lax.rsqrt(jnp.mean(grads * grads, axis=1, keepdims=True) + 1e-06) / rank_dim
    own_part = lax.dynamic_slice_in_dim(vectors, lax.axis_index("sub") * dims_local, dims_local, 1)
    every = gather_over_dp(own_part).reshape(-1, dims_local)
    tests_all = every.shape[0]

    layer_scores = jnp.dot(
        jnp.concatenate(split_high_low(every), axis=0), decoded, preferred_element_type=jnp.float32
    )
    layer_scores = layer_scores[:tests_all] + layer_scores[tests_all:]
    total = sum_over_layer_sub(layer_scores)
    return jnp.transpose(jnp.where(live_rows[None, :], total, jnp.float32(0.0)))


def solution(mesh):
    return jax.shard_map(
        per_device,
        mesh=mesh,
        in_specs=(
            P("layer", ("groups", "dp"), None),
            P("layer", ("groups", "dp"), "sub"),
            P("layer", "dp", "sub"),
            P(),
            P(),
            P("sub", None, None),
            P(("groups", "dp"), "layer", "sub"),
            P(("groups", "dp")),
        ),
        out_specs=P(("groups", "dp"), None),
        check_vma=False,
    )
```

```python
import jax
import jax.numpy as jnp
from jax import lax
from jax.experimental import pallas as pl
from jax.experimental.pallas import tpu as pltpu
from jax.sharding import PartitionSpec as P

SEQ = 64
LANES = 128
LINK_SCALE = 1024.0


def decode_kernel(codes_ref, book_ref, out_ref, ids_ref):
    subs, width, code_count = book_ref.shape
    slots = codes_ref.shape[0]
    for left in range(0, slots, LANES):
        for top in range(0, subs, LANES):
            block = codes_ref[left : left + LANES, 0, top : top + LANES]
            ids_ref[top : top + LANES, left : left + LANES] = jnp.transpose(block)

    def eight(step, carry):
        first = pl.multiple_of(step * 8, 8)
        ids = ids_ref[pl.ds(first, 8), :]
        low = ids & (LANES - 1)
        for pair in range(0, 8, 2):
            halves = []
            for sub in (pair, pair + 1):
                table = book_ref[first + sub].astype(jnp.float32)
                columns = []
                for left in range(0, slots, LANES):
                    own = jnp.broadcast_to(ids[sub : sub + 1, left : left + LANES], (width, LANES))
                    spot = jnp.broadcast_to(low[sub : sub + 1, left : left + LANES], (width, LANES))
                    picked = None
                    for part in range(0, code_count, LANES):
                        found = jnp.take_along_axis(
                            table[:, part : part + LANES], spot, axis=1, mode="promise_in_bounds"
                        )
                        picked = found if picked is None else jnp.where(own >= part, found, picked)
                    columns.append(picked)
                halves.append(jnp.concatenate(columns, axis=1))
            rows = pl.multiple_of((first + pair) * width, 2 * width)
            out_ref[pl.ds(rows, 2 * width), :] = jnp.concatenate(halves, axis=0).astype(jnp.bfloat16)
        return carry

    lax.fori_loop(0, subs // 8, eight, 0)


def decode(codes, book_t):
    slots, _, subs = codes.shape
    width = book_t.shape[1]
    return pl.pallas_call(
        decode_kernel,
        out_shape=jax.ShapeDtypeStruct((subs * width, slots), jnp.bfloat16),
        in_specs=[pl.BlockSpec(memory_space=pltpu.VMEM)] * 2,
        out_specs=pl.BlockSpec(memory_space=pltpu.VMEM),
        scratch_shapes=[pltpu.VMEM((subs, slots), jnp.int32)],
        compiler_params=pltpu.CompilerParams(vmem_limit_bytes=8 * 1024 * 1024),
        cost_estimate=pl.CostEstimate(flops=0, bytes_accessed=2 * 1024 * 1024, transcendentals=0),
        name="decode",
    )(codes, book_t)


def split_high_low(x):
    high = lax.reduce_precision(x, 8, 7)
    return high.astype(jnp.bfloat16), (x - high).astype(jnp.bfloat16)


def partners(size, step):
    return [(i, i ^ step) for i in range(size)]


def is_power_of_two(n):
    return n & (n - 1) == 0


def sum_over_dp(x, beside):
    size = lax.axis_size("dp")
    beside = list(beside)
    made = []
    if not is_power_of_two(size):
        return lax.psum(x, "dp"), [work() for work in beside]
    step = 1
    while step < size:
        got = lax.ppermute((x * LINK_SCALE).astype(jnp.float16), "dp", partners(size, step))
        if beside:
            got, done = lax.optimization_barrier((got, beside.pop(0)()))
            made.append(done)
        x = x + got.astype(jnp.float32) * (1.0 / LINK_SCALE)
        step *= 2
    return x, made + [work() for work in beside]


def gather_over_dp(x):
    size = lax.axis_size("dp")
    if size > 4 or not is_power_of_two(size):
        return lax.all_gather(x, "dp", axis=0)
    own = lax.axis_index("dp")
    got = jnp.zeros((size,) + x.shape, x.dtype)
    got = lax.dynamic_update_index_in_dim(got, x, own, 0)
    for step in range(1, size):
        block = lax.ppermute(x, "dp", partners(size, step))
        got = lax.dynamic_update_index_in_dim(got, block, own ^ step, 0)
    return got


def sum_over_layer_sub(x):
    if lax.axis_size("layer") != 2 or lax.axis_size("sub") != 2:
        return lax.psum(x, ("layer", "sub"))
    by_sub = lax.ppermute(x, "sub", partners(2, 1))
    by_layer = lax.ppermute(x, "layer", partners(2, 1))
    by_both = lax.ppermute(x, ("layer", "sub"), partners(4, 3))
    return (x + by_sub) + (by_layer + by_both)


def per_device(acts, kv_grad, kv_weight, proj_in, proj_out, codebook, codes, counts):
    tok_local = acts.shape[1]
    rank_dim = proj_in.shape[1]
    sub_local, code_count, sub_width = codebook.shape
    train_local = codes.shape[0]
    tests_local = tok_local // SEQ
    rows_local = kv_weight.shape[1]
    dims_local = sub_local * sub_width
    live_rows = jnp.arange(train_local, dtype=jnp.int32) < counts[0]

    own_rows = lax.dynamic_slice_in_dim(proj_out, lax.axis_index("dp") * rows_local, rows_local, 0)
    folded = lax.dot_general(
        own_rows, kv_weight[0], (((0,), (0,)), ((), ())), preferred_element_type=jnp.float32
    )
    folded, ((live, in_side), decoded) = sum_over_dp(
        folded,
        [
            lambda: (
                jnp.broadcast_to(live_rows, (8, train_local)).astype(jnp.float32),
                lax.dot_general(
                    proj_in, acts[0], (((0,), (1,)), ((), ())), preferred_element_type=jnp.float32
                ),
            ),
            lambda: decode(codes, jnp.transpose(codebook, (0, 2, 1))),
        ],
    )
    out_side = lax.dot_general(
        jnp.concatenate(split_high_low(folded), axis=0),
        kv_grad[0],
        (((1,), (1,)), ((), ())),
        preferred_element_type=jnp.float32,
    )
    out_side = out_side[:rank_dim] + out_side[rank_dim:]
    out_side = lax.psum(out_side, "sub") if lax.axis_size("sub") != 2 else (
        out_side + lax.ppermute(out_side, "sub", partners(2, 1))
    )
    grads = jnp.einsum(
        "ies,jes->eij",
        in_side.reshape(rank_dim, tests_local, SEQ),
        out_side.reshape(rank_dim, tests_local, SEQ),
        precision=lax.Precision.HIGHEST,
    ).reshape(tests_local, rank_dim * rank_dim)
    vectors = grads * lax.rsqrt(jnp.mean(grads * grads, axis=1, keepdims=True) + 1e-06) / rank_dim
    own_part = lax.dynamic_slice_in_dim(vectors, lax.axis_index("sub") * dims_local, dims_local, 1)
    every = gather_over_dp(own_part).reshape(-1, dims_local)
    tests_all = every.shape[0]

    layer_scores = jnp.dot(
        jnp.concatenate(split_high_low(every), axis=0), decoded, preferred_element_type=jnp.float32
    )
    layer_scores = layer_scores[:tests_all] + layer_scores[tests_all:]
    total = sum_over_layer_sub(layer_scores)
    return jnp.transpose(jnp.where(live[:1] > 0.0, total, jnp.float32(0.0)))


def solution(mesh):
    return jax.shard_map(
        per_device,
        mesh=mesh,
        in_specs=(
            P("layer", ("groups", "dp"), None),
            P("layer", ("groups", "dp"), "sub"),
            P("layer", "dp", "sub"),
            P(),
            P(),
            P("sub", None, None),
            P(("groups", "dp"), "layer", "sub"),
            P(("groups", "dp")),
        ),
        out_specs=P(("groups", "dp"), None),
        check_vma=False,
    )
```

```python
import jax
import jax.numpy as jnp
from jax import lax
from jax.experimental import pallas as pl
from jax.experimental.pallas import tpu as pltpu
from jax.sharding import PartitionSpec as P

SEQ = 64
LANES = 128
LINK_SCALE = 1024.0
VECTOR_SCALE = 16384.0


def decode_kernel(codes_ref, book_ref, out_ref, ids_ref):
    subs, width, code_count = book_ref.shape
    slots = codes_ref.shape[0]
    for left in range(0, slots, LANES):
        for top in range(0, subs, LANES):
            block = codes_ref[left : left + LANES, 0, top : top + LANES]
            ids_ref[top : top + LANES, left : left + LANES] = jnp.transpose(block)

    def eight(step, carry):
        first = pl.multiple_of(step * 8, 8)
        ids = ids_ref[pl.ds(first, 8), :]
        low = ids & (LANES - 1)
        for pair in range(0, 8, 2):
            halves = []
            for sub in (pair, pair + 1):
                table = book_ref[first + sub].astype(jnp.float32)
                columns = []
                for left in range(0, slots, LANES):
                    own = jnp.broadcast_to(ids[sub : sub + 1, left : left + LANES], (width, LANES))
                    spot = jnp.broadcast_to(low[sub : sub + 1, left : left + LANES], (width, LANES))
                    picked = None
                    for part in range(0, code_count, LANES):
                        found = jnp.take_along_axis(
                            table[:, part : part + LANES], spot, axis=1, mode="promise_in_bounds"
                        )
                        picked = found if picked is None else jnp.where(own >= part, found, picked)
                    columns.append(picked)
                halves.append(jnp.concatenate(columns, axis=1))
            rows = pl.multiple_of((first + pair) * width, 2 * width)
            out_ref[pl.ds(rows, 2 * width), :] = jnp.concatenate(halves, axis=0).astype(jnp.bfloat16)
        return carry

    lax.fori_loop(0, subs // 8, eight, 0)


def decode(codes, book_t):
    slots, _, subs = codes.shape
    width = book_t.shape[1]
    return pl.pallas_call(
        decode_kernel,
        out_shape=jax.ShapeDtypeStruct((subs * width, slots), jnp.bfloat16),
        in_specs=[pl.BlockSpec(memory_space=pltpu.VMEM)] * 2,
        out_specs=pl.BlockSpec(memory_space=pltpu.VMEM),
        scratch_shapes=[pltpu.VMEM((subs, slots), jnp.int32)],
        compiler_params=pltpu.CompilerParams(vmem_limit_bytes=8 * 1024 * 1024),
        cost_estimate=pl.CostEstimate(flops=0, bytes_accessed=2 * 1024 * 1024, transcendentals=0),
        name="decode",
    )(codes, book_t)


def vectors_kernel(in_ref, own_ref, other_ref, out_ref, grads_ref, flat_ref):
    rank_dim, tokens = in_ref.shape
    tests, dims = out_ref.shape
    pairs = rank_dim // 2
    tall = dims // LANES
    in_side = in_ref[...]
    test_of = lax.broadcasted_iota(jnp.int32, in_side.shape, 1) // SEQ
    grads_ref[:, :rank_dim] = lax.dot_general(
        jnp.concatenate([jnp.where(test_of == test, in_side, 0.0) for test in range(tests)], axis=0),
        own_ref[...] + other_ref[...],
        (((1,), (1,)), ((), ())),
        precision=lax.Precision.HIGHEST,
        preferred_element_type=jnp.float32,
    )
    for test in range(tests):
        even = grads_ref[pl.ds(test * rank_dim, pairs, stride=2), :][:, :rank_dim]
        odd = grads_ref[pl.ds(test * rank_dim + 1, pairs, stride=2), :][:, :rank_dim]
        both = jnp.concatenate([even, odd], axis=1)
        squares = jnp.sum(jnp.sum(both * both, axis=0, keepdims=True), axis=1, keepdims=True)
        mean = squares * (1.0 / (rank_dim * rank_dim))
        flat_ref[test * pairs : (test + 1) * pairs, :] = both * (lax.rsqrt(mean + 1e-06) / rank_dim)
    first = lax.axis_index("sub") * tall
    for row in range(tall):
        out_ref[:, row * LANES : (row + 1) * LANES] = flat_ref[
            pl.ds(first + row, tests, stride=pairs), :
        ]


def make_vectors(in_side, own, other, dims_local):
    rank_dim, tokens = in_side.shape
    tests = tokens // SEQ
    return pl.pallas_call(
        vectors_kernel,
        out_shape=jax.ShapeDtypeStruct((tests, dims_local), jnp.float32),
        in_specs=[pl.BlockSpec(memory_space=pltpu.VMEM)] * 3,
        out_specs=pl.BlockSpec(memory_space=pltpu.VMEM),
        scratch_shapes=[
            pltpu.VMEM((tests * rank_dim, LANES), jnp.float32),
            pltpu.VMEM((tests * rank_dim // 2, LANES), jnp.float32),
        ],
        compiler_params=pltpu.CompilerParams(vmem_limit_bytes=4 * 1024 * 1024),
        name="vectors",
    )(in_side, own, other)


def split_high_low(x):
    high = lax.reduce_precision(x, 8, 7)
    return high.astype(jnp.bfloat16), (x - high).astype(jnp.bfloat16)


def partners(size, step):
    return [(i, i ^ step) for i in range(size)]


def is_power_of_two(n):
    return n & (n - 1) == 0


def sum_over_dp(x, beside):
    size = lax.axis_size("dp")
    beside = list(beside)
    made = []
    if not is_power_of_two(size):
        return lax.psum(x, "dp"), [work() for work in beside]
    step = 1
    while step < size:
        got = lax.ppermute((x * LINK_SCALE).astype(jnp.float16), "dp", partners(size, step))
        if beside:
            got, done = lax.optimization_barrier((got, beside.pop(0)()))
            made.append(done)
        x = x + got.astype(jnp.float32) * (1.0 / LINK_SCALE)
        step *= 2
    return x, made + [work() for work in beside]


def gather_over_dp(x):
    size = lax.axis_size("dp")
    if size > 4 or not is_power_of_two(size):
        return lax.all_gather(x, "dp", axis=0)
    own = lax.axis_index("dp")
    got = jnp.zeros((size,) + x.shape, x.dtype)
    got = lax.dynamic_update_index_in_dim(got, x, own, 0)
    for step in range(1, size):
        block = lax.ppermute(x, "dp", partners(size, step))
        got = lax.dynamic_update_index_in_dim(got, block, own ^ step, 0)
    return got


def sum_over_layer_sub(x):
    if lax.axis_size("layer") != 2 or lax.axis_size("sub") != 2:
        return lax.psum(x, ("layer", "sub"))
    by_sub = lax.ppermute(x, "sub", partners(2, 1))
    by_layer = lax.ppermute(x, "layer", partners(2, 1))
    by_both = lax.ppermute(x, ("layer", "sub"), partners(4, 3))
    return (x + by_sub) + (by_layer + by_both)


def per_device(acts, kv_grad, kv_weight, proj_in, proj_out, codebook, codes, counts):
    rank_dim = proj_in.shape[1]
    sub_local, code_count, sub_width = codebook.shape
    train_local = codes.shape[0]
    dims_local = sub_local * sub_width
    live_rows = jnp.arange(train_local, dtype=jnp.int32) < counts[0]

    rows_local = kv_weight.shape[1]
    own_rows = lax.dynamic_slice_in_dim(proj_out, lax.axis_index("dp") * rows_local, rows_local, 0)
    folded = lax.dot_general(
        own_rows,
        kv_weight[0],
        (((0,), (0,)), ((), ())),
        preferred_element_type=jnp.float32,
    )
    folded, ((live, in_side), decoded) = sum_over_dp(
        folded,
        [
            lambda: (
                jnp.broadcast_to(live_rows, (8, train_local)).astype(jnp.float32),
                lax.dot_general(
                    proj_in, acts[0], (((0,), (1,)), ((), ())), preferred_element_type=jnp.float32
                ),
            ),
            lambda: decode(codes, jnp.transpose(codebook, (0, 2, 1))),
        ],
    )
    out_side = lax.dot_general(
        jnp.concatenate(split_high_low(folded), axis=0),
        kv_grad[0],
        (((1,), (1,)), ((), ())),
        preferred_element_type=jnp.float32,
    )
    out_side = out_side[:rank_dim] + out_side[rank_dim:]
    other_side = lax.psum(out_side, "sub") - out_side if lax.axis_size("sub") != 2 else (
        lax.ppermute(out_side, "sub", partners(2, 1))
    )
    vectors = make_vectors(in_side, out_side, other_side, dims_local)
    every = gather_over_dp((vectors * VECTOR_SCALE).astype(jnp.float16))
    every = every.reshape(-1, dims_local).astype(jnp.float32) * (1.0 / VECTOR_SCALE)
    tests_all = every.shape[0]

    layer_scores = jnp.dot(
        jnp.concatenate(split_high_low(every), axis=0), decoded, preferred_element_type=jnp.float32
    )
    layer_scores = layer_scores[:tests_all] + layer_scores[tests_all:]
    total = sum_over_layer_sub(layer_scores)
    return jnp.transpose(jnp.where(live[:1] > 0.0, total, jnp.float32(0.0)))


def solution(mesh):
    return jax.shard_map(
        per_device,
        mesh=mesh,
        in_specs=(
            P("layer", ("groups", "dp"), None),
            P("layer", ("groups", "dp"), "sub"),
            P("layer", "dp", "sub"),
            P(),
            P(),
            P("sub", None, None),
            P(("groups", "dp"), "layer", "sub"),
            P(("groups", "dp")),
        ),
        out_specs=P(("groups", "dp"), None),
        check_vma=False,
    )
```

```python
import math

import jax
import jax.numpy as jnp
from jax import lax
from jax.experimental import pallas as pl
from jax.experimental.pallas import tpu as pltpu
from jax.sharding import PartitionSpec as P

SEQ = 64
LANES = 128
LINK_SCALE = 1024.0
VECTOR_SCALE = 16384.0


def decode_kernel(codes_ref, book_ref, out_ref, ids_ref):
    subs, width, code_count = book_ref.shape
    slots = codes_ref.shape[0]
    for left in range(0, slots, LANES):
        for top in range(0, subs, LANES):
            block = codes_ref[left : left + LANES, 0, top : top + LANES]
            ids_ref[top : top + LANES, left : left + LANES] = jnp.transpose(block)

    group = math.gcd(subs, 64)

    def several(step, carry):
        first = pl.multiple_of(step * group, group)
        for top in range(0, group, 8):
            ids = ids_ref[pl.ds(pl.multiple_of(first + top, 8), 8), :]
            for pair in range(0, 8, 2):
                halves = []
                for sub in (pair, pair + 1):
                    table = book_ref[first + top + sub].astype(jnp.float32)
                    columns = []
                    for left in range(0, slots, LANES):
                        own = jnp.broadcast_to(ids[sub : sub + 1, left : left + LANES], (width, LANES))
                        spot = own & (LANES - 1)
                        picked = None
                        for part in range(0, code_count, LANES):
                            found = jnp.take_along_axis(
                                table[:, part : part + LANES], spot, axis=1, mode="promise_in_bounds"
                            )
                            picked = found if picked is None else jnp.where(own >= part, found, picked)
                        columns.append(picked)
                    halves.append(jnp.concatenate(columns, axis=1))
                rows = pl.multiple_of((first + top + pair) * width, 2 * width)
                out_ref[pl.ds(rows, 2 * width), :] = jnp.concatenate(halves, axis=0).astype(jnp.bfloat16)
        return carry

    lax.fori_loop(0, subs // group, several, 0)


def decode(codes, book_t):
    slots, _, subs = codes.shape
    width = book_t.shape[1]
    return pl.pallas_call(
        decode_kernel,
        out_shape=jax.ShapeDtypeStruct((subs * width, slots), jnp.bfloat16),
        in_specs=[pl.BlockSpec(memory_space=pltpu.VMEM)] * 2,
        out_specs=pl.BlockSpec(memory_space=pltpu.VMEM),
        scratch_shapes=[pltpu.VMEM((subs, slots), jnp.int32)],
        compiler_params=pltpu.CompilerParams(vmem_limit_bytes=8 * 1024 * 1024),
        cost_estimate=pl.CostEstimate(flops=0, bytes_accessed=2 * 1024 * 1024, transcendentals=0),
        name="decode",
    )(codes, book_t)


def vectors_kernel(in_ref, own_ref, other_ref, out_ref, grads_ref, flat_ref):
    rank_dim, tokens = in_ref.shape
    tests, dims = out_ref.shape
    pairs = rank_dim // 2
    tall = dims // LANES
    in_side = in_ref[...]
    test_of = lax.broadcasted_iota(jnp.int32, in_side.shape, 1) // SEQ
    grads_ref[:, :rank_dim] = lax.dot_general(
        jnp.concatenate([jnp.where(test_of == test, in_side, 0.0) for test in range(tests)], axis=0),
        own_ref[...] + other_ref[...],
        (((1,), (1,)), ((), ())),
        precision=lax.Precision.HIGHEST,
        preferred_element_type=jnp.float32,
    )
    for test in range(tests):
        even = grads_ref[pl.ds(test * rank_dim, pairs, stride=2), :][:, :rank_dim]
        odd = grads_ref[pl.ds(test * rank_dim + 1, pairs, stride=2), :][:, :rank_dim]
        both = jnp.concatenate([even, odd], axis=1)
        squares = jnp.sum(jnp.sum(both * both, axis=0, keepdims=True), axis=1, keepdims=True)
        mean = squares * (1.0 / (rank_dim * rank_dim))
        flat_ref[test * pairs : (test + 1) * pairs, :] = both * (lax.rsqrt(mean + 1e-06) / rank_dim)
    first = lax.axis_index("sub") * tall
    for row in range(tall):
        out_ref[:, row * LANES : (row + 1) * LANES] = flat_ref[
            pl.ds(first + row, tests, stride=pairs), :
        ]


def make_vectors(in_side, own, other, dims_local):
    rank_dim, tokens = in_side.shape
    tests = tokens // SEQ
    return pl.pallas_call(
        vectors_kernel,
        out_shape=jax.ShapeDtypeStruct((tests, dims_local), jnp.float32),
        in_specs=[pl.BlockSpec(memory_space=pltpu.VMEM)] * 3,
        out_specs=pl.BlockSpec(memory_space=pltpu.VMEM),
        scratch_shapes=[
            pltpu.VMEM((tests * rank_dim, LANES), jnp.float32),
            pltpu.VMEM((tests * rank_dim // 2, LANES), jnp.float32),
        ],
        compiler_params=pltpu.CompilerParams(vmem_limit_bytes=4 * 1024 * 1024),
        name="vectors",
    )(in_side, own, other)


def split_high_low(x):
    high = lax.reduce_precision(x, 8, 7)
    return high.astype(jnp.bfloat16), (x - high).astype(jnp.bfloat16)


def partners(size, step):
    return [(i, i ^ step) for i in range(size)]


def is_power_of_two(n):
    return n & (n - 1) == 0


def sum_over_dp(x, beside):
    size = lax.axis_size("dp")
    beside = list(beside)
    made = []
    if not is_power_of_two(size):
        return lax.psum(x, "dp"), [work() for work in beside]
    step = 1
    while step < size:
        got = lax.ppermute((x * LINK_SCALE).astype(jnp.float16), "dp", partners(size, step))
        if beside:
            got, done = lax.optimization_barrier((got, beside.pop(0)()))
            made.append(done)
        x = x + got.astype(jnp.float32) * (1.0 / LINK_SCALE)
        step *= 2
    return x, made + [work() for work in beside]


def gather_over_dp(x):
    size = lax.axis_size("dp")
    if size > 4 or not is_power_of_two(size):
        return lax.all_gather(x, "dp", axis=0)
    own = lax.axis_index("dp")
    got = jnp.zeros((size,) + x.shape, x.dtype)
    got = lax.dynamic_update_index_in_dim(got, x, own, 0)
    for step in (2, 3, 1):
        block = lax.ppermute(x, "dp", partners(size, step))
        got = lax.dynamic_update_index_in_dim(got, block, own ^ step, 0)
    return got


def sum_over_layer_sub(x):
    if lax.axis_size("layer") != 2 or lax.axis_size("sub") != 2:
        return lax.psum(x, ("layer", "sub"))
    by_sub = lax.ppermute(x, "sub", partners(2, 1))
    by_layer = lax.ppermute(x, "layer", partners(2, 1))
    by_both = lax.ppermute(x, ("layer", "sub"), partners(4, 3))
    return (x + by_sub) + (by_layer + by_both)


def per_device(acts, kv_grad, kv_weight, proj_in, proj_out, codebook, codes, counts):
    rank_dim = proj_in.shape[1]
    sub_local, code_count, sub_width = codebook.shape
    train_local = codes.shape[0]
    dims_local = sub_local * sub_width
    live_rows = jnp.arange(train_local, dtype=jnp.int32) < counts[0]

    rows_local = kv_weight.shape[1]
    own_rows = lax.dynamic_slice_in_dim(proj_out, lax.axis_index("dp") * rows_local, rows_local, 0)
    folded = lax.dot_general(
        own_rows,
        kv_weight[0],
        (((0,), (0,)), ((), ())),
        preferred_element_type=jnp.float32,
    )
    folded, ((live, in_side), decoded) = sum_over_dp(
        folded,
        [
            lambda: (
                jnp.broadcast_to(live_rows, (8, train_local)).astype(jnp.float32),
                lax.dot_general(
                    proj_in, acts[0], (((0,), (1,)), ((), ())), preferred_element_type=jnp.float32
                ),
            ),
            lambda: decode(codes, jnp.transpose(codebook, (0, 2, 1))),
        ],
    )
    out_side = lax.dot_general(
        jnp.concatenate(split_high_low(folded), axis=0),
        kv_grad[0],
        (((1,), (1,)), ((), ())),
        preferred_element_type=jnp.float32,
    )
    out_side = out_side[:rank_dim] + out_side[rank_dim:]
    other_side = lax.psum(out_side, "sub") - out_side if lax.axis_size("sub") != 2 else (
        lax.ppermute(out_side, "sub", partners(2, 1))
    )
    vectors = make_vectors(in_side, out_side, other_side, dims_local)
    every = gather_over_dp((vectors * VECTOR_SCALE).astype(jnp.float16))
    every = every.reshape(-1, dims_local).astype(jnp.float32) * (1.0 / VECTOR_SCALE)
    tests_all = every.shape[0]

    layer_scores = jnp.dot(
        jnp.concatenate(split_high_low(every), axis=0), decoded, preferred_element_type=jnp.float32
    )
    layer_scores = layer_scores[:tests_all] + layer_scores[tests_all:]
    total = sum_over_layer_sub(layer_scores)
    return jnp.transpose(jnp.where(live[:1] > 0.0, total, jnp.float32(0.0)))


def solution(mesh):
    return jax.shard_map(
        per_device,
        mesh=mesh,
        in_specs=(
            P("layer", ("groups", "dp"), None),
            P("layer", ("groups", "dp"), "sub"),
            P("layer", "dp", "sub"),
            P(),
            P(),
            P("sub", None, None),
            P(("groups", "dp"), "layer", "sub"),
            P(("groups", "dp")),
        ),
        out_specs=P(("groups", "dp"), None),
        check_vma=False,
    )
```

```python
import math

import jax
import jax.numpy as jnp
from jax import lax
from jax.experimental import pallas as pl
from jax.experimental.pallas import tpu as pltpu
from jax.sharding import PartitionSpec as P

SEQ = 64
LANES = 128
LINK_SCALE = 1024.0
VECTOR_SCALE = 16384.0


def decode_kernel(codes_ref, book_ref, out_ref, ids_ref):
    subs, width, code_count = book_ref.shape
    slots = codes_ref.shape[0]
    for left in range(0, slots, LANES):
        for top in range(0, subs, LANES):
            block = codes_ref[left : left + LANES, 0, top : top + LANES]
            ids_ref[top : top + LANES, left : left + LANES] = jnp.transpose(block)

    group = math.gcd(subs, 64)

    def several(step, carry):
        first = pl.multiple_of(step * group, group)
        for top in range(0, group, 8):
            ids = ids_ref[pl.ds(pl.multiple_of(first + top, 8), 8), :]
            for pair in range(0, 8, 2):
                halves = []
                for sub in (pair, pair + 1):
                    table = book_ref[first + top + sub].astype(jnp.float32)
                    columns = []
                    for left in range(0, slots, LANES):
                        own = jnp.broadcast_to(ids[sub : sub + 1, left : left + LANES], (width, LANES))
                        spot = own & (LANES - 1)
                        picked = None
                        for part in range(0, code_count, LANES):
                            found = jnp.take_along_axis(
                                table[:, part : part + LANES], spot, axis=1, mode="promise_in_bounds"
                            )
                            picked = found if picked is None else jnp.where(own >= part, found, picked)
                        columns.append(picked)
                    halves.append(jnp.concatenate(columns, axis=1))
                rows = pl.multiple_of((first + top + pair) * width, 2 * width)
                out_ref[pl.ds(rows, 2 * width), :] = jnp.concatenate(halves, axis=0).astype(jnp.bfloat16)
        return carry

    lax.fori_loop(0, subs // group, several, 0)


def decode(codes, book_t):
    slots, _, subs = codes.shape
    width = book_t.shape[1]
    return pl.pallas_call(
        decode_kernel,
        out_shape=jax.ShapeDtypeStruct((subs * width, slots), jnp.bfloat16),
        in_specs=[pl.BlockSpec(memory_space=pltpu.VMEM)] * 2,
        out_specs=pl.BlockSpec(memory_space=pltpu.VMEM),
        scratch_shapes=[pltpu.VMEM((subs, slots), jnp.int32)],
        compiler_params=pltpu.CompilerParams(vmem_limit_bytes=8 * 1024 * 1024),
        cost_estimate=pl.CostEstimate(flops=0, bytes_accessed=2 * 1024 * 1024, transcendentals=0),
        name="decode",
    )(codes, book_t)


def vectors_kernel(in_ref, own_ref, other_ref, out_ref, grads_ref, flat_ref):
    rank_dim, tokens = in_ref.shape
    tests, dims = out_ref.shape
    pairs = rank_dim // 2
    tall = dims // LANES
    in_side = in_ref[...]
    test_of = lax.broadcasted_iota(jnp.int32, in_side.shape, 1) // SEQ
    grads_ref[:, :rank_dim] = lax.dot_general(
        jnp.concatenate([jnp.where(test_of == test, in_side, 0.0) for test in range(tests)], axis=0),
        own_ref[...] + other_ref[...],
        (((1,), (1,)), ((), ())),
        precision=lax.Precision.HIGHEST,
        preferred_element_type=jnp.float32,
    )
    for test in range(tests):
        even = grads_ref[pl.ds(test * rank_dim, pairs, stride=2), :][:, :rank_dim]
        odd = grads_ref[pl.ds(test * rank_dim + 1, pairs, stride=2), :][:, :rank_dim]
        both = jnp.concatenate([even, odd], axis=1)
        squares = jnp.sum(jnp.sum(both * both, axis=0, keepdims=True), axis=1, keepdims=True)
        mean = squares * (1.0 / (rank_dim * rank_dim))
        flat_ref[test * pairs : (test + 1) * pairs, :] = both * (lax.rsqrt(mean + 1e-06) / rank_dim)
    first = lax.axis_index("sub") * tall
    for row in range(tall):
        out_ref[:, row * LANES : (row + 1) * LANES] = flat_ref[
            pl.ds(first + row, tests, stride=pairs), :
        ]


def make_vectors(in_side, own, other, dims_local):
    rank_dim, tokens = in_side.shape
    tests = tokens // SEQ
    return pl.pallas_call(
        vectors_kernel,
        out_shape=jax.ShapeDtypeStruct((tests, dims_local), jnp.float32),
        in_specs=[pl.BlockSpec(memory_space=pltpu.VMEM)] * 3,
        out_specs=pl.BlockSpec(memory_space=pltpu.VMEM),
        scratch_shapes=[
            pltpu.VMEM((tests * rank_dim, LANES), jnp.float32),
            pltpu.VMEM((tests * rank_dim // 2, LANES), jnp.float32),
        ],
        compiler_params=pltpu.CompilerParams(vmem_limit_bytes=4 * 1024 * 1024),
        name="vectors",
    )(in_side, own, other)


def split_high_low(x):
    high = lax.reduce_precision(x, 8, 7)
    return high.astype(jnp.bfloat16), (x - high).astype(jnp.bfloat16)


def partners(size, step):
    return [(i, i ^ step) for i in range(size)]


def is_power_of_two(n):
    return n & (n - 1) == 0


def sum_over_dp(x, beside):
    size = lax.axis_size("dp")
    beside = list(beside)
    made = []
    if not is_power_of_two(size):
        return lax.psum(x, "dp"), [work() for work in beside]
    step = 1
    while step < size:
        got = lax.ppermute((x * LINK_SCALE).astype(jnp.float16), "dp", partners(size, step))
        if beside:
            got, done = lax.optimization_barrier((got, beside.pop(0)()))
            made.append(done)
        x = x + got.astype(jnp.float32) * (1.0 / LINK_SCALE)
        step *= 2
    return x, made + [work() for work in beside]


def gather_over_dp(x):
    size = lax.axis_size("dp")
    if size > 4 or not is_power_of_two(size):
        return lax.all_gather(x, "dp", axis=0)
    own = lax.axis_index("dp")
    got = jnp.zeros((size,) + x.shape, x.dtype)
    got = lax.dynamic_update_index_in_dim(got, x, own, 0)
    for step in (2, 3, 1):
        block = lax.ppermute(x, "dp", partners(size, step))
        got = lax.dynamic_update_index_in_dim(got, block, own ^ step, 0)
    return got


def sum_over_layer_sub(x):
    if lax.axis_size("layer") != 2 or lax.axis_size("sub") != 2:
        return lax.psum(x, ("layer", "sub"))
    by_sub = lax.ppermute(x, "sub", partners(2, 1))
    by_layer = lax.ppermute(x, "layer", partners(2, 1))
    by_both = lax.ppermute(x, ("layer", "sub"), partners(4, 3))
    return (x + by_sub) + (by_layer + by_both)


def per_device(acts, kv_grad, kv_weight, proj_in, proj_out, codebook, codes, counts):
    rank_dim = proj_in.shape[1]
    sub_local, code_count, sub_width = codebook.shape
    train_local = codes.shape[0]
    dims_local = sub_local * sub_width
    live_rows = jnp.arange(train_local, dtype=jnp.int32) < counts[0]

    rows_local = kv_weight.shape[1]
    own_rows = lax.optimization_barrier(
        lax.dynamic_slice_in_dim(
            jnp.transpose(proj_out), lax.axis_index("dp") * rows_local, rows_local, 1
        )
    )
    folded = jnp.dot(own_rows, kv_weight[0], preferred_element_type=jnp.float32)
    folded, ((live, in_side), decoded) = sum_over_dp(
        folded,
        [
            lambda: (
                jnp.broadcast_to(live_rows, (8, train_local)).astype(jnp.float32),
                lax.dot_general(
                    proj_in, acts[0], (((0,), (1,)), ((), ())), preferred_element_type=jnp.float32
                ),
            ),
            lambda: decode(codes, jnp.transpose(codebook, (0, 2, 1))),
        ],
    )
    out_side = lax.dot_general(
        jnp.concatenate(split_high_low(folded), axis=0),
        kv_grad[0],
        (((1,), (1,)), ((), ())),
        preferred_element_type=jnp.float32,
    )
    out_side = out_side[:rank_dim] + out_side[rank_dim:]
    other_side = lax.psum(out_side, "sub") - out_side if lax.axis_size("sub") != 2 else (
        lax.ppermute(out_side, "sub", partners(2, 1))
    )
    vectors = make_vectors(in_side, out_side, other_side, dims_local)
    every = gather_over_dp((vectors * VECTOR_SCALE).astype(jnp.float16))
    every = every.reshape(-1, dims_local).astype(jnp.float32) * (1.0 / VECTOR_SCALE)
    tests_all = every.shape[0]

    layer_scores = jnp.dot(
        jnp.concatenate(split_high_low(every), axis=0), decoded, preferred_element_type=jnp.float32
    )
    layer_scores = layer_scores[:tests_all] + layer_scores[tests_all:]
    total = sum_over_layer_sub(layer_scores)
    return jnp.transpose(jnp.where(live[:1] > 0.0, total, jnp.float32(0.0)))


def solution(mesh):
    return jax.shard_map(
        per_device,
        mesh=mesh,
        in_specs=(
            P("layer", ("groups", "dp"), None),
            P("layer", ("groups", "dp"), "sub"),
            P("layer", "dp", "sub"),
            P(),
            P(),
            P("sub", None, None),
            P(("groups", "dp"), "layer", "sub"),
            P(("groups", "dp")),
        ),
        out_specs=P(("groups", "dp"), None),
        check_vma=False,
    )
```

```python
import math

import jax
import jax.numpy as jnp
from jax import lax
from jax.experimental import pallas as pl
from jax.experimental.pallas import tpu as pltpu
from jax.sharding import PartitionSpec as P

SEQ = 64
LANES = 128
LINK_SCALE = 1024.0
VECTOR_SCALE = 16384.0
GATHER_ORDER = (0, 1, 3, 2)


def rows_kernel(proj_ref, out_ref, sem):
    rows = out_ref.shape[1]
    first = pl.multiple_of(lax.axis_index("dp") * rows, LANES)
    copy = pltpu.make_async_copy(proj_ref.at[:, pl.ds(first, rows)], out_ref, sem)
    copy.start()
    copy.wait()


def take_rows(proj_t, rows):
    return pl.pallas_call(
        rows_kernel,
        out_shape=jax.ShapeDtypeStruct((proj_t.shape[0], rows), proj_t.dtype),
        in_specs=[pl.BlockSpec(memory_space=pl.ANY)],
        out_specs=pl.BlockSpec(memory_space=pltpu.VMEM),
        scratch_shapes=[pltpu.SemaphoreType.DMA],
        compiler_params=pltpu.CompilerParams(vmem_limit_bytes=1024 * 1024),
        name="rows",
    )(proj_t)


def ids_kernel(codes_ref, out_ref):
    slots, _, subs = codes_ref.shape
    for left in range(0, slots, LANES):
        for top in range(0, subs, LANES):
            block = codes_ref[left : left + LANES, 0, top : top + LANES]
            out_ref[top : top + LANES, left : left + LANES] = (
                jnp.transpose(block).astype(jnp.float32).astype(jnp.bfloat16)
            )


def make_ids(codes):
    slots, _, subs = codes.shape
    return pl.pallas_call(
        ids_kernel,
        out_shape=jax.ShapeDtypeStruct((subs, slots), jnp.bfloat16),
        in_specs=[pl.BlockSpec(memory_space=pltpu.VMEM)],
        out_specs=pl.BlockSpec(memory_space=pltpu.VMEM),
        compiler_params=pltpu.CompilerParams(vmem_limit_bytes=4 * 1024 * 1024),
        name="ids",
    )(codes)


def decode_kernel(ids_ref, book_ref, out_ref):
    subs, width, code_count = book_ref.shape
    slots = ids_ref.shape[1]
    group = math.gcd(subs, 64)

    def several(step, carry):
        first = pl.multiple_of(step * group, group)
        for top in range(0, group, 16):
            ids = ids_ref[pl.ds(pl.multiple_of(first + top, 16), 16), :]
            ids = ids.astype(jnp.float32).astype(jnp.int32)
            for pair in range(0, 16, 2):
                halves = []
                for sub in (pair, pair + 1):
                    table = book_ref[first + top + sub].astype(jnp.float32)
                    columns = []
                    for left in range(0, slots, LANES):
                        own = jnp.broadcast_to(ids[sub : sub + 1, left : left + LANES], (width, LANES))
                        spot = own & (LANES - 1)
                        picked = None
                        for part in range(0, code_count, LANES):
                            found = jnp.take_along_axis(
                                table[:, part : part + LANES], spot, axis=1, mode="promise_in_bounds"
                            )
                            picked = found if picked is None else jnp.where(own >= part, found, picked)
                        columns.append(picked)
                    halves.append(jnp.concatenate(columns, axis=1))
                rows = pl.multiple_of((first + top + pair) * width, 2 * width)
                out_ref[pl.ds(rows, 2 * width), :] = jnp.concatenate(halves, axis=0).astype(jnp.bfloat16)
        return carry

    lax.fori_loop(0, subs // group, several, 0)


def decode(ids, book_t):
    subs, width, _ = book_t.shape
    slots = ids.shape[1]
    return pl.pallas_call(
        decode_kernel,
        out_shape=jax.ShapeDtypeStruct((subs * width, slots), jnp.bfloat16),
        in_specs=[pl.BlockSpec(memory_space=pltpu.VMEM)] * 2,
        out_specs=pl.BlockSpec(memory_space=pltpu.VMEM),
        compiler_params=pltpu.CompilerParams(vmem_limit_bytes=8 * 1024 * 1024),
        cost_estimate=pl.CostEstimate(flops=0, bytes_accessed=2 * 1024 * 1024, transcendentals=0),
        name="decode",
    )(ids, book_t)


def vectors_kernel(in_ref, own_ref, other_ref, out_ref, grads_ref, flat_ref):
    rank_dim, tokens = in_ref.shape
    parts, tests, dims = out_ref.shape
    pairs = rank_dim // 2
    tall = dims // LANES
    in_side = in_ref[...]
    test_of = lax.broadcasted_iota(jnp.int32, in_side.shape, 1) // SEQ
    grads_ref[:, :rank_dim] = lax.dot_general(
        jnp.concatenate([jnp.where(test_of == test, in_side, 0.0) for test in range(tests)], axis=0),
        own_ref[...] + other_ref[...],
        (((1,), (1,)), ((), ())),
        precision=lax.Precision.HIGHEST,
        preferred_element_type=jnp.float32,
    )
    for test in range(tests):
        even = grads_ref[pl.ds(test * rank_dim, pairs, stride=2), :][:, :rank_dim]
        odd = grads_ref[pl.ds(test * rank_dim + 1, pairs, stride=2), :][:, :rank_dim]
        both = jnp.concatenate([even, odd], axis=1)
        squares = jnp.sum(jnp.sum(both * both, axis=0, keepdims=True), axis=1, keepdims=True)
        mean = squares * (1.0 / (rank_dim * rank_dim))
        flat_ref[test * pairs : (test + 1) * pairs, :] = both * (lax.rsqrt(mean + 1e-06) / rank_dim)
    for part in range(parts):
        for row in range(tall):
            out_ref[part, :, row * LANES : (row + 1) * LANES] = flat_ref[
                pl.ds(part * tall + row, tests, stride=pairs), :
            ]


def score_kernel(*refs):
    *vector_refs, near_ref, far_ref, out_ref = refs
    tests = vector_refs[0].shape[1]
    core = lax.axis_index("sub")
    own = lax.axis_index("dp")
    total = None
    for part, table_ref in ((core, near_ref), (1 - core, far_ref)):
        vectors = jnp.concatenate([ref[part] for ref in vector_refs], axis=0)
        high = vectors.astype(jnp.bfloat16)
        low = (vectors - high.astype(jnp.float32)).astype(jnp.bfloat16)
        both = jnp.dot(
            jnp.concatenate([high, low], axis=0), table_ref[...], preferred_element_type=jnp.float32
        )
        total = both if total is None else total + both
    blocks = len(vector_refs)
    total = total[: blocks * tests] + total[blocks * tests :]
    rows = [None] * blocks
    for at, xor in enumerate(GATHER_ORDER):
        rows[xor] = total[at * tests : (at + 1) * tests]
    step = 1
    while step < blocks:
        rows = [jnp.where((own & step) != 0, rows[at ^ step], rows[at]) for at in range(blocks)]
        step *= 2
    out_ref[...] = jnp.concatenate(rows, axis=0)


def score_blocks(blocks, near, far):
    tests = blocks[0].shape[1]
    return pl.pallas_call(
        score_kernel,
        out_shape=jax.ShapeDtypeStruct((len(blocks) * tests, near.shape[1]), jnp.float32),
        in_specs=[pl.BlockSpec(memory_space=pltpu.VMEM)] * (len(blocks) + 2),
        out_specs=pl.BlockSpec(memory_space=pltpu.VMEM),
        compiler_params=pltpu.CompilerParams(vmem_limit_bytes=8 * 1024 * 1024),
        name="score",
    )(*blocks, near, far)


def score(vectors, table):
    tests = vectors.shape[0]
    both = jnp.dot(
        jnp.concatenate(split_high_low(vectors), axis=0), table, preferred_element_type=jnp.float32
    )
    return both[:tests] + both[tests:]


def make_vectors(in_side, own, other, dims_local):
    rank_dim, tokens = in_side.shape
    tests = tokens // SEQ
    return pl.pallas_call(
        vectors_kernel,
        out_shape=jax.ShapeDtypeStruct((rank_dim * rank_dim // dims_local, tests, dims_local), jnp.float32),
        in_specs=[pl.BlockSpec(memory_space=pltpu.VMEM)] * 3,
        out_specs=pl.BlockSpec(memory_space=pltpu.VMEM),
        scratch_shapes=[
            pltpu.VMEM((tests * rank_dim, LANES), jnp.float32),
            pltpu.VMEM((tests * rank_dim // 2, LANES), jnp.float32),
        ],
        compiler_params=pltpu.CompilerParams(vmem_limit_bytes=4 * 1024 * 1024),
        name="vectors",
    )(in_side, own, other)


def split_high_low(x):
    high = lax.reduce_precision(x, 8, 7)
    return high.astype(jnp.bfloat16), (x - high).astype(jnp.bfloat16)


def partners(size, step):
    return [(i, i ^ step) for i in range(size)]


def is_power_of_two(n):
    return n & (n - 1) == 0


def sum_over_dp(x, sent, beside):
    size = lax.axis_size("dp")
    beside = list(beside)
    made = []
    if not is_power_of_two(size):
        return lax.psum(x, "dp"), [work() for work in beside]
    step = 1
    while step < size:
        got = lax.ppermute(sent, "dp", partners(size, step))
        if beside:
            got, done = lax.optimization_barrier((got, beside.pop(0)()))
            made.append(done)
        x = x + got.astype(jnp.float32) * (1.0 / LINK_SCALE)
        sent = (x * LINK_SCALE).astype(jnp.float16)
        step *= 2
    return x, made + [work() for work in beside]


def gather_over_dp(x):
    size = lax.axis_size("dp")
    if size > 4 or not is_power_of_two(size):
        return lax.all_gather(x, "dp", axis=0)
    own = lax.axis_index("dp")
    got = jnp.zeros((size,) + x.shape, x.dtype)
    got = lax.dynamic_update_index_in_dim(got, x, own, 0)
    for step in (2, 3, 1):
        block = lax.ppermute(x, "dp", partners(size, step))
        got = lax.dynamic_update_index_in_dim(got, block, own ^ step, 0)
    return got


def has_two_by_two():
    return lax.axis_size("layer") == 2 and lax.axis_size("sub") == 2


NEAR_CODES = [(0, 0), (2, 2), (3, 1), (1, 3)]
FAR_CODES = [(1, 0), (3, 2), (2, 1), (0, 3)]


def gather_by_core(x):
    size = lax.axis_size("dp")
    blocks = []
    for step in GATHER_ORDER:
        pairs = [
            (4 * at + 2 * layer + core, 4 * (at ^ step) + 2 * (layer ^ core) + core)
            for at in range(size)
            for layer in range(2)
            for core in range(2)
        ]
        blocks.append(lax.ppermute(x, ("dp", "layer", "sub"), pairs))
    return blocks


def per_device(acts, kv_grad, kv_weight, proj_in, proj_out, codebook, codes, counts):
    rank_dim = proj_in.shape[1]
    sub_local, code_count, sub_width = codebook.shape
    train_local = codes.shape[0]
    dims_local = sub_local * sub_width
    live_rows = jnp.arange(train_local, dtype=jnp.int32) < counts[0]

    rows_local = kv_weight.shape[1]
    own_rows = lax.optimization_barrier(
        lax.dynamic_slice_in_dim(
            jnp.transpose(proj_out), lax.axis_index("dp") * rows_local, rows_local, 1
        )
    )
    folded = jnp.dot(own_rows, kv_weight[0], preferred_element_type=jnp.float32)
    book_t = jnp.transpose(codebook, (0, 2, 1))
    by_core = has_two_by_two() and lax.axis_size("dp") == 4

    sent = (folded * LINK_SCALE).astype(jnp.float16)
    live = jnp.broadcast_to(live_rows, (8, train_local)).astype(jnp.float32)
    live, moved_codes = lax.optimization_barrier((live, codes))
    ids = make_ids(moved_codes)
    if by_core:
        sent, moved_book = lax.optimization_barrier((sent, codebook))
        near_ids = lax.ppermute(ids, ("layer", "sub"), NEAR_CODES)
        far_ids = lax.ppermute(ids, ("layer", "sub"), FAR_CODES)
        other_book = lax.ppermute(moved_book, "sub", partners(2, 1))

    def first_side():
        return lax.dot_general(
            proj_in, acts[0], (((0,), (1,)), ((), ())), preferred_element_type=jnp.float32
        )

    def tables():
        if not by_core:
            return (decode(ids, book_t),)
        return decode(near_ids, book_t), decode(far_ids, jnp.transpose(other_book, (0, 2, 1)))

    folded, (live, (in_side, decoded)) = sum_over_dp(
        folded, sent, [lambda: live, lambda: (first_side(), tables())]
    )
    out_side = lax.dot_general(
        jnp.concatenate(split_high_low(folded), axis=0),
        kv_grad[0],
        (((1,), (1,)), ((), ())),
        preferred_element_type=jnp.float32,
    )
    out_side = out_side[:rank_dim] + out_side[rank_dim:]
    other_side = lax.psum(out_side, "sub") - out_side if lax.axis_size("sub") != 2 else (
        lax.ppermute(out_side, "sub", partners(2, 1))
    )
    vectors = make_vectors(in_side, out_side, other_side, dims_local)
    sent = (vectors * VECTOR_SCALE).astype(jnp.float16)
    core = lax.axis_index("sub")
    if by_core:
        blocks = [
            block.astype(jnp.float32) * (1.0 / VECTOR_SCALE) for block in gather_by_core(sent)
        ]
        total = score_blocks(blocks, *decoded)
        total = total + lax.ppermute(total, "sub", partners(2, 1))
    else:
        every = gather_over_dp(lax.dynamic_index_in_dim(sent, core, 0, False))
        every = every.reshape(-1, dims_local).astype(jnp.float32) * (1.0 / VECTOR_SCALE)
        total = lax.psum(score(every, decoded[0]), ("layer", "sub"))
    return jnp.transpose(jnp.where(live[:1] > 0.0, total, jnp.float32(0.0)))


def solution(mesh):
    return jax.shard_map(
        per_device,
        mesh=mesh,
        in_specs=(
            P("layer", ("groups", "dp"), None),
            P("layer", ("groups", "dp"), "sub"),
            P("layer", "dp", "sub"),
            P(),
            P(),
            P("sub", None, None),
            P(("groups", "dp"), "layer", "sub"),
            P(("groups", "dp")),
        ),
        out_specs=P(("groups", "dp"), None),
        check_vma=False,
    )
```

```python
import math

import jax
import jax.numpy as jnp
from jax import lax
from jax.experimental import pallas as pl
from jax.experimental.pallas import tpu as pltpu
from jax.sharding import PartitionSpec as P

SEQ = 64
LANES = 128
LINK_SCALE = 1024.0
VECTOR_SCALE = 16384.0
GATHER_ORDER = (0, 1, 3, 2)


def rows_kernel(proj_ref, out_ref, sem):
    rows = out_ref.shape[1]
    first = pl.multiple_of(lax.axis_index("dp") * rows, LANES)
    copy = pltpu.make_async_copy(proj_ref.at[:, pl.ds(first, rows)], out_ref, sem)
    copy.start()
    copy.wait()


def take_rows(proj_t, rows):
    return pl.pallas_call(
        rows_kernel,
        out_shape=jax.ShapeDtypeStruct((proj_t.shape[0], rows), proj_t.dtype),
        in_specs=[pl.BlockSpec(memory_space=pl.ANY)],
        out_specs=pl.BlockSpec(memory_space=pltpu.VMEM),
        scratch_shapes=[pltpu.SemaphoreType.DMA],
        compiler_params=pltpu.CompilerParams(vmem_limit_bytes=1024 * 1024),
        name="rows",
    )(proj_t)


def ids_kernel(codes_ref, out_ref):
    slots, _, subs = codes_ref.shape
    for left in range(0, slots, LANES):
        for top in range(0, subs, LANES):
            block = codes_ref[left : left + LANES, 0, top : top + LANES]
            out_ref[top : top + LANES, left : left + LANES] = (
                jnp.transpose(block).astype(jnp.float32).astype(jnp.bfloat16)
            )


def make_ids(codes):
    slots, _, subs = codes.shape
    return pl.pallas_call(
        ids_kernel,
        out_shape=jax.ShapeDtypeStruct((subs, slots), jnp.bfloat16),
        in_specs=[pl.BlockSpec(memory_space=pltpu.VMEM)],
        out_specs=pl.BlockSpec(memory_space=pltpu.VMEM),
        compiler_params=pltpu.CompilerParams(vmem_limit_bytes=4 * 1024 * 1024),
        name="ids",
    )(codes)


def decode_kernel(*refs):
    *ids_refs, book_ref, out_ref = refs
    core = lax.axis_index("sub")
    subs, width, code_count = book_ref.shape
    slots = ids_refs[0].shape[1]
    group = math.gcd(subs, 64)

    def several(step, carry):
        first = pl.multiple_of(step * group, group)
        for top in range(0, group, 16):
            rows = pl.ds(pl.multiple_of(first + top, 16), 16)
            ids = [ref[rows, :].astype(jnp.float32) for ref in ids_refs]
            ids = jnp.where(core == 0, ids[0], ids[-1]).astype(jnp.int32)
            for pair in range(0, 16, 2):
                halves = []
                for sub in (pair, pair + 1):
                    table = book_ref[first + top + sub].astype(jnp.float32)
                    columns = []
                    for left in range(0, slots, LANES):
                        own = jnp.broadcast_to(ids[sub : sub + 1, left : left + LANES], (width, LANES))
                        spot = own & (LANES - 1)
                        picked = None
                        for part in range(0, code_count, LANES):
                            found = jnp.take_along_axis(
                                table[:, part : part + LANES], spot, axis=1, mode="promise_in_bounds"
                            )
                            picked = found if picked is None else jnp.where(own >= part, found, picked)
                        columns.append(picked)
                    halves.append(jnp.concatenate(columns, axis=1))
                rows = pl.multiple_of((first + top + pair) * width, 2 * width)
                out_ref[pl.ds(rows, 2 * width), :] = jnp.concatenate(halves, axis=0).astype(jnp.bfloat16)
        return carry

    lax.fori_loop(0, subs // group, several, 0)


def decode(ids, book_t):
    subs, width, _ = book_t.shape
    slots = ids[0].shape[1]
    return pl.pallas_call(
        decode_kernel,
        out_shape=jax.ShapeDtypeStruct((subs * width, slots), jnp.bfloat16),
        in_specs=[pl.BlockSpec(memory_space=pltpu.VMEM)] * (len(ids) + 1),
        out_specs=pl.BlockSpec(memory_space=pltpu.VMEM),
        compiler_params=pltpu.CompilerParams(vmem_limit_bytes=8 * 1024 * 1024),
        cost_estimate=pl.CostEstimate(flops=0, bytes_accessed=2 * 1024 * 1024, transcendentals=0),
        name="decode",
    )(*ids, book_t)


def vectors_kernel(in_ref, own_ref, other_ref, out_ref, grads_ref, flat_ref):
    rank_dim, tokens = in_ref.shape
    parts, tests, dims = out_ref.shape
    pairs = rank_dim // 2
    tall = dims // LANES
    in_side = in_ref[...]
    test_of = lax.broadcasted_iota(jnp.int32, in_side.shape, 1) // SEQ
    grads_ref[:, :rank_dim] = lax.dot_general(
        jnp.concatenate([jnp.where(test_of == test, in_side, 0.0) for test in range(tests)], axis=0),
        own_ref[...] + other_ref[...],
        (((1,), (1,)), ((), ())),
        precision=lax.Precision.HIGHEST,
        preferred_element_type=jnp.float32,
    )
    for test in range(tests):
        even = grads_ref[pl.ds(test * rank_dim, pairs, stride=2), :][:, :rank_dim]
        odd = grads_ref[pl.ds(test * rank_dim + 1, pairs, stride=2), :][:, :rank_dim]
        both = jnp.concatenate([even, odd], axis=1)
        squares = jnp.sum(jnp.sum(both * both, axis=0, keepdims=True), axis=1, keepdims=True)
        mean = squares * (1.0 / (rank_dim * rank_dim))
        flat_ref[test * pairs : (test + 1) * pairs, :] = both * (lax.rsqrt(mean + 1e-06) / rank_dim)
    for part in range(parts):
        for row in range(tall):
            out_ref[part, :, row * LANES : (row + 1) * LANES] = flat_ref[
                pl.ds(part * tall + row, tests, stride=pairs), :
            ]


def score_kernel(*refs):
    own_ref, *vector_refs, near_ref, far_ref, out_ref = refs
    tests = own_ref.shape[1]
    core = lax.axis_index("sub")
    own = lax.axis_index("dp")
    total = None
    for part, table_ref in ((core, near_ref), (1 - core, far_ref)):
        vectors = [ref[part] for ref in vector_refs]
        at = GATHER_ORDER.index(0)
        vectors[at] = jnp.where(core == 0, own_ref[part], vectors[at])
        vectors = jnp.concatenate(vectors, axis=0)
        high = vectors.astype(jnp.bfloat16)
        low = (vectors - high.astype(jnp.float32)).astype(jnp.bfloat16)
        both = jnp.dot(
            jnp.concatenate([high, low], axis=0), table_ref[...], preferred_element_type=jnp.float32
        )
        total = both if total is None else total + both
    blocks = len(vector_refs)
    total = total[: blocks * tests] + total[blocks * tests :]
    rows = [None] * blocks
    for at, xor in enumerate(GATHER_ORDER):
        rows[xor] = total[at * tests : (at + 1) * tests]
    step = 1
    while step < blocks:
        rows = [jnp.where((own & step) != 0, rows[at ^ step], rows[at]) for at in range(blocks)]
        step *= 2
    out_ref[...] = jnp.concatenate(rows, axis=0)


def score_blocks(own, blocks, near, far):
    tests = blocks[0].shape[1]
    return pl.pallas_call(
        score_kernel,
        out_shape=jax.ShapeDtypeStruct((len(blocks) * tests, near.shape[1]), jnp.float32),
        in_specs=[pl.BlockSpec(memory_space=pltpu.VMEM)] * (len(blocks) + 3),
        out_specs=pl.BlockSpec(memory_space=pltpu.VMEM),
        compiler_params=pltpu.CompilerParams(vmem_limit_bytes=8 * 1024 * 1024),
        name="score",
    )(own, *blocks, near, far)


def score(vectors, table):
    tests = vectors.shape[0]
    both = jnp.dot(
        jnp.concatenate(split_high_low(vectors), axis=0), table, preferred_element_type=jnp.float32
    )
    return both[:tests] + both[tests:]


def make_vectors(in_side, own, other, dims_local):
    rank_dim, tokens = in_side.shape
    tests = tokens // SEQ
    return pl.pallas_call(
        vectors_kernel,
        out_shape=jax.ShapeDtypeStruct((rank_dim * rank_dim // dims_local, tests, dims_local), jnp.float32),
        in_specs=[pl.BlockSpec(memory_space=pltpu.VMEM)] * 3,
        out_specs=pl.BlockSpec(memory_space=pltpu.VMEM),
        scratch_shapes=[
            pltpu.VMEM((tests * rank_dim, LANES), jnp.float32),
            pltpu.VMEM((tests * rank_dim // 2, LANES), jnp.float32),
        ],
        compiler_params=pltpu.CompilerParams(vmem_limit_bytes=4 * 1024 * 1024),
        name="vectors",
    )(in_side, own, other)


def split_high_low(x):
    high = lax.reduce_precision(x, 8, 7)
    return high.astype(jnp.bfloat16), (x - high).astype(jnp.bfloat16)


def partners(size, step):
    return [(i, i ^ step) for i in range(size)]


def is_power_of_two(n):
    return n & (n - 1) == 0


def sum_over_dp(x, sent, beside):
    size = lax.axis_size("dp")
    beside = list(beside)
    made = []
    if not is_power_of_two(size):
        return lax.psum(x, "dp"), [work() for work in beside]
    step = 1
    while step < size:
        got = lax.ppermute(sent, "dp", partners(size, step))
        if beside:
            got, done = lax.optimization_barrier((got, beside.pop(0)()))
            made.append(done)
        x = x + got.astype(jnp.float32) * (1.0 / LINK_SCALE)
        sent = (x * LINK_SCALE).astype(jnp.float16)
        step *= 2
    return x, made + [work() for work in beside]


def gather_over_dp(x):
    size = lax.axis_size("dp")
    if size > 4 or not is_power_of_two(size):
        return lax.all_gather(x, "dp", axis=0)
    own = lax.axis_index("dp")
    got = jnp.zeros((size,) + x.shape, x.dtype)
    got = lax.dynamic_update_index_in_dim(got, x, own, 0)
    for step in (2, 3, 1):
        block = lax.ppermute(x, "dp", partners(size, step))
        got = lax.dynamic_update_index_in_dim(got, block, own ^ step, 0)
    return got


def has_two_by_two():
    return lax.axis_size("layer") == 2 and lax.axis_size("sub") == 2


NEAR_CODES = [(3, 1), (1, 3)]
FAR_CODES = [(1, 0), (3, 2), (2, 1), (0, 3)]


def gather_by_core(x):
    size = lax.axis_size("dp")
    blocks = []
    for step in GATHER_ORDER:
        pairs = [
            (4 * at + 2 * layer + core, 4 * (at ^ step) + 2 * (layer ^ core) + core)
            for at in range(size)
            for layer in range(2)
            for core in range(2)
        ]
        if not step:
            pairs = [(i, i ^ 2) for i in range(4 * size)]
        blocks.append(lax.ppermute(x, ("dp", "layer", "sub"), pairs))
    return blocks


def per_device(acts, kv_grad, kv_weight, proj_in, proj_out, codebook, codes, counts):
    rank_dim = proj_in.shape[1]
    sub_local, code_count, sub_width = codebook.shape
    train_local = codes.shape[0]
    dims_local = sub_local * sub_width
    live_rows = jnp.arange(train_local, dtype=jnp.int32) < counts[0]

    rows_local = kv_weight.shape[1]
    own_rows = lax.optimization_barrier(
        lax.dynamic_slice_in_dim(
            jnp.transpose(proj_out), lax.axis_index("dp") * rows_local, rows_local, 1
        )
    )
    folded = jnp.dot(own_rows, kv_weight[0], preferred_element_type=jnp.float32)
    book_t = jnp.transpose(codebook, (0, 2, 1))
    by_core = has_two_by_two() and lax.axis_size("dp") == 4

    sent = (folded * LINK_SCALE).astype(jnp.float16)
    live = jnp.broadcast_to(live_rows, (8, train_local)).astype(jnp.float32)
    live, moved_codes = lax.optimization_barrier((live, codes))
    ids = make_ids(moved_codes)
    if by_core:
        sent, moved_book = lax.optimization_barrier((sent, codebook))
        near_ids = lax.ppermute(ids, "layer", partners(2, 1))
        far_ids = lax.ppermute(ids, ("layer", "sub"), FAR_CODES)
        other_book = lax.ppermute(moved_book, "sub", partners(2, 1))

    def first_side():
        return lax.dot_general(
            proj_in, acts[0], (((0,), (1,)), ((), ())), preferred_element_type=jnp.float32
        )

    def tables():
        if not by_core:
            return (decode([ids], book_t),)
        far = decode([far_ids], jnp.transpose(other_book, (0, 2, 1)))
        far, late_ids = lax.optimization_barrier((far, near_ids))
        return decode([ids, late_ids], book_t), far

    folded, (live, decoded) = sum_over_dp(
        folded, sent, [lambda: live, tables]
    )
    out_side = lax.dot_general(
        jnp.concatenate(split_high_low(folded), axis=0),
        kv_grad[0],
        (((1,), (1,)), ((), ())),
        preferred_element_type=jnp.float32,
    )
    out_side = out_side[:rank_dim] + out_side[rank_dim:]
    other_side = lax.psum(out_side, "sub") - out_side if lax.axis_size("sub") != 2 else (
        lax.ppermute(out_side, "sub", partners(2, 1))
    )
    other_side, in_side = lax.optimization_barrier((other_side, first_side()))
    vectors = make_vectors(in_side, out_side, other_side, dims_local)
    sent = (vectors * VECTOR_SCALE).astype(jnp.float16)
    core = lax.axis_index("sub")
    if by_core:
        blocks = [
            block.astype(jnp.float32) * (1.0 / VECTOR_SCALE) for block in gather_by_core(sent)
        ]
        total = score_blocks(vectors, blocks, *decoded)
        total = total + lax.ppermute(total, "sub", partners(2, 1))
    else:
        every = gather_over_dp(lax.dynamic_index_in_dim(sent, core, 0, False))
        every = every.reshape(-1, dims_local).astype(jnp.float32) * (1.0 / VECTOR_SCALE)
        total = lax.psum(score(every, decoded[0]), ("layer", "sub"))
    return jnp.transpose(jnp.where(live[:1] > 0.0, total, jnp.float32(0.0)))


def solution(mesh):
    return jax.shard_map(
        per_device,
        mesh=mesh,
        in_specs=(
            P("layer", ("groups", "dp"), None),
            P("layer", ("groups", "dp"), "sub"),
            P("layer", "dp", "sub"),
            P(),
            P(),
            P("sub", None, None),
            P(("groups", "dp"), "layer", "sub"),
            P(("groups", "dp")),
        ),
        out_specs=P(("groups", "dp"), None),
        check_vma=False,
    )
```

```python
import math

import jax
import jax.numpy as jnp
from jax import lax
from jax.experimental import pallas as pl
from jax.experimental.pallas import tpu as pltpu
from jax.sharding import PartitionSpec as P

SEQ = 64
LANES = 128
LINK_SCALE = 1024.0
VECTOR_SCALE = 16384.0
GATHER_ORDER = (0, 1, 3, 2)


def rows_kernel(proj_ref, out_ref, sem):
    rows = out_ref.shape[1]
    first = pl.multiple_of(lax.axis_index("dp") * rows, LANES)
    copy = pltpu.make_async_copy(proj_ref.at[:, pl.ds(first, rows)], out_ref, sem)
    copy.start()
    copy.wait()


def take_rows(proj_t, rows):
    return pl.pallas_call(
        rows_kernel,
        out_shape=jax.ShapeDtypeStruct((proj_t.shape[0], rows), proj_t.dtype),
        in_specs=[pl.BlockSpec(memory_space=pl.ANY)],
        out_specs=pl.BlockSpec(memory_space=pltpu.VMEM),
        scratch_shapes=[pltpu.SemaphoreType.DMA],
        compiler_params=pltpu.CompilerParams(vmem_limit_bytes=1024 * 1024),
        name="rows",
    )(proj_t)


def ids_kernel(codes_ref, out_ref):
    slots, _, subs = codes_ref.shape
    for left in range(0, slots, LANES):
        for top in range(0, subs, LANES):
            block = codes_ref[left : left + LANES, 0, top : top + LANES]
            out_ref[top : top + LANES, left : left + LANES] = (
                jnp.transpose(block).astype(jnp.float32).astype(jnp.bfloat16)
            )


def make_ids(codes):
    slots, _, subs = codes.shape
    return pl.pallas_call(
        ids_kernel,
        out_shape=jax.ShapeDtypeStruct((subs, slots), jnp.bfloat16),
        in_specs=[pl.BlockSpec(memory_space=pltpu.VMEM)],
        out_specs=pl.BlockSpec(memory_space=pltpu.VMEM),
        compiler_params=pltpu.CompilerParams(vmem_limit_bytes=4 * 1024 * 1024),
        name="ids",
    )(codes)


def decode_kernel(*refs):
    *ids_refs, book_ref, out_ref = refs
    core = lax.axis_index("sub")
    subs, width, code_count = book_ref.shape
    slots = ids_refs[0].shape[1]
    group = math.gcd(subs, 64)

    def several(step, carry):
        first = pl.multiple_of(step * group, group)
        for top in range(0, group, 16):
            rows = pl.ds(pl.multiple_of(first + top, 16), 16)
            ids = [ref[rows, :].astype(jnp.float32) for ref in ids_refs]
            ids = jnp.where(core == 0, ids[0], ids[-1]).astype(jnp.int32)
            for pair in range(0, 16, 2):
                halves = []
                for sub in (pair, pair + 1):
                    table = book_ref[first + top + sub].astype(jnp.float32)
                    columns = []
                    for left in range(0, slots, LANES):
                        own = jnp.broadcast_to(ids[sub : sub + 1, left : left + LANES], (width, LANES))
                        spot = own & (LANES - 1)
                        picked = None
                        for part in range(0, code_count, LANES):
                            found = jnp.take_along_axis(
                                table[:, part : part + LANES], spot, axis=1, mode="promise_in_bounds"
                            )
                            picked = found if picked is None else jnp.where(own >= part, found, picked)
                        columns.append(picked)
                    halves.append(jnp.concatenate(columns, axis=1))
                rows = pl.multiple_of((first + top + pair) * width, 2 * width)
                out_ref[pl.ds(rows, 2 * width), :] = jnp.concatenate(halves, axis=0).astype(jnp.bfloat16)
        return carry

    lax.fori_loop(0, subs // group, several, 0)


def decode(ids, book_t):
    subs, width, _ = book_t.shape
    slots = ids[0].shape[1]
    return pl.pallas_call(
        decode_kernel,
        out_shape=jax.ShapeDtypeStruct((subs * width, slots), jnp.bfloat16),
        in_specs=[pl.BlockSpec(memory_space=pltpu.VMEM)] * (len(ids) + 1),
        out_specs=pl.BlockSpec(memory_space=pltpu.VMEM),
        compiler_params=pltpu.CompilerParams(vmem_limit_bytes=8 * 1024 * 1024),
        cost_estimate=pl.CostEstimate(flops=0, bytes_accessed=2 * 1024 * 1024, transcendentals=0),
        name="decode",
    )(*ids, book_t)


def vectors_kernel(in_ref, own_ref, other_ref, out_ref, grads_ref, flat_ref):
    rank_dim, tokens = in_ref.shape
    parts, tests, dims = out_ref.shape
    pairs = rank_dim // 2
    tall = dims // LANES
    in_side = in_ref[...]
    test_of = lax.broadcasted_iota(jnp.int32, in_side.shape, 1) // SEQ
    grads_ref[:, :rank_dim] = lax.dot_general(
        jnp.concatenate([jnp.where(test_of == test, in_side, 0.0) for test in range(tests)], axis=0),
        own_ref[...] + other_ref[...],
        (((1,), (1,)), ((), ())),
        precision=lax.Precision.HIGHEST,
        preferred_element_type=jnp.float32,
    )
    for test in range(tests):
        even = grads_ref[pl.ds(test * rank_dim, pairs, stride=2), :][:, :rank_dim]
        odd = grads_ref[pl.ds(test * rank_dim + 1, pairs, stride=2), :][:, :rank_dim]
        both = jnp.concatenate([even, odd], axis=1)
        squares = jnp.sum(jnp.sum(both * both, axis=0, keepdims=True), axis=1, keepdims=True)
        mean = squares * (1.0 / (rank_dim * rank_dim))
        flat_ref[test * pairs : (test + 1) * pairs, :] = both * (lax.rsqrt(mean + 1e-06) / rank_dim)
    for part in range(parts):
        for row in range(tall):
            out_ref[part, :, row * LANES : (row + 1) * LANES] = flat_ref[
                pl.ds(part * tall + row, tests, stride=pairs), :
            ]


def score_kernel(*refs):
    own_ref, *vector_refs, near_ref, far_ref, out_ref = refs
    tests = own_ref.shape[1]
    core = lax.axis_index("sub")
    own = lax.axis_index("dp")
    total = None
    for part, table_ref in ((core, near_ref), (1 - core, far_ref)):
        vectors = [ref[part] for ref in vector_refs]
        at = GATHER_ORDER.index(0)
        vectors[at] = jnp.where(core == 0, own_ref[part], vectors[at])
        vectors = jnp.concatenate(vectors, axis=0)
        high = vectors.astype(jnp.bfloat16)
        low = (vectors - high.astype(jnp.float32)).astype(jnp.bfloat16)
        both = jnp.dot(
            jnp.concatenate([high, low], axis=0), table_ref[...], preferred_element_type=jnp.float32
        )
        total = both if total is None else total + both
    blocks = len(vector_refs)
    total = total[: blocks * tests] + total[blocks * tests :]
    rows = [None] * blocks
    for at, xor in enumerate(GATHER_ORDER):
        rows[xor] = total[at * tests : (at + 1) * tests]
    step = 1
    while step < blocks:
        rows = [jnp.where((own & step) != 0, rows[at ^ step], rows[at]) for at in range(blocks)]
        step *= 2
    out_ref[...] = jnp.concatenate(rows, axis=0)


def score_blocks(own, blocks, near, far):
    tests = blocks[0].shape[1]
    return pl.pallas_call(
        score_kernel,
        out_shape=jax.ShapeDtypeStruct((len(blocks) * tests, near.shape[1]), jnp.float32),
        in_specs=[pl.BlockSpec(memory_space=pltpu.VMEM)] * (len(blocks) + 3),
        out_specs=pl.BlockSpec(memory_space=pltpu.VMEM),
        compiler_params=pltpu.CompilerParams(vmem_limit_bytes=8 * 1024 * 1024),
        name="score",
    )(own, *blocks, near, far)


def score(vectors, table):
    tests = vectors.shape[0]
    both = jnp.dot(
        jnp.concatenate(split_high_low(vectors), axis=0), table, preferred_element_type=jnp.float32
    )
    return both[:tests] + both[tests:]


def make_vectors(in_side, own, other, dims_local):
    rank_dim, tokens = in_side.shape
    tests = tokens // SEQ
    return pl.pallas_call(
        vectors_kernel,
        out_shape=jax.ShapeDtypeStruct((rank_dim * rank_dim // dims_local, tests, dims_local), jnp.float32),
        in_specs=[pl.BlockSpec(memory_space=pltpu.VMEM)] * 3,
        out_specs=pl.BlockSpec(memory_space=pltpu.VMEM),
        scratch_shapes=[
            pltpu.VMEM((tests * rank_dim, LANES), jnp.float32),
            pltpu.VMEM((tests * rank_dim // 2, LANES), jnp.float32),
        ],
        compiler_params=pltpu.CompilerParams(vmem_limit_bytes=4 * 1024 * 1024),
        name="vectors",
    )(in_side, own, other)


def split_high_low(x):
    high = lax.reduce_precision(x, 8, 7)
    return high.astype(jnp.bfloat16), (x - high).astype(jnp.bfloat16)


def partners(size, step):
    return [(i, i ^ step) for i in range(size)]


def is_power_of_two(n):
    return n & (n - 1) == 0


def sum_over_dp(x, sent, beside):
    size, cores = lax.axis_size("dp"), lax.axis_size("sub")
    beside = list(beside)
    made = []
    if not is_power_of_two(size):
        return lax.psum(x, "dp"), [work() for work in beside]
    steps = [1 << at for at in range(size.bit_length() - 1)]
    for steps_of_core in zip(steps, steps[::-1]):
        pairs = [
            (cores * at + core, cores * (at ^ steps_of_core[1 - core % 2]) + core)
            for at in range(size)
            for core in range(cores)
        ]
        got = lax.ppermute(sent, ("dp", "sub"), pairs)
        if beside:
            got, done = lax.optimization_barrier((got, beside.pop(0)()))
            made.append(done)
        x = x + got.astype(jnp.float32) * (1.0 / LINK_SCALE)
        sent = (x * LINK_SCALE).astype(jnp.float16)
    return x, made + [work() for work in beside]


def gather_over_dp(x):
    size = lax.axis_size("dp")
    if size > 4 or not is_power_of_two(size):
        return lax.all_gather(x, "dp", axis=0)
    own = lax.axis_index("dp")
    got = jnp.zeros((size,) + x.shape, x.dtype)
    got = lax.dynamic_update_index_in_dim(got, x, own, 0)
    for step in (2, 3, 1):
        block = lax.ppermute(x, "dp", partners(size, step))
        got = lax.dynamic_update_index_in_dim(got, block, own ^ step, 0)
    return got


def has_two_by_two():
    return lax.axis_size("layer") == 2 and lax.axis_size("sub") == 2


NEAR_CODES = [(3, 1), (1, 3)]
FAR_CODES = [(1, 0), (3, 2), (2, 1), (0, 3)]


def gather_by_core(x):
    size = lax.axis_size("dp")
    blocks = []
    for step in GATHER_ORDER:
        pairs = [
            (4 * at + 2 * layer + core, 4 * (at ^ step) + 2 * (layer ^ core) + core)
            for at in range(size)
            for layer in range(2)
            for core in range(2)
        ]
        if not step:
            pairs = [(i, i ^ 2) for i in range(4 * size)]
        blocks.append(lax.ppermute(x, ("dp", "layer", "sub"), pairs))
    return blocks


def per_device(acts, kv_grad, kv_weight, proj_in, proj_out, codebook, codes, counts):
    rank_dim = proj_in.shape[1]
    sub_local, code_count, sub_width = codebook.shape
    train_local = codes.shape[0]
    dims_local = sub_local * sub_width
    live_rows = jnp.arange(train_local, dtype=jnp.int32) < counts[0]

    rows_local = kv_weight.shape[1]
    own_rows = lax.optimization_barrier(
        lax.dynamic_slice_in_dim(
            jnp.transpose(proj_out), lax.axis_index("dp") * rows_local, rows_local, 1
        )
    )
    folded = jnp.dot(own_rows, kv_weight[0], preferred_element_type=jnp.float32)
    book_t = jnp.transpose(codebook, (0, 2, 1))
    by_core = has_two_by_two() and lax.axis_size("dp") == 4

    sent = (folded * LINK_SCALE).astype(jnp.float16)
    live = jnp.broadcast_to(live_rows, (8, train_local)).astype(jnp.float32)
    live, moved_codes = lax.optimization_barrier((live, codes))
    ids = make_ids(moved_codes)
    if by_core:
        sent, moved_book = lax.optimization_barrier((sent, codebook))
        near_ids = lax.ppermute(ids, "layer", partners(2, 1))
        far_ids = lax.ppermute(ids, ("layer", "sub"), FAR_CODES)
        other_book = lax.ppermute(moved_book, "sub", partners(2, 1))

    def first_side():
        return lax.dot_general(
            proj_in, acts[0], (((0,), (1,)), ((), ())), preferred_element_type=jnp.float32
        )

    def tables():
        if not by_core:
            return (decode([ids], book_t),)
        far = decode([far_ids], jnp.transpose(other_book, (0, 2, 1)))
        far, late_ids = lax.optimization_barrier((far, near_ids))
        return decode([ids, late_ids], book_t), far

    folded, (live, decoded) = sum_over_dp(
        folded, sent, [lambda: live, tables]
    )
    out_side = lax.dot_general(
        jnp.concatenate(split_high_low(folded), axis=0),
        kv_grad[0],
        (((1,), (1,)), ((), ())),
        preferred_element_type=jnp.float32,
    )
    out_side = out_side[:rank_dim] + out_side[rank_dim:]
    other_side = lax.psum(out_side, "sub") - out_side if lax.axis_size("sub") != 2 else (
        lax.ppermute(out_side, "sub", partners(2, 1))
    )
    other_side, in_side = lax.optimization_barrier((other_side, first_side()))
    vectors = make_vectors(in_side, out_side, other_side, dims_local)
    sent = (vectors * VECTOR_SCALE).astype(jnp.float16)
    core = lax.axis_index("sub")
    if by_core:
        blocks = [
            block.astype(jnp.float32) * (1.0 / VECTOR_SCALE) for block in gather_by_core(sent)
        ]
        total = score_blocks(vectors, blocks, *decoded)
        total = total + lax.ppermute(total, "sub", partners(2, 1))
    else:
        every = gather_over_dp(lax.dynamic_index_in_dim(sent, core, 0, False))
        every = every.reshape(-1, dims_local).astype(jnp.float32) * (1.0 / VECTOR_SCALE)
        total = lax.psum(score(every, decoded[0]), ("layer", "sub"))
    return jnp.transpose(jnp.where(live[:1] > 0.0, total, jnp.float32(0.0)))


def solution(mesh):
    return jax.shard_map(
        per_device,
        mesh=mesh,
        in_specs=(
            P("layer", ("groups", "dp"), None),
            P("layer", ("groups", "dp"), "sub"),
            P("layer", "dp", "sub"),
            P(),
            P(),
            P("sub", None, None),
            P(("groups", "dp"), "layer", "sub"),
            P(("groups", "dp")),
        ),
        out_specs=P(("groups", "dp"), None),
        check_vma=False,
    )
```

```python
import math

import jax
import jax.numpy as jnp
from jax import lax
from jax.experimental import pallas as pl
from jax.experimental.pallas import tpu as pltpu
from jax.sharding import PartitionSpec as P

SEQ = 64
LANES = 128
LINK_SCALE = 1024.0
VECTOR_SCALE = 16384.0
GATHER_ORDER = (0, 1, 2, 3)


def rows_kernel(proj_ref, out_ref, sem):
    rows = out_ref.shape[1]
    first = pl.multiple_of(lax.axis_index("dp") * rows, LANES)
    copy = pltpu.make_async_copy(proj_ref.at[:, pl.ds(first, rows)], out_ref, sem)
    copy.start()
    copy.wait()


def take_rows(proj_t, rows):
    return pl.pallas_call(
        rows_kernel,
        out_shape=jax.ShapeDtypeStruct((proj_t.shape[0], rows), proj_t.dtype),
        in_specs=[pl.BlockSpec(memory_space=pl.ANY)],
        out_specs=pl.BlockSpec(memory_space=pltpu.VMEM),
        scratch_shapes=[pltpu.SemaphoreType.DMA],
        compiler_params=pltpu.CompilerParams(vmem_limit_bytes=1024 * 1024),
        name="rows",
    )(proj_t)


def ids_kernel(codes_ref, out_ref):
    slots, _, subs = codes_ref.shape
    for left in range(0, slots, LANES):
        for top in range(0, subs, LANES):
            block = codes_ref[left : left + LANES, 0, top : top + LANES]
            out_ref[top : top + LANES, left : left + LANES] = (
                jnp.transpose(block).astype(jnp.float32).astype(jnp.bfloat16)
            )


def make_ids(codes):
    slots, _, subs = codes.shape
    return pl.pallas_call(
        ids_kernel,
        out_shape=jax.ShapeDtypeStruct((subs, slots), jnp.bfloat16),
        in_specs=[pl.BlockSpec(memory_space=pltpu.VMEM)],
        out_specs=pl.BlockSpec(memory_space=pltpu.VMEM),
        compiler_params=pltpu.CompilerParams(vmem_limit_bytes=4 * 1024 * 1024),
        name="ids",
    )(codes)


def decode_kernel(*refs):
    *ids_refs, book_ref, out_ref = refs
    core = lax.axis_index("sub")
    subs, width, code_count = book_ref.shape
    slots = ids_refs[0].shape[1]
    group = math.gcd(subs, 64)

    def several(step, carry):
        first = pl.multiple_of(step * group, group)
        for top in range(0, group, 16):
            rows = pl.ds(pl.multiple_of(first + top, 16), 16)
            ids = [ref[rows, :].astype(jnp.float32) for ref in ids_refs]
            ids = jnp.where(core == 0, ids[0], ids[-1]).astype(jnp.int32)
            for pair in range(0, 16, 2):
                halves = []
                for sub in (pair, pair + 1):
                    table = book_ref[first + top + sub].astype(jnp.float32)
                    columns = []
                    for left in range(0, slots, LANES):
                        own = jnp.broadcast_to(ids[sub : sub + 1, left : left + LANES], (width, LANES))
                        spot = own & (LANES - 1)
                        picked = None
                        for part in range(0, code_count, LANES):
                            found = jnp.take_along_axis(
                                table[:, part : part + LANES], spot, axis=1, mode="promise_in_bounds"
                            )
                            picked = found if picked is None else jnp.where(own >= part, found, picked)
                        columns.append(picked)
                    halves.append(jnp.concatenate(columns, axis=1))
                rows = pl.multiple_of((first + top + pair) * width, 2 * width)
                out_ref[pl.ds(rows, 2 * width), :] = jnp.concatenate(halves, axis=0).astype(jnp.bfloat16)
        return carry

    lax.fori_loop(0, subs // group, several, 0)


def decode(ids, book_t):
    subs, width, _ = book_t.shape
    slots = ids[0].shape[1]
    return pl.pallas_call(
        decode_kernel,
        out_shape=jax.ShapeDtypeStruct((subs * width, slots), jnp.bfloat16),
        in_specs=[pl.BlockSpec(memory_space=pltpu.VMEM)] * (len(ids) + 1),
        out_specs=pl.BlockSpec(memory_space=pltpu.VMEM),
        compiler_params=pltpu.CompilerParams(vmem_limit_bytes=8 * 1024 * 1024),
        cost_estimate=pl.CostEstimate(flops=0, bytes_accessed=2 * 1024 * 1024, transcendentals=0),
        name="decode",
    )(*ids, book_t)


def vectors_kernel(in_ref, own_ref, other_ref, out_ref, grads_ref, flat_ref):
    rank_dim, tokens = in_ref.shape
    parts, tests, dims = out_ref.shape
    pairs = rank_dim // 2
    tall = dims // LANES
    in_side = in_ref[...]
    test_of = lax.broadcasted_iota(jnp.int32, in_side.shape, 1) // SEQ
    grads_ref[:, :rank_dim] = lax.dot_general(
        jnp.concatenate([jnp.where(test_of == test, in_side, 0.0) for test in range(tests)], axis=0),
        own_ref[...] + other_ref[...],
        (((1,), (1,)), ((), ())),
        precision=lax.Precision.HIGHEST,
        preferred_element_type=jnp.float32,
    )
    for test in range(tests):
        even = grads_ref[pl.ds(test * rank_dim, pairs, stride=2), :][:, :rank_dim]
        odd = grads_ref[pl.ds(test * rank_dim + 1, pairs, stride=2), :][:, :rank_dim]
        both = jnp.concatenate([even, odd], axis=1)
        squares = jnp.sum(jnp.sum(both * both, axis=0, keepdims=True), axis=1, keepdims=True)
        mean = squares * (1.0 / (rank_dim * rank_dim))
        flat_ref[test * pairs : (test + 1) * pairs, :] = both * (lax.rsqrt(mean + 1e-06) / rank_dim)
    for part in range(parts):
        for row in range(tall):
            out_ref[part, :, row * LANES : (row + 1) * LANES] = flat_ref[
                pl.ds(part * tall + row, tests, stride=pairs), :
            ]


def score_kernel(*refs):
    own_ref, *vector_refs, near_ref, far_ref, out_ref = refs
    tests = own_ref.shape[1]
    core = lax.axis_index("sub")
    own = lax.axis_index("dp")
    total = None
    for part, table_ref in ((core, near_ref), (1 - core, far_ref)):
        vectors = [ref[part] for ref in vector_refs]
        at = GATHER_ORDER.index(0)
        vectors[at] = jnp.where(core == 0, own_ref[part], vectors[at])
        vectors = jnp.concatenate(vectors, axis=0)
        high = vectors.astype(jnp.bfloat16)
        low = (vectors - high.astype(jnp.float32)).astype(jnp.bfloat16)
        both = jnp.dot(
            jnp.concatenate([high, low], axis=0), table_ref[...], preferred_element_type=jnp.float32
        )
        total = both if total is None else total + both
    blocks = len(vector_refs)
    total = total[: blocks * tests] + total[blocks * tests :]
    rows = [None] * blocks
    for at, xor in enumerate(GATHER_ORDER):
        rows[xor] = total[at * tests : (at + 1) * tests]
    step = 1
    while step < blocks:
        rows = [jnp.where((own & step) != 0, rows[at ^ step], rows[at]) for at in range(blocks)]
        step *= 2
    out_ref[...] = jnp.concatenate(rows, axis=0)


def score_blocks(own, blocks, near, far):
    tests = blocks[0].shape[1]
    return pl.pallas_call(
        score_kernel,
        out_shape=jax.ShapeDtypeStruct((len(blocks) * tests, near.shape[1]), jnp.float32),
        in_specs=[pl.BlockSpec(memory_space=pltpu.VMEM)] * (len(blocks) + 3),
        out_specs=pl.BlockSpec(memory_space=pltpu.VMEM),
        compiler_params=pltpu.CompilerParams(vmem_limit_bytes=8 * 1024 * 1024),
        name="score",
    )(own, *blocks, near, far)


def score(vectors, table):
    tests = vectors.shape[0]
    both = jnp.dot(
        jnp.concatenate(split_high_low(vectors), axis=0), table, preferred_element_type=jnp.float32
    )
    return both[:tests] + both[tests:]


def make_vectors(in_side, own, other, dims_local):
    rank_dim, tokens = in_side.shape
    tests = tokens // SEQ
    return pl.pallas_call(
        vectors_kernel,
        out_shape=jax.ShapeDtypeStruct((rank_dim * rank_dim // dims_local, tests, dims_local), jnp.float32),
        in_specs=[pl.BlockSpec(memory_space=pltpu.VMEM)] * 3,
        out_specs=pl.BlockSpec(memory_space=pltpu.VMEM),
        scratch_shapes=[
            pltpu.VMEM((tests * rank_dim, LANES), jnp.float32),
            pltpu.VMEM((tests * rank_dim // 2, LANES), jnp.float32),
        ],
        compiler_params=pltpu.CompilerParams(vmem_limit_bytes=4 * 1024 * 1024),
        name="vectors",
    )(in_side, own, other)


def split_high_low(x):
    high = lax.reduce_precision(x, 8, 7)
    return high.astype(jnp.bfloat16), (x - high).astype(jnp.bfloat16)


def partners(size, step):
    return [(i, i ^ step) for i in range(size)]


def is_power_of_two(n):
    return n & (n - 1) == 0


def sum_over_dp(x, sent, beside):
    size, cores = lax.axis_size("dp"), lax.axis_size("sub")
    beside = list(beside)
    made = []
    if not is_power_of_two(size):
        return lax.psum(x, "dp"), [work() for work in beside]
    steps = [1 << at for at in range(size.bit_length() - 1)]
    for steps_of_core in zip(steps, steps[::-1]):
        pairs = [
            (cores * at + core, cores * (at ^ steps_of_core[1 - core % 2]) + core)
            for at in range(size)
            for core in range(cores)
        ]
        got = lax.ppermute(sent, ("dp", "sub"), pairs)
        if beside:
            got, done = lax.optimization_barrier((got, beside.pop(0)()))
            made.append(done)
        x = x + got.astype(jnp.float32) * (1.0 / LINK_SCALE)
        sent = (x * LINK_SCALE).astype(jnp.float16)
    return x, made + [work() for work in beside]


def gather_over_dp(x):
    size = lax.axis_size("dp")
    if size > 4 or not is_power_of_two(size):
        return lax.all_gather(x, "dp", axis=0)
    own = lax.axis_index("dp")
    got = jnp.zeros((size,) + x.shape, x.dtype)
    got = lax.dynamic_update_index_in_dim(got, x, own, 0)
    for step in (2, 3, 1):
        block = lax.ppermute(x, "dp", partners(size, step))
        got = lax.dynamic_update_index_in_dim(got, block, own ^ step, 0)
    return got


def has_two_by_two():
    return lax.axis_size("layer") == 2 and lax.axis_size("sub") == 2


NEAR_CODES = [(3, 1), (1, 3)]
FAR_CODES = [(1, 0), (3, 2), (2, 1), (0, 3)]


def gather_by_core(x):
    size = lax.axis_size("dp")
    blocks = []
    for step in GATHER_ORDER:
        pairs = [
            (4 * at + 2 * layer + core, 4 * (at ^ step) + 2 * (layer ^ core) + core)
            for at in range(size)
            for layer in range(2)
            for core in range(2)
        ]
        if not step:
            pairs = [(i, i ^ 2) for i in range(4 * size)]
        blocks.append(lax.ppermute(x, ("dp", "layer", "sub"), pairs))
    return blocks


def per_device(acts, kv_grad, kv_weight, proj_in, proj_out, codebook, codes, counts):
    rank_dim = proj_in.shape[1]
    sub_local, code_count, sub_width = codebook.shape
    train_local = codes.shape[0]
    dims_local = sub_local * sub_width
    live_rows = jnp.arange(train_local, dtype=jnp.int32) < counts[0]

    rows_local = kv_weight.shape[1]
    own_rows = lax.optimization_barrier(
        lax.dynamic_slice_in_dim(
            jnp.transpose(proj_out), lax.axis_index("dp") * rows_local, rows_local, 1
        )
    )
    folded = jnp.dot(own_rows, kv_weight[0], preferred_element_type=jnp.float32)
    book_t = jnp.transpose(codebook, (0, 2, 1))
    by_core = has_two_by_two() and lax.axis_size("dp") == 4

    sent = (folded * LINK_SCALE).astype(jnp.float16)
    live = jnp.broadcast_to(live_rows, (8, train_local)).astype(jnp.float32)
    live, moved_codes = lax.optimization_barrier((live, codes))
    ids = make_ids(moved_codes)
    if by_core:
        sent, moved_book = lax.optimization_barrier((sent, codebook))
        near_ids = lax.ppermute(ids, "layer", partners(2, 1))
        far_ids = lax.ppermute(ids, ("layer", "sub"), FAR_CODES)
        other_book = lax.ppermute(moved_book, "sub", partners(2, 1))

    def first_side():
        return lax.dot_general(
            proj_in, acts[0], (((0,), (1,)), ((), ())), preferred_element_type=jnp.float32
        )

    def tables():
        if not by_core:
            return (decode([ids], book_t),)
        far = decode([far_ids], jnp.transpose(other_book, (0, 2, 1)))
        far, late_ids = lax.optimization_barrier((far, near_ids))
        return decode([ids, late_ids], book_t), far

    folded, (live, decoded) = sum_over_dp(
        folded, sent, [lambda: live, tables]
    )
    out_side = lax.dot_general(
        jnp.concatenate(split_high_low(folded), axis=0),
        kv_grad[0],
        (((1,), (1,)), ((), ())),
        preferred_element_type=jnp.float32,
    )
    out_side = out_side[:rank_dim] + out_side[rank_dim:]
    other_side = lax.psum(out_side, "sub") - out_side if lax.axis_size("sub") != 2 else (
        lax.ppermute(out_side, "sub", partners(2, 1))
    )
    other_side, in_side = lax.optimization_barrier((other_side, first_side()))
    vectors = make_vectors(in_side, out_side, other_side, dims_local)
    sent = (vectors * VECTOR_SCALE).astype(jnp.float16)
    core = lax.axis_index("sub")
    if by_core:
        blocks = [
            block.astype(jnp.float32) * (1.0 / VECTOR_SCALE) for block in gather_by_core(sent)
        ]
        total = score_blocks(vectors, blocks, *decoded)
        total = total + lax.ppermute(total, "sub", partners(2, 1))
    else:
        every = gather_over_dp(lax.dynamic_index_in_dim(sent, core, 0, False))
        every = every.reshape(-1, dims_local).astype(jnp.float32) * (1.0 / VECTOR_SCALE)
        total = lax.psum(score(every, decoded[0]), ("layer", "sub"))
    return jnp.transpose(jnp.where(live[:1] > 0.0, total, jnp.float32(0.0)))


def solution(mesh):
    return jax.shard_map(
        per_device,
        mesh=mesh,
        in_specs=(
            P("layer", ("groups", "dp"), None),
            P("layer", ("groups", "dp"), "sub"),
            P("layer", "dp", "sub"),
            P(),
            P(),
            P("sub", None, None),
            P(("groups", "dp"), "layer", "sub"),
            P(("groups", "dp")),
        ),
        out_specs=P(("groups", "dp"), None),
        check_vma=False,
    )
```

```python
import math

import jax
import jax.numpy as jnp
from jax import lax
from jax.experimental import pallas as pl
from jax.experimental.pallas import tpu as pltpu
from jax.sharding import PartitionSpec as P

SEQ = 64
LANES = 128
LINK_SCALE = 1024.0
VECTOR_SCALE = 16384.0
GATHER_ORDER = (0, 1, 2, 3)


def ids_kernel(codes_ref, out_ref):
    slots, _, subs = codes_ref.shape
    for left in range(0, slots, LANES):
        for top in range(0, subs, LANES):
            block = codes_ref[left : left + LANES, 0, top : top + LANES]
            out_ref[top : top + LANES, left : left + LANES] = (
                jnp.transpose(block).astype(jnp.float32).astype(jnp.bfloat16)
            )


def make_ids(codes):
    slots, _, subs = codes.shape
    return pl.pallas_call(
        ids_kernel,
        out_shape=jax.ShapeDtypeStruct((subs, slots), jnp.bfloat16),
        in_specs=[pl.BlockSpec(memory_space=pltpu.VMEM)],
        out_specs=pl.BlockSpec(memory_space=pltpu.VMEM),
        compiler_params=pltpu.CompilerParams(vmem_limit_bytes=4 * 1024 * 1024),
        name="ids",
    )(codes)


def decode_kernel(*refs):
    *ids_refs, book_ref, out_ref = refs
    core = lax.axis_index("sub")
    subs, width, code_count = book_ref.shape
    slots = ids_refs[0].shape[1]
    group = math.gcd(subs, 64)

    def several(step, carry):
        first = pl.multiple_of(step * group, group)
        for top in range(0, group, 16):
            rows = pl.ds(pl.multiple_of(first + top, 16), 16)
            ids = [ref[rows, :].astype(jnp.float32) for ref in ids_refs]
            ids = jnp.where(core == 0, ids[0], ids[-1]).astype(jnp.int32)
            for pair in range(0, 16, 2):
                halves = []
                for sub in (pair, pair + 1):
                    table = book_ref[first + top + sub].astype(jnp.float32)
                    columns = []
                    for left in range(0, slots, LANES):
                        own = jnp.broadcast_to(ids[sub : sub + 1, left : left + LANES], (width, LANES))
                        spot = own & (LANES - 1)
                        picked = None
                        for part in range(0, code_count, LANES):
                            found = jnp.take_along_axis(
                                table[:, part : part + LANES], spot, axis=1, mode="promise_in_bounds"
                            )
                            picked = found if picked is None else jnp.where(own >= part, found, picked)
                        columns.append(picked)
                    halves.append(jnp.concatenate(columns, axis=1))
                rows = pl.multiple_of((first + top + pair) * width, 2 * width)
                out_ref[pl.ds(rows, 2 * width), :] = jnp.concatenate(halves, axis=0).astype(jnp.bfloat16)
        return carry

    lax.fori_loop(0, subs // group, several, 0)


def decode(ids, book_t):
    subs, width, _ = book_t.shape
    slots = ids[0].shape[1]
    return pl.pallas_call(
        decode_kernel,
        out_shape=jax.ShapeDtypeStruct((subs * width, slots), jnp.bfloat16),
        in_specs=[pl.BlockSpec(memory_space=pltpu.VMEM)] * (len(ids) + 1),
        out_specs=pl.BlockSpec(memory_space=pltpu.VMEM),
        compiler_params=pltpu.CompilerParams(vmem_limit_bytes=8 * 1024 * 1024),
        cost_estimate=pl.CostEstimate(flops=0, bytes_accessed=2 * 1024 * 1024, transcendentals=0),
        name="decode",
    )(*ids, book_t)


def split_in_kernel(x):
    high = x.astype(jnp.bfloat16)
    return high, (x - high.astype(jnp.float32)).astype(jnp.bfloat16)


def vectors_kernel(in_ref, own_ref, other_ref, out_ref, grads_ref, flat_ref):
    rank_dim, tokens = in_ref.shape
    parts, tests, dims = out_ref.shape
    pairs = rank_dim // 2
    tall = dims // LANES
    in_side = in_ref[...]
    test_of = lax.broadcasted_iota(jnp.int32, in_side.shape, 1) // SEQ
    out_side = own_ref[...] + other_ref[...]
    in_high, in_low = split_in_kernel(in_side)
    out_high, out_low = split_in_kernel(out_side)

    def by_test(x):
        zero = jnp.zeros_like(x)
        return jnp.concatenate([jnp.where(test_of == test, x, zero) for test in range(tests)], axis=0)

    def product(x, y):
        return lax.dot_general(
            x, y, (((1,), (1,)), ((), ())), preferred_element_type=jnp.float32
        )

    wide_high = by_test(in_high)
    grads_ref[:, :rank_dim] = product(wide_high, out_high) + (
        product(wide_high, out_low) + product(by_test(in_low), out_high)
    )
    for test in range(tests):
        even = grads_ref[pl.ds(test * rank_dim, pairs, stride=2), :][:, :rank_dim]
        odd = grads_ref[pl.ds(test * rank_dim + 1, pairs, stride=2), :][:, :rank_dim]
        both = jnp.concatenate([even, odd], axis=1)
        squares = jnp.sum(jnp.sum(both * both, axis=0, keepdims=True), axis=1, keepdims=True)
        mean = squares * (1.0 / (rank_dim * rank_dim))
        flat_ref[test * pairs : (test + 1) * pairs, :] = both * (lax.rsqrt(mean + 1e-06) / rank_dim)
    for part in range(parts):
        for row in range(tall):
            out_ref[part, :, row * LANES : (row + 1) * LANES] = flat_ref[
                pl.ds(part * tall + row, tests, stride=pairs), :
            ]


def score_kernel(*refs):
    own_ref, *vector_refs, near_ref, far_ref, out_ref = refs
    tests = own_ref.shape[1]
    core = lax.axis_index("sub")
    own = lax.axis_index("dp")
    total = None
    for part, table_ref in ((core, near_ref), (1 - core, far_ref)):
        vectors = [ref[part] for ref in vector_refs]
        at = GATHER_ORDER.index(0)
        vectors[at] = jnp.where(core == 0, own_ref[part], vectors[at])
        vectors = jnp.concatenate(vectors, axis=0)
        high = vectors.astype(jnp.bfloat16)
        low = (vectors - high.astype(jnp.float32)).astype(jnp.bfloat16)
        both = jnp.dot(
            jnp.concatenate([high, low], axis=0), table_ref[...], preferred_element_type=jnp.float32
        )
        total = both if total is None else total + both
    blocks = len(vector_refs)
    total = total[: blocks * tests] + total[blocks * tests :]
    rows = [None] * blocks
    for at, xor in enumerate(GATHER_ORDER):
        rows[xor] = total[at * tests : (at + 1) * tests]
    step = 1
    while step < blocks:
        rows = [jnp.where((own & step) != 0, rows[at ^ step], rows[at]) for at in range(blocks)]
        step *= 2
    out_ref[...] = jnp.concatenate(rows, axis=0)


def score_blocks(own, blocks, near, far):
    tests = blocks[0].shape[1]
    return pl.pallas_call(
        score_kernel,
        out_shape=jax.ShapeDtypeStruct((len(blocks) * tests, near.shape[1]), jnp.float32),
        in_specs=[pl.BlockSpec(memory_space=pltpu.VMEM)] * (len(blocks) + 3),
        out_specs=pl.BlockSpec(memory_space=pltpu.VMEM),
        compiler_params=pltpu.CompilerParams(vmem_limit_bytes=8 * 1024 * 1024),
        name="score",
    )(own, *blocks, near, far)


def score(vectors, table):
    tests = vectors.shape[0]
    both = jnp.dot(
        jnp.concatenate(split_high_low(vectors), axis=0), table, preferred_element_type=jnp.float32
    )
    return both[:tests] + both[tests:]


def make_vectors(in_side, own, other, dims_local):
    rank_dim, tokens = in_side.shape
    tests = tokens // SEQ
    return pl.pallas_call(
        vectors_kernel,
        out_shape=jax.ShapeDtypeStruct((rank_dim * rank_dim // dims_local, tests, dims_local), jnp.float32),
        in_specs=[pl.BlockSpec(memory_space=pltpu.VMEM)] * 3,
        out_specs=pl.BlockSpec(memory_space=pltpu.VMEM),
        scratch_shapes=[
            pltpu.VMEM((tests * rank_dim, LANES), jnp.float32),
            pltpu.VMEM((tests * rank_dim // 2, LANES), jnp.float32),
        ],
        compiler_params=pltpu.CompilerParams(vmem_limit_bytes=4 * 1024 * 1024),
        name="vectors",
    )(in_side, own, other)


def split_high_low(x):
    high = lax.reduce_precision(x, 8, 7)
    return high.astype(jnp.bfloat16), (x - high).astype(jnp.bfloat16)


def partners(size, step):
    return [(i, i ^ step) for i in range(size)]


def is_power_of_two(n):
    return n & (n - 1) == 0


def sum_over_dp(x, sent, beside):
    size, cores = lax.axis_size("dp"), lax.axis_size("sub")
    beside = list(beside)
    made = []
    if not is_power_of_two(size):
        return lax.psum(x, "dp"), [work() for work in beside]
    steps = [1 << at for at in range(size.bit_length() - 1)]
    for steps_of_core in zip(steps, steps[::-1]):
        pairs = [
            (cores * at + core, cores * (at ^ steps_of_core[1 - core % 2]) + core)
            for at in range(size)
            for core in range(cores)
        ]
        got = lax.ppermute(sent, ("dp", "sub"), pairs)
        if beside:
            got, done = lax.optimization_barrier((got, beside.pop(0)()))
            made.append(done)
        x = x + got.astype(jnp.float32) * (1.0 / LINK_SCALE)
        sent = (x * LINK_SCALE).astype(jnp.float16)
    return x, made + [work() for work in beside]


def gather_over_dp(x):
    size = lax.axis_size("dp")
    if size > 4 or not is_power_of_two(size):
        return lax.all_gather(x, "dp", axis=0)
    own = lax.axis_index("dp")
    got = jnp.zeros((size,) + x.shape, x.dtype)
    got = lax.dynamic_update_index_in_dim(got, x, own, 0)
    for step in reversed(range(1, size)):
        block = lax.ppermute(x, "dp", partners(size, step))
        got = lax.dynamic_update_index_in_dim(got, block, own ^ step, 0)
    return got


def has_two_by_two():
    return lax.axis_size("layer") == 2 and lax.axis_size("sub") == 2


FAR_CODES = [(1, 0), (3, 2), (2, 1), (0, 3)]


def gather_by_core(x):
    size = lax.axis_size("dp")
    blocks = []
    for step in GATHER_ORDER:
        pairs = [
            (4 * at + 2 * layer + core, 4 * (at ^ step) + 2 * (layer ^ core) + core)
            for at in range(size)
            for layer in range(2)
            for core in range(2)
        ]
        if not step:
            pairs = [(i, i ^ 2) for i in range(4 * size)]
        blocks.append(lax.ppermute(x, ("dp", "layer", "sub"), pairs))
    return blocks


def per_device(acts, kv_grad, kv_weight, proj_in, proj_out, codebook, codes, counts):
    rank_dim = proj_in.shape[1]
    sub_local, code_count, sub_width = codebook.shape
    train_local = codes.shape[0]
    dims_local = sub_local * sub_width
    live_rows = jnp.arange(train_local, dtype=jnp.int32) < counts[0]

    rows_local = kv_weight.shape[1]
    own_rows = lax.optimization_barrier(
        lax.dynamic_slice_in_dim(
            jnp.transpose(proj_out), lax.axis_index("dp") * rows_local, rows_local, 1
        )
    )
    own_rows, moved_book = lax.optimization_barrier((own_rows, codebook))
    folded = jnp.dot(own_rows, kv_weight[0], preferred_element_type=jnp.float32)
    book_t = jnp.transpose(codebook, (0, 2, 1))
    by_core = has_two_by_two() and lax.axis_size("dp") == 4

    sent = (folded * LINK_SCALE).astype(jnp.float16)
    live = jnp.broadcast_to(live_rows, (8, train_local)).astype(jnp.float32)
    live, moved_codes = lax.optimization_barrier((live, codes))
    ids = make_ids(moved_codes)
    if by_core:
        near_ids = lax.ppermute(ids, "layer", partners(2, 1))
        far_ids = lax.ppermute(ids, ("layer", "sub"), FAR_CODES)
        other_book = lax.ppermute(moved_book, "sub", partners(2, 1))

    def first_side():
        return lax.dot_general(
            proj_in, acts[0], (((0,), (1,)), ((), ())), preferred_element_type=jnp.float32
        )

    def tables():
        if not by_core:
            return (decode([ids], book_t),)
        far = decode([far_ids], jnp.transpose(other_book, (0, 2, 1)))
        far, late_ids = lax.optimization_barrier((far, near_ids))
        return decode([ids, late_ids], book_t), far

    folded, (live, decoded) = sum_over_dp(folded, sent, [lambda: live, tables])
    out_side = lax.dot_general(
        jnp.concatenate(split_high_low(folded), axis=0),
        kv_grad[0],
        (((1,), (1,)), ((), ())),
        preferred_element_type=jnp.float32,
    )
    out_side = out_side[:rank_dim] + out_side[rank_dim:]
    other_side = lax.psum(out_side, "sub") - out_side if lax.axis_size("sub") != 2 else (
        lax.ppermute(out_side, "sub", partners(2, 1))
    )
    other_side, in_side = lax.optimization_barrier((other_side, first_side()))
    vectors = make_vectors(in_side, out_side, other_side, dims_local)
    sent = (vectors * VECTOR_SCALE).astype(jnp.float16)
    core = lax.axis_index("sub")
    if by_core:
        blocks = [
            block.astype(jnp.float32) * (1.0 / VECTOR_SCALE) for block in gather_by_core(sent)
        ]
        total = score_blocks(vectors, blocks, *decoded)
        total = total + lax.ppermute(total, "sub", partners(2, 1))
    else:
        every = gather_over_dp(lax.dynamic_index_in_dim(sent, core, 0, False))
        every = every.reshape(-1, dims_local).astype(jnp.float32) * (1.0 / VECTOR_SCALE)
        total = lax.psum(score(every, decoded[0]), ("layer", "sub"))
    return jnp.transpose(jnp.where(live[:1] > 0.0, total, jnp.float32(0.0)))


def solution(mesh):
    return jax.shard_map(
        per_device,
        mesh=mesh,
        in_specs=(
            P("layer", ("groups", "dp"), None),
            P("layer", ("groups", "dp"), "sub"),
            P("layer", "dp", "sub"),
            P(),
            P(),
            P("sub", None, None),
            P(("groups", "dp"), "layer", "sub"),
            P(("groups", "dp")),
        ),
        out_specs=P(("groups", "dp"), None),
        check_vma=False,
    )
```

```python
import math

import jax
import jax.numpy as jnp
from jax import lax
from jax.experimental import pallas as pl
from jax.experimental.pallas import tpu as pltpu
from jax.sharding import PartitionSpec as P

SEQ = 64
LANES = 128
LINK_SCALE = 1024.0
VECTOR_SCALE = 16384.0
GATHER_ORDER = (2, 1, 0, 3)


def ids_kernel(codes_ref, out_ref):
    slots, _, subs = codes_ref.shape
    for left in range(0, slots, LANES):
        for top in range(0, subs, LANES):
            block = codes_ref[left : left + LANES, 0, top : top + LANES]
            out_ref[top : top + LANES, left : left + LANES] = (
                jnp.transpose(block).astype(jnp.float32).astype(jnp.bfloat16)
            )


def make_ids(codes):
    slots, _, subs = codes.shape
    return pl.pallas_call(
        ids_kernel,
        out_shape=jax.ShapeDtypeStruct((subs, slots), jnp.bfloat16),
        in_specs=[pl.BlockSpec(memory_space=pltpu.VMEM)],
        out_specs=pl.BlockSpec(memory_space=pltpu.VMEM),
        compiler_params=pltpu.CompilerParams(vmem_limit_bytes=4 * 1024 * 1024),
        name="ids",
    )(codes)


def decode_kernel(*refs):
    *ids_refs, book_ref, out_ref = refs
    core = lax.axis_index("sub")
    subs, width, code_count = book_ref.shape
    slots = ids_refs[0].shape[1]
    group = math.gcd(subs, 64)

    def several(step, carry):
        first = pl.multiple_of(step * group, group)
        for top in range(0, group, 16):
            rows = pl.ds(pl.multiple_of(first + top, 16), 16)
            ids = [ref[rows, :].astype(jnp.float32) for ref in ids_refs]
            ids = jnp.where(core == 0, ids[0], ids[-1]).astype(jnp.int32)
            for pair in range(0, 16, 2):
                halves = []
                for sub in (pair, pair + 1):
                    table = book_ref[first + top + sub].astype(jnp.float32)
                    columns = []
                    for left in range(0, slots, LANES):
                        own = jnp.broadcast_to(ids[sub : sub + 1, left : left + LANES], (width, LANES))
                        spot = own & (LANES - 1)
                        picked = None
                        for part in range(0, code_count, LANES):
                            found = jnp.take_along_axis(
                                table[:, part : part + LANES], spot, axis=1, mode="promise_in_bounds"
                            )
                            picked = found if picked is None else jnp.where(own >= part, found, picked)
                        columns.append(picked)
                    halves.append(jnp.concatenate(columns, axis=1))
                rows = pl.multiple_of((first + top + pair) * width, 2 * width)
                out_ref[pl.ds(rows, 2 * width), :] = jnp.concatenate(halves, axis=0).astype(jnp.bfloat16)
        return carry

    lax.fori_loop(0, subs // group, several, 0)


def decode(ids, book_t):
    subs, width, _ = book_t.shape
    slots = ids[0].shape[1]
    return pl.pallas_call(
        decode_kernel,
        out_shape=jax.ShapeDtypeStruct((subs * width, slots), jnp.bfloat16),
        in_specs=[pl.BlockSpec(memory_space=pltpu.VMEM)] * (len(ids) + 1),
        out_specs=pl.BlockSpec(memory_space=pltpu.VMEM),
        compiler_params=pltpu.CompilerParams(vmem_limit_bytes=8 * 1024 * 1024),
        cost_estimate=pl.CostEstimate(flops=0, bytes_accessed=2 * 1024 * 1024, transcendentals=0),
        name="decode",
    )(*ids, book_t)


def split_in_kernel(x):
    high = x.astype(jnp.bfloat16)
    return high, (x - high.astype(jnp.float32)).astype(jnp.bfloat16)


def vectors_kernel(in_ref, own_ref, other_ref, out_ref, grads_ref, flat_ref):
    rank_dim, tokens = in_ref.shape
    parts, tests, dims = out_ref.shape
    pairs = rank_dim // 2
    tall = dims // LANES
    in_side = in_ref[...]
    test_of = lax.broadcasted_iota(jnp.int32, in_side.shape, 1) // SEQ
    out_side = own_ref[...] + other_ref[...]
    in_high, in_low = split_in_kernel(in_side)
    out_high, out_low = split_in_kernel(out_side)

    def by_test(x):
        zero = jnp.zeros_like(x)
        return jnp.concatenate([jnp.where(test_of == test, x, zero) for test in range(tests)], axis=0)

    def product(x, y):
        return lax.dot_general(
            x, y, (((1,), (1,)), ((), ())), preferred_element_type=jnp.float32
        )

    wide_high = by_test(in_high)
    grads_ref[:, :rank_dim] = product(wide_high, out_high) + (
        product(wide_high, out_low) + product(by_test(in_low), out_high)
    )
    for test in range(tests):
        even = grads_ref[pl.ds(test * rank_dim, pairs, stride=2), :][:, :rank_dim]
        odd = grads_ref[pl.ds(test * rank_dim + 1, pairs, stride=2), :][:, :rank_dim]
        both = jnp.concatenate([even, odd], axis=1)
        squares = jnp.sum(jnp.sum(both * both, axis=0, keepdims=True), axis=1, keepdims=True)
        mean = squares * (1.0 / (rank_dim * rank_dim))
        flat_ref[test * pairs : (test + 1) * pairs, :] = both * (lax.rsqrt(mean + 1e-06) / rank_dim)
    for part in range(parts):
        for row in range(tall):
            out_ref[part, :, row * LANES : (row + 1) * LANES] = flat_ref[
                pl.ds(part * tall + row, tests, stride=pairs), :
            ]


def score_kernel(*refs):
    own_ref, *vector_refs, near_ref, far_ref, out_ref = refs
    tests = own_ref.shape[1]
    core = lax.axis_index("sub")
    own = lax.axis_index("dp")
    total = None
    for part, table_ref in ((core, near_ref), (1 - core, far_ref)):
        vectors = [ref[part] for ref in vector_refs]
        at = GATHER_ORDER.index(0)
        vectors[at] = jnp.where(core == 0, own_ref[part], vectors[at])
        vectors = jnp.concatenate(vectors, axis=0)
        high = vectors.astype(jnp.bfloat16)
        low = (vectors - high.astype(jnp.float32)).astype(jnp.bfloat16)
        both = jnp.dot(
            jnp.concatenate([high, low], axis=0), table_ref[...], preferred_element_type=jnp.float32
        )
        total = both if total is None else total + both
    blocks = len(vector_refs)
    total = total[: blocks * tests] + total[blocks * tests :]
    rows = [None] * blocks
    for at, xor in enumerate(GATHER_ORDER):
        rows[xor] = total[at * tests : (at + 1) * tests]
    step = 1
    while step < blocks:
        rows = [jnp.where((own & step) != 0, rows[at ^ step], rows[at]) for at in range(blocks)]
        step *= 2
    out_ref[...] = jnp.concatenate(rows, axis=0)


def score_blocks(own, blocks, near, far):
    tests = blocks[0].shape[1]
    return pl.pallas_call(
        score_kernel,
        out_shape=jax.ShapeDtypeStruct((len(blocks) * tests, near.shape[1]), jnp.float32),
        in_specs=[pl.BlockSpec(memory_space=pltpu.VMEM)] * (len(blocks) + 3),
        out_specs=pl.BlockSpec(memory_space=pltpu.VMEM),
        compiler_params=pltpu.CompilerParams(vmem_limit_bytes=8 * 1024 * 1024),
        name="score",
    )(own, *blocks, near, far)


def score(vectors, table):
    tests = vectors.shape[0]
    both = jnp.dot(
        jnp.concatenate(split_high_low(vectors), axis=0), table, preferred_element_type=jnp.float32
    )
    return both[:tests] + both[tests:]


def make_vectors(in_side, own, other, dims_local):
    rank_dim, tokens = in_side.shape
    tests = tokens // SEQ
    return pl.pallas_call(
        vectors_kernel,
        out_shape=jax.ShapeDtypeStruct((rank_dim * rank_dim // dims_local, tests, dims_local), jnp.float32),
        in_specs=[pl.BlockSpec(memory_space=pltpu.VMEM)] * 3,
        out_specs=pl.BlockSpec(memory_space=pltpu.VMEM),
        scratch_shapes=[
            pltpu.VMEM((tests * rank_dim, LANES), jnp.float32),
            pltpu.VMEM((tests * rank_dim // 2, LANES), jnp.float32),
        ],
        compiler_params=pltpu.CompilerParams(vmem_limit_bytes=4 * 1024 * 1024),
        name="vectors",
    )(in_side, own, other)


def split_high_low(x):
    high = lax.reduce_precision(x, 8, 7)
    return high.astype(jnp.bfloat16), (x - high).astype(jnp.bfloat16)


def partners(size, step):
    return [(i, i ^ step) for i in range(size)]


def is_power_of_two(n):
    return n & (n - 1) == 0


def sum_over_dp(x, sent, beside):
    size, cores = lax.axis_size("dp"), lax.axis_size("sub")
    beside = list(beside)
    made = []
    if not is_power_of_two(size):
        return lax.psum(x, "dp"), [work() for work in beside]
    steps = [1 << at for at in range(size.bit_length() - 1)]
    for steps_of_core in zip(steps, steps[::-1]):
        pairs = [
            (cores * at + core, cores * (at ^ steps_of_core[1 - core % 2]) + core)
            for at in range(size)
            for core in range(cores)
        ]
        got = lax.ppermute(sent, ("dp", "sub"), pairs)
        if beside:
            got, done = lax.optimization_barrier((got, beside.pop(0)()))
            made.append(done)
        x = x + got.astype(jnp.float32) * (1.0 / LINK_SCALE)
        sent = (x * LINK_SCALE).astype(jnp.float16)
    return x, made + [work() for work in beside]


def gather_over_dp(x):
    size = lax.axis_size("dp")
    if size > 4 or not is_power_of_two(size):
        return lax.all_gather(x, "dp", axis=0)
    own = lax.axis_index("dp")
    got = jnp.zeros((size,) + x.shape, x.dtype)
    got = lax.dynamic_update_index_in_dim(got, x, own, 0)
    for step in reversed(range(1, size)):
        block = lax.ppermute(x, "dp", partners(size, step))
        got = lax.dynamic_update_index_in_dim(got, block, own ^ step, 0)
    return got


def has_two_by_two():
    return lax.axis_size("layer") == 2 and lax.axis_size("sub") == 2


FAR_CODES = [(1, 0), (3, 2), (2, 1), (0, 3)]


def gather_by_core(x):
    size = lax.axis_size("dp")
    blocks = []
    for step in GATHER_ORDER:
        pairs = [
            (4 * at + 2 * layer + core, 4 * (at ^ step) + 2 * (layer ^ core) + core)
            for at in range(size)
            for layer in range(2)
            for core in range(2)
        ]
        if not step:
            pairs = [(i, i ^ 2) for i in range(4 * size)]
        blocks.append(lax.ppermute(x, ("dp", "layer", "sub"), pairs))
    return blocks


def per_device(acts, kv_grad, kv_weight, proj_in, proj_out, codebook, codes, counts):
    rank_dim = proj_in.shape[1]
    sub_local, code_count, sub_width = codebook.shape
    train_local = codes.shape[0]
    dims_local = sub_local * sub_width
    live_rows = jnp.arange(train_local, dtype=jnp.int32) < counts[0]

    rows_local = kv_weight.shape[1]
    own_rows = lax.optimization_barrier(
        lax.dynamic_slice_in_dim(
            jnp.transpose(proj_out), lax.axis_index("dp") * rows_local, rows_local, 1
        )
    )
    folded = jnp.dot(own_rows, kv_weight[0], preferred_element_type=jnp.float32)
    book_t = jnp.transpose(codebook, (0, 2, 1))
    by_core = has_two_by_two() and lax.axis_size("dp") == 4

    sent = (folded * LINK_SCALE).astype(jnp.float16)
    live = jnp.broadcast_to(live_rows, (8, train_local)).astype(jnp.float32)
    live, moved_codes = lax.optimization_barrier((live, codes))
    ids = make_ids(moved_codes)
    if by_core:
        sent, moved_book = lax.optimization_barrier((sent, codebook))
        near_moved = lax.ppermute(ids, "layer", partners(2, 1))
        far_ids = lax.ppermute(ids, ("layer", "sub"), FAR_CODES)
        other_book = lax.ppermute(moved_book, "sub", partners(2, 1))

    def first_side():
        return lax.dot_general(
            proj_in, acts[0], (((0,), (1,)), ((), ())), preferred_element_type=jnp.float32
        )

    def far_table():
        if not by_core:
            return decode([ids], book_t), ids
        return decode([far_ids], jnp.transpose(other_book, (0, 2, 1))), near_moved

    folded, (live, (far, near_ids)) = sum_over_dp(folded, sent, [lambda: live, far_table])
    out_side = lax.dot_general(
        jnp.concatenate(split_high_low(folded), axis=0),
        kv_grad[0],
        (((1,), (1,)), ((), ())),
        preferred_element_type=jnp.float32,
    )
    out_side = out_side[:rank_dim] + out_side[rank_dim:]
    other_side = lax.psum(out_side, "sub") - out_side if lax.axis_size("sub") != 2 else (
        lax.ppermute(out_side, "sub", partners(2, 1))
    )
    other_side, in_side = lax.optimization_barrier((other_side, first_side()))
    vectors = make_vectors(in_side, out_side, other_side, dims_local)
    sent = (vectors * VECTOR_SCALE).astype(jnp.float16)
    core = lax.axis_index("sub")
    if by_core:
        blocks = gather_by_core(sent)
        blocks[-1], own_ids, late_ids = lax.optimization_barrier((blocks[-1], ids, near_ids))
        near = decode([own_ids, late_ids], book_t)
        *blocks, near = lax.optimization_barrier((*blocks, near))
        blocks = [block.astype(jnp.float32) * (1.0 / VECTOR_SCALE) for block in blocks]
        total = score_blocks(vectors, blocks, near, far)
        total = total + lax.ppermute(total, "sub", partners(2, 1))
    else:
        every = gather_over_dp(lax.dynamic_index_in_dim(sent, core, 0, False))
        every = every.reshape(-1, dims_local).astype(jnp.float32) * (1.0 / VECTOR_SCALE)
        total = lax.psum(score(every, far), ("layer", "sub"))
    return jnp.transpose(jnp.where(live[:1] > 0.0, total, jnp.float32(0.0)))


def solution(mesh):
    return jax.shard_map(
        per_device,
        mesh=mesh,
        in_specs=(
            P("layer", ("groups", "dp"), None),
            P("layer", ("groups", "dp"), "sub"),
            P("layer", "dp", "sub"),
            P(),
            P(),
            P("sub", None, None),
            P(("groups", "dp"), "layer", "sub"),
            P(("groups", "dp")),
        ),
        out_specs=P(("groups", "dp"), None),
        check_vma=False,
    )
```

```python
import math

import jax
import jax.numpy as jnp
from jax import lax
from jax.experimental import pallas as pl
from jax.experimental.pallas import tpu as pltpu
from jax.sharding import PartitionSpec as P

SEQ = 64
LANES = 128
LINK_SCALE = 1024.0
VECTOR_SCALE = 16384.0
GATHER_ORDER = (2, 1, 0, 3)


def ids_kernel(codes_ref, out_ref):
    slots, _, subs = codes_ref.shape
    for left in range(0, slots, LANES):
        for top in range(0, subs, LANES):
            block = codes_ref[left : left + LANES, 0, top : top + LANES]
            out_ref[top : top + LANES, left : left + LANES] = (
                jnp.transpose(block).astype(jnp.float32).astype(jnp.bfloat16)
            )


def make_ids(codes):
    slots, _, subs = codes.shape
    return pl.pallas_call(
        ids_kernel,
        out_shape=jax.ShapeDtypeStruct((subs, slots), jnp.bfloat16),
        in_specs=[pl.BlockSpec(memory_space=pltpu.VMEM)],
        out_specs=pl.BlockSpec(memory_space=pltpu.VMEM),
        compiler_params=pltpu.CompilerParams(vmem_limit_bytes=4 * 1024 * 1024),
        name="ids",
    )(codes)


def decode_kernel(*refs):
    *ids_refs, book_ref, out_ref = refs
    core = lax.axis_index("sub")
    subs, width, code_count = book_ref.shape
    slots = ids_refs[0].shape[1]
    group = math.gcd(subs, 64)

    def several(step, carry):
        first = pl.multiple_of(step * group, group)
        for top in range(0, group, 16):
            rows = pl.ds(pl.multiple_of(first + top, 16), 16)
            ids = [ref[rows, :].astype(jnp.float32) for ref in ids_refs]
            ids = jnp.where(core == 0, ids[0], ids[-1]).astype(jnp.int32)
            for pair in range(0, 16, 2):
                halves = []
                for sub in (pair, pair + 1):
                    table = book_ref[first + top + sub].astype(jnp.float32)
                    columns = []
                    for left in range(0, slots, LANES):
                        own = jnp.broadcast_to(ids[sub : sub + 1, left : left + LANES], (width, LANES))
                        spot = own & (LANES - 1)
                        picked = None
                        for part in range(0, code_count, LANES):
                            found = jnp.take_along_axis(
                                table[:, part : part + LANES], spot, axis=1, mode="promise_in_bounds"
                            )
                            picked = found if picked is None else jnp.where(own >= part, found, picked)
                        columns.append(picked)
                    halves.append(jnp.concatenate(columns, axis=1))
                rows = pl.multiple_of((first + top + pair) * width, 2 * width)
                out_ref[pl.ds(rows, 2 * width), :] = jnp.concatenate(halves, axis=0).astype(jnp.bfloat16)
        return carry

    lax.fori_loop(0, subs // group, several, 0)


def decode(ids, book_t):
    subs, width, _ = book_t.shape
    slots = ids[0].shape[1]
    return pl.pallas_call(
        decode_kernel,
        out_shape=jax.ShapeDtypeStruct((subs * width, slots), jnp.bfloat16),
        in_specs=[pl.BlockSpec(memory_space=pltpu.VMEM)] * (len(ids) + 1),
        out_specs=pl.BlockSpec(memory_space=pltpu.VMEM),
        compiler_params=pltpu.CompilerParams(vmem_limit_bytes=8 * 1024 * 1024),
        cost_estimate=pl.CostEstimate(flops=0, bytes_accessed=2 * 1024 * 1024, transcendentals=0),
        name="decode",
    )(*ids, book_t)


def split_in_kernel(x):
    high = x.astype(jnp.bfloat16)
    return high, (x - high.astype(jnp.float32)).astype(jnp.bfloat16)


def vectors_kernel(in_ref, own_ref, other_ref, out_ref, grads_ref, flat_ref):
    rank_dim, tokens = in_ref.shape
    parts, tests, dims = out_ref.shape
    pairs = rank_dim // 2
    tall = dims // LANES
    in_side = in_ref[...]
    test_of = lax.broadcasted_iota(jnp.int32, in_side.shape, 1) // SEQ
    out_side = own_ref[...] + other_ref[...]
    in_high, in_low = split_in_kernel(in_side)
    out_high, out_low = split_in_kernel(out_side)

    def by_test(x):
        zero = jnp.zeros_like(x)
        return jnp.concatenate([jnp.where(test_of == test, x, zero) for test in range(tests)], axis=0)

    def product(x, y):
        return lax.dot_general(
            x, y, (((1,), (1,)), ((), ())), preferred_element_type=jnp.float32
        )

    wide_high = by_test(in_high)
    grads_ref[:, :rank_dim] = product(wide_high, out_high) + (
        product(wide_high, out_low) + product(by_test(in_low), out_high)
    )
    for test in range(tests):
        even = grads_ref[pl.ds(test * rank_dim, pairs, stride=2), :][:, :rank_dim]
        odd = grads_ref[pl.ds(test * rank_dim + 1, pairs, stride=2), :][:, :rank_dim]
        both = jnp.concatenate([even, odd], axis=1)
        squares = jnp.sum(jnp.sum(both * both, axis=0, keepdims=True), axis=1, keepdims=True)
        mean = squares * (1.0 / (rank_dim * rank_dim))
        flat_ref[test * pairs : (test + 1) * pairs, :] = both * (lax.rsqrt(mean + 1e-06) / rank_dim)
    for part in range(parts):
        for row in range(tall):
            out_ref[part, :, row * LANES : (row + 1) * LANES] = flat_ref[
                pl.ds(part * tall + row, tests, stride=pairs), :
            ]


def score_kernel(*refs):
    own_ref, *vector_refs, near_ref, far_ref, out_ref = refs
    tests = own_ref.shape[1]
    core = lax.axis_index("sub")
    own = lax.axis_index("dp")
    total = None
    for part, table_ref in ((core, near_ref), (1 - core, far_ref)):
        vectors = [ref[part] for ref in vector_refs]
        at = GATHER_ORDER.index(0)
        vectors[at] = jnp.where(core == 0, own_ref[part], vectors[at])
        vectors = jnp.concatenate(vectors, axis=0)
        high = vectors.astype(jnp.bfloat16)
        low = (vectors - high.astype(jnp.float32)).astype(jnp.bfloat16)
        both = jnp.dot(
            jnp.concatenate([high, low], axis=0), table_ref[...], preferred_element_type=jnp.float32
        )
        total = both if total is None else total + both
    blocks = len(vector_refs)
    total = total[: blocks * tests] + total[blocks * tests :]
    rows = [None] * blocks
    for at, xor in enumerate(GATHER_ORDER):
        rows[xor] = total[at * tests : (at + 1) * tests]
    step = 1
    while step < blocks:
        rows = [jnp.where((own & step) != 0, rows[at ^ step], rows[at]) for at in range(blocks)]
        step *= 2
    out_ref[...] = jnp.concatenate(rows, axis=0)


def score_blocks(own, blocks, near, far):
    tests = blocks[0].shape[1]
    return pl.pallas_call(
        score_kernel,
        out_shape=jax.ShapeDtypeStruct((len(blocks) * tests, near.shape[1]), jnp.float32),
        in_specs=[pl.BlockSpec(memory_space=pltpu.VMEM)] * (len(blocks) + 3),
        out_specs=pl.BlockSpec(memory_space=pltpu.VMEM),
        compiler_params=pltpu.CompilerParams(vmem_limit_bytes=8 * 1024 * 1024),
        name="score",
    )(own, *blocks, near, far)


def score(vectors, table):
    tests = vectors.shape[0]
    both = jnp.dot(
        jnp.concatenate(split_high_low(vectors), axis=0), table, preferred_element_type=jnp.float32
    )
    return both[:tests] + both[tests:]


def make_vectors(in_side, own, other, dims_local):
    rank_dim, tokens = in_side.shape
    tests = tokens // SEQ
    return pl.pallas_call(
        vectors_kernel,
        out_shape=jax.ShapeDtypeStruct((rank_dim * rank_dim // dims_local, tests, dims_local), jnp.float32),
        in_specs=[pl.BlockSpec(memory_space=pltpu.VMEM)] * 3,
        out_specs=pl.BlockSpec(memory_space=pltpu.VMEM),
        scratch_shapes=[
            pltpu.VMEM((tests * rank_dim, LANES), jnp.float32),
            pltpu.VMEM((tests * rank_dim // 2, LANES), jnp.float32),
        ],
        compiler_params=pltpu.CompilerParams(vmem_limit_bytes=4 * 1024 * 1024),
        name="vectors",
    )(in_side, own, other)


def split_high_low(x):
    high = lax.reduce_precision(x, 8, 7)
    return high.astype(jnp.bfloat16), (x - high).astype(jnp.bfloat16)


def partners(size, step):
    return [(i, i ^ step) for i in range(size)]


def is_power_of_two(n):
    return n & (n - 1) == 0


def sum_over_dp(x, sent, beside):
    size, cores = lax.axis_size("dp"), lax.axis_size("sub")
    beside = list(beside)
    made = []
    if not is_power_of_two(size):
        return lax.psum(x, "dp"), [work() for work in beside]
    steps = [1 << at for at in range(size.bit_length() - 1)]
    for steps_of_core in zip(steps, steps[::-1]):
        pairs = [
            (cores * at + core, cores * (at ^ steps_of_core[1 - core % 2]) + core)
            for at in range(size)
            for core in range(cores)
        ]
        got = lax.ppermute(sent, ("dp", "sub"), pairs)
        if beside:
            got, done = lax.optimization_barrier((got, beside.pop(0)()))
            made.append(done)
        x = x + got.astype(jnp.float32) * (1.0 / LINK_SCALE)
        sent = (x * LINK_SCALE).astype(jnp.float16)
    return x, made + [work() for work in beside]


def gather_over_dp(x):
    size = lax.axis_size("dp")
    if size > 4 or not is_power_of_two(size):
        return lax.all_gather(x, "dp", axis=0)
    own = lax.axis_index("dp")
    got = jnp.zeros((size,) + x.shape, x.dtype)
    got = lax.dynamic_update_index_in_dim(got, x, own, 0)
    for step in reversed(range(1, size)):
        block = lax.ppermute(x, "dp", partners(size, step))
        got = lax.dynamic_update_index_in_dim(got, block, own ^ step, 0)
    return got


def has_two_by_two():
    return lax.axis_size("layer") == 2 and lax.axis_size("sub") == 2


FAR_CODES = [(1, 0), (3, 2), (2, 1), (0, 3)]


def gather_by_core(x):
    size = lax.axis_size("dp")
    blocks = []
    for step in GATHER_ORDER:
        pairs = [
            (4 * at + 2 * layer + core, 4 * (at ^ step) + 2 * (layer ^ core) + core)
            for at in range(size)
            for layer in range(2)
            for core in range(2)
        ]
        if not step:
            pairs = [(i, i ^ 2) for i in range(4 * size)]
        blocks.append(lax.ppermute(x, ("dp", "layer", "sub"), pairs))
    return blocks


def per_device(acts, kv_grad, kv_weight, proj_in, proj_out, codebook, codes, counts):
    rank_dim = proj_in.shape[1]
    sub_local, code_count, sub_width = codebook.shape
    train_local = codes.shape[0]
    dims_local = sub_local * sub_width
    live_rows = jnp.arange(train_local, dtype=jnp.int32) < counts[0]

    rows_local = kv_weight.shape[1]
    own_rows = lax.optimization_barrier(
        lax.dynamic_slice_in_dim(
            jnp.transpose(proj_out), lax.axis_index("dp") * rows_local, rows_local, 1
        )
    )
    own_rows, moved_book = lax.optimization_barrier((own_rows, codebook))
    folded = jnp.dot(own_rows, kv_weight[0], preferred_element_type=jnp.float32)
    book_t = jnp.transpose(codebook, (0, 2, 1))
    by_core = has_two_by_two() and lax.axis_size("dp") == 4

    sent = (folded * LINK_SCALE).astype(jnp.float16)
    live = jnp.broadcast_to(live_rows, (8, train_local)).astype(jnp.float32)
    live, moved_codes = lax.optimization_barrier((live, codes))
    ids = make_ids(moved_codes)
    if by_core:
        near_moved = lax.ppermute(ids, "layer", partners(2, 1))
        far_ids = lax.ppermute(ids, ("layer", "sub"), FAR_CODES)
        other_book = lax.ppermute(moved_book, "sub", partners(2, 1))

    def first_side():
        return lax.dot_general(
            proj_in, acts[0], (((0,), (1,)), ((), ())), preferred_element_type=jnp.float32
        )

    def far_table():
        if not by_core:
            return decode([ids], book_t), ids
        return decode([far_ids], jnp.transpose(other_book, (0, 2, 1))), near_moved

    folded, (live, (far, near_ids)) = sum_over_dp(folded, sent, [lambda: live, far_table])
    out_side = lax.dot_general(
        jnp.concatenate(split_high_low(folded), axis=0),
        kv_grad[0],
        (((1,), (1,)), ((), ())),
        preferred_element_type=jnp.float32,
    )
    out_side = out_side[:rank_dim] + out_side[rank_dim:]
    other_side = lax.psum(out_side, "sub") - out_side if lax.axis_size("sub") != 2 else (
        lax.ppermute(out_side, "sub", partners(2, 1))
    )
    other_side, in_side = lax.optimization_barrier((other_side, first_side()))
    vectors = make_vectors(in_side, out_side, other_side, dims_local)
    sent = (vectors * VECTOR_SCALE).astype(jnp.float16)
    core = lax.axis_index("sub")
    if by_core:
        blocks = gather_by_core(sent)
        blocks[-1], own_ids, late_ids = lax.optimization_barrier((blocks[-1], ids, near_ids))
        near = decode([own_ids, late_ids], book_t)
        *blocks, near = lax.optimization_barrier((*blocks, near))
        blocks = [block.astype(jnp.float32) * (1.0 / VECTOR_SCALE) for block in blocks]
        total = score_blocks(vectors, blocks, near, far)
        total = total + lax.ppermute(total, "sub", partners(2, 1))
    else:
        every = gather_over_dp(lax.dynamic_index_in_dim(sent, core, 0, False))
        every = every.reshape(-1, dims_local).astype(jnp.float32) * (1.0 / VECTOR_SCALE)
        total = lax.psum(score(every, far), ("layer", "sub"))
    return jnp.transpose(jnp.where(live[:1] > 0.0, total, jnp.float32(0.0)))


def solution(mesh):
    return jax.shard_map(
        per_device,
        mesh=mesh,
        in_specs=(
            P("layer", ("groups", "dp"), None),
            P("layer", ("groups", "dp"), "sub"),
            P("layer", "dp", "sub"),
            P(),
            P(),
            P("sub", None, None),
            P(("groups", "dp"), "layer", "sub"),
            P(("groups", "dp")),
        ),
        out_specs=P(("groups", "dp"), None),
        check_vma=False,
    )
```

```python
import math

import jax
import jax.numpy as jnp
from jax import lax
from jax.experimental import pallas as pl
from jax.experimental.pallas import tpu as pltpu
from jax.sharding import PartitionSpec as P

SEQ = 64
LANES = 128
LINK_SCALE = 1024.0
VECTOR_SCALE = 16384.0
GATHER_ORDER = (0, 1, 2, 3)


def ids_kernel(codes_ref, out_ref):
    slots, _, subs = codes_ref.shape
    for left in range(0, slots, LANES):
        for top in range(0, subs, LANES):
            block = codes_ref[left : left + LANES, 0, top : top + LANES]
            out_ref[top : top + LANES, left : left + LANES] = (
                jnp.transpose(block).astype(jnp.float32).astype(jnp.bfloat16)
            )


def make_ids(codes):
    slots, _, subs = codes.shape
    return pl.pallas_call(
        ids_kernel,
        out_shape=jax.ShapeDtypeStruct((subs, slots), jnp.bfloat16),
        in_specs=[pl.BlockSpec(memory_space=pltpu.VMEM)],
        out_specs=pl.BlockSpec(memory_space=pltpu.VMEM),
        compiler_params=pltpu.CompilerParams(vmem_limit_bytes=4 * 1024 * 1024),
        name="ids",
    )(codes)


def decode_kernel(*refs):
    *ids_refs, book_ref, out_ref = refs
    core = lax.axis_index("sub")
    subs, width, code_count = book_ref.shape
    slots = ids_refs[0].shape[1]
    group = math.gcd(subs, 64)

    def several(step, carry):
        first = pl.multiple_of(step * group, group)
        for top in range(0, group, 16):
            rows = pl.ds(pl.multiple_of(first + top, 16), 16)
            ids = [ref[rows, :].astype(jnp.float32) for ref in ids_refs]
            ids = jnp.where(core == 0, ids[0], ids[-1]).astype(jnp.int32)
            for pair in range(0, 16, 2):
                halves = []
                for sub in (pair, pair + 1):
                    table = book_ref[first + top + sub].astype(jnp.float32)
                    columns = []
                    for left in range(0, slots, LANES):
                        own = jnp.broadcast_to(ids[sub : sub + 1, left : left + LANES], (width, LANES))
                        spot = own & (LANES - 1)
                        picked = None
                        for part in range(0, code_count, LANES):
                            found = jnp.take_along_axis(
                                table[:, part : part + LANES], spot, axis=1, mode="promise_in_bounds"
                            )
                            picked = found if picked is None else jnp.where(own >= part, found, picked)
                        columns.append(picked)
                    halves.append(jnp.concatenate(columns, axis=1))
                rows = pl.multiple_of((first + top + pair) * width, 2 * width)
                out_ref[pl.ds(rows, 2 * width), :] = jnp.concatenate(halves, axis=0).astype(jnp.bfloat16)
        return carry

    lax.fori_loop(0, subs // group, several, 0)


def decode(ids, book_t):
    subs, width, _ = book_t.shape
    slots = ids[0].shape[1]
    return pl.pallas_call(
        decode_kernel,
        out_shape=jax.ShapeDtypeStruct((subs * width, slots), jnp.bfloat16),
        in_specs=[pl.BlockSpec(memory_space=pltpu.VMEM)] * (len(ids) + 1),
        out_specs=pl.BlockSpec(memory_space=pltpu.VMEM),
        compiler_params=pltpu.CompilerParams(vmem_limit_bytes=8 * 1024 * 1024),
        cost_estimate=pl.CostEstimate(flops=0, bytes_accessed=2 * 1024 * 1024, transcendentals=0),
        name="decode",
    )(*ids, book_t)


def split_in_kernel(x):
    high = x.astype(jnp.bfloat16)
    return high, (x - high.astype(jnp.float32)).astype(jnp.bfloat16)


def vectors_kernel(in_ref, own_ref, other_ref, out_ref, grads_ref, flat_ref):
    rank_dim, tokens = in_ref.shape
    parts, tests, dims = out_ref.shape
    pairs = rank_dim // 2
    tall = dims // LANES
    in_side = in_ref[...]
    test_of = lax.broadcasted_iota(jnp.int32, in_side.shape, 1) // SEQ
    out_side = own_ref[...] + other_ref[...]
    in_high, in_low = split_in_kernel(in_side)
    out_high, out_low = split_in_kernel(out_side)

    def by_test(x):
        zero = jnp.zeros_like(x)
        return jnp.concatenate([jnp.where(test_of == test, x, zero) for test in range(tests)], axis=0)

    def product(x, y):
        return lax.dot_general(
            x, y, (((1,), (1,)), ((), ())), preferred_element_type=jnp.float32
        )

    wide_high = by_test(in_high)
    grads_ref[:, :rank_dim] = product(wide_high, out_high) + (
        product(wide_high, out_low) + product(by_test(in_low), out_high)
    )
    for test in range(tests):
        even = grads_ref[pl.ds(test * rank_dim, pairs, stride=2), :][:, :rank_dim]
        odd = grads_ref[pl.ds(test * rank_dim + 1, pairs, stride=2), :][:, :rank_dim]
        both = jnp.concatenate([even, odd], axis=1)
        squares = jnp.sum(jnp.sum(both * both, axis=0, keepdims=True), axis=1, keepdims=True)
        mean = squares * (1.0 / (rank_dim * rank_dim))
        flat_ref[test * pairs : (test + 1) * pairs, :] = both * (lax.rsqrt(mean + 1e-06) / rank_dim)
    for part in range(parts):
        for row in range(tall):
            out_ref[part, :, row * LANES : (row + 1) * LANES] = flat_ref[
                pl.ds(part * tall + row, tests, stride=pairs), :
            ]


def score_kernel(*refs):
    own_ref, *vector_refs, near_ref, far_ref, out_ref = refs
    tests = own_ref.shape[1]
    core = lax.axis_index("sub")
    own = lax.axis_index("dp")
    total = None
    for part, table_ref in ((core, near_ref), (1 - core, far_ref)):
        vectors = [ref[part] for ref in vector_refs]
        at = GATHER_ORDER.index(0)
        vectors[at] = jnp.where(core == 0, own_ref[part], vectors[at])
        vectors = jnp.concatenate(vectors, axis=0)
        high = vectors.astype(jnp.bfloat16)
        low = (vectors - high.astype(jnp.float32)).astype(jnp.bfloat16)
        both = jnp.dot(
            jnp.concatenate([high, low], axis=0), table_ref[...], preferred_element_type=jnp.float32
        )
        total = both if total is None else total + both
    blocks = len(vector_refs)
    total = total[: blocks * tests] + total[blocks * tests :]
    rows = [None] * blocks
    for at, xor in enumerate(GATHER_ORDER):
        rows[xor] = total[at * tests : (at + 1) * tests]
    step = 1
    while step < blocks:
        rows = [jnp.where((own & step) != 0, rows[at ^ step], rows[at]) for at in range(blocks)]
        step *= 2
    out_ref[...] = jnp.concatenate(rows, axis=0)


def score_blocks(own, blocks, near, far):
    tests = blocks[0].shape[1]
    return pl.pallas_call(
        score_kernel,
        out_shape=jax.ShapeDtypeStruct((len(blocks) * tests, near.shape[1]), jnp.float32),
        in_specs=[pl.BlockSpec(memory_space=pltpu.VMEM)] * (len(blocks) + 3),
        out_specs=pl.BlockSpec(memory_space=pltpu.VMEM),
        compiler_params=pltpu.CompilerParams(vmem_limit_bytes=8 * 1024 * 1024),
        name="score",
    )(own, *blocks, near, far)


def score(vectors, table):
    tests = vectors.shape[0]
    both = jnp.dot(
        jnp.concatenate(split_high_low(vectors), axis=0), table, preferred_element_type=jnp.float32
    )
    return both[:tests] + both[tests:]


def make_vectors(in_side, own, other, dims_local):
    rank_dim, tokens = in_side.shape
    tests = tokens // SEQ
    return pl.pallas_call(
        vectors_kernel,
        out_shape=jax.ShapeDtypeStruct((rank_dim * rank_dim // dims_local, tests, dims_local), jnp.float32),
        in_specs=[pl.BlockSpec(memory_space=pltpu.VMEM)] * 3,
        out_specs=pl.BlockSpec(memory_space=pltpu.VMEM),
        scratch_shapes=[
            pltpu.VMEM((tests * rank_dim, LANES), jnp.float32),
            pltpu.VMEM((tests * rank_dim // 2, LANES), jnp.float32),
        ],
        compiler_params=pltpu.CompilerParams(vmem_limit_bytes=4 * 1024 * 1024),
        name="vectors",
    )(in_side, own, other)


def split_high_low(x):
    high = lax.reduce_precision(x, 8, 7)
    return high.astype(jnp.bfloat16), (x - high).astype(jnp.bfloat16)


def partners(size, step):
    return [(i, i ^ step) for i in range(size)]


def is_power_of_two(n):
    return n & (n - 1) == 0


def sum_over_dp(x, sent, beside):
    size, cores = lax.axis_size("dp"), lax.axis_size("sub")
    beside = list(beside)
    made = []
    if not is_power_of_two(size):
        return lax.psum(x, "dp"), [work() for work in beside]
    steps = [1 << at for at in range(size.bit_length() - 1)]
    for steps_of_core in zip(steps, steps[::-1]):
        pairs = [
            (cores * at + core, cores * (at ^ steps_of_core[1 - core % 2]) + core)
            for at in range(size)
            for core in range(cores)
        ]
        got = lax.ppermute(sent, ("dp", "sub"), pairs)
        if beside:
            got, done = lax.optimization_barrier((got, beside.pop(0)()))
            made.append(done)
        x = x + got.astype(jnp.float32) * (1.0 / LINK_SCALE)
        sent = (x * LINK_SCALE).astype(jnp.float16)
    return x, made + [work() for work in beside]


def gather_over_dp(x):
    size = lax.axis_size("dp")
    if size > 4 or not is_power_of_two(size):
        return lax.all_gather(x, "dp", axis=0)
    own = lax.axis_index("dp")
    got = jnp.zeros((size,) + x.shape, x.dtype)
    got = lax.dynamic_update_index_in_dim(got, x, own, 0)
    for step in reversed(range(1, size)):
        block = lax.ppermute(x, "dp", partners(size, step))
        got = lax.dynamic_update_index_in_dim(got, block, own ^ step, 0)
    return got


def has_two_by_two():
    return lax.axis_size("layer") == 2 and lax.axis_size("sub") == 2


FAR_CODES = [(1, 0), (3, 2), (2, 1), (0, 3)]


def gather_by_core(x):
    size = lax.axis_size("dp")
    blocks = []
    for step in GATHER_ORDER:
        pairs = [
            (4 * at + 2 * layer + core, 4 * (at ^ step) + 2 * (layer ^ core) + core)
            for at in range(size)
            for layer in range(2)
            for core in range(2)
        ]
        if not step:
            pairs = [(i, i ^ 2) for i in range(4 * size)]
        blocks.append(lax.ppermute(x, ("dp", "layer", "sub"), pairs))
    return blocks


def per_device(acts, kv_grad, kv_weight, proj_in, proj_out, codebook, codes, counts):
    rank_dim = proj_in.shape[1]
    sub_local, code_count, sub_width = codebook.shape
    train_local = codes.shape[0]
    dims_local = sub_local * sub_width
    live_rows = jnp.arange(train_local, dtype=jnp.int32) < counts[0]

    rows_local = kv_weight.shape[1]
    own_rows = lax.optimization_barrier(
        lax.dynamic_slice_in_dim(
            jnp.transpose(proj_out), lax.axis_index("dp") * rows_local, rows_local, 1
        )
    )
    folded = jnp.dot(own_rows, kv_weight[0], preferred_element_type=jnp.float32)
    book_t = jnp.transpose(codebook, (0, 2, 1))
    by_core = has_two_by_two() and lax.axis_size("dp") == 4

    sent = (folded * LINK_SCALE).astype(jnp.float16)
    live = jnp.broadcast_to(live_rows, (8, train_local)).astype(jnp.float32)
    live, moved_codes = lax.optimization_barrier((live, codes))
    ids = make_ids(moved_codes)
    if by_core:
        sent, moved_book = lax.optimization_barrier((sent, codebook))
        near_ids = lax.ppermute(ids, "layer", partners(2, 1))
        far_ids = lax.ppermute(ids, ("layer", "sub"), FAR_CODES)
        other_book = lax.ppermute(moved_book, "sub", partners(2, 1))

    def first_side():
        return lax.dot_general(
            proj_in, acts[0], (((0,), (1,)), ((), ())), preferred_element_type=jnp.float32
        )

    def tables():
        if not by_core:
            return (decode([ids], book_t),)
        far = decode([far_ids], jnp.transpose(other_book, (0, 2, 1)))
        far, late_ids = lax.optimization_barrier((far, near_ids))
        return decode([ids, late_ids], book_t), far

    folded, (live, decoded) = sum_over_dp(folded, sent, [lambda: live, tables])
    out_side = lax.dot_general(
        jnp.concatenate(split_high_low(folded), axis=0),
        kv_grad[0],
        (((1,), (1,)), ((), ())),
        preferred_element_type=jnp.float32,
    )
    out_side = out_side[:rank_dim] + out_side[rank_dim:]
    other_side = lax.psum(out_side, "sub") - out_side if lax.axis_size("sub") != 2 else (
        lax.ppermute(out_side, "sub", partners(2, 1))
    )
    other_side, in_side = lax.optimization_barrier((other_side, first_side()))
    vectors = make_vectors(in_side, out_side, other_side, dims_local)
    sent = (vectors * VECTOR_SCALE).astype(jnp.float16)
    core = lax.axis_index("sub")
    if by_core:
        blocks = [
            block.astype(jnp.float32) * (1.0 / VECTOR_SCALE) for block in gather_by_core(sent)
        ]
        total = score_blocks(vectors, blocks, *decoded)
        total = total + lax.ppermute(total, "sub", partners(2, 1))
    else:
        every = gather_over_dp(lax.dynamic_index_in_dim(sent, core, 0, False))
        every = every.reshape(-1, dims_local).astype(jnp.float32) * (1.0 / VECTOR_SCALE)
        total = lax.psum(score(every, decoded[0]), ("layer", "sub"))
    return jnp.transpose(jnp.where(live[:1] > 0.0, total, jnp.float32(0.0)))


def solution(mesh):
    return jax.shard_map(
        per_device,
        mesh=mesh,
        in_specs=(
            P("layer", ("groups", "dp"), None),
            P("layer", ("groups", "dp"), "sub"),
            P("layer", "dp", "sub"),
            P(),
            P(),
            P("sub", None, None),
            P(("groups", "dp"), "layer", "sub"),
            P(("groups", "dp")),
        ),
        out_specs=P(("groups", "dp"), None),
        check_vma=False,
    )
```

```python
import math

import jax
import jax.numpy as jnp
from jax import lax
from jax.experimental import pallas as pl
from jax.experimental.pallas import tpu as pltpu
from jax.sharding import PartitionSpec as P

SEQ = 64
LANES = 128
LINK_SCALE = 1024.0
VECTOR_SCALE = 16384.0
GATHER_ORDER = (0, 2, 1, 3)


def ids_kernel(codes_ref, out_ref):
    slots, _, subs = codes_ref.shape
    for left in range(0, slots, LANES):
        for top in range(0, subs, LANES):
            block = codes_ref[left : left + LANES, 0, top : top + LANES]
            out_ref[top : top + LANES, left : left + LANES] = (
                jnp.transpose(block).astype(jnp.float32).astype(jnp.bfloat16)
            )


def make_ids(codes):
    slots, _, subs = codes.shape
    return pl.pallas_call(
        ids_kernel,
        out_shape=jax.ShapeDtypeStruct((subs, slots), jnp.bfloat16),
        in_specs=[pl.BlockSpec(memory_space=pltpu.VMEM)],
        out_specs=pl.BlockSpec(memory_space=pltpu.VMEM),
        compiler_params=pltpu.CompilerParams(vmem_limit_bytes=4 * 1024 * 1024),
        name="ids",
    )(codes)


def decode_kernel(*refs):
    *ids_refs, book_ref, out_ref = refs
    core = lax.axis_index("sub")
    subs, width, code_count = book_ref.shape
    slots = ids_refs[0].shape[1]
    group = math.gcd(subs, 64)

    def several(step, carry):
        first = pl.multiple_of(step * group, group)
        for top in range(0, group, 16):
            rows = pl.ds(pl.multiple_of(first + top, 16), 16)
            ids = [ref[rows, :].astype(jnp.float32) for ref in ids_refs]
            ids = jnp.where(core == 0, ids[0], ids[-1]).astype(jnp.int32)
            for pair in range(0, 16, 2):
                halves = []
                for sub in (pair, pair + 1):
                    table = book_ref[first + top + sub].astype(jnp.float32)
                    columns = []
                    for left in range(0, slots, LANES):
                        own = jnp.broadcast_to(ids[sub : sub + 1, left : left + LANES], (width, LANES))
                        spot = own & (LANES - 1)
                        picked = None
                        for part in range(0, code_count, LANES):
                            found = jnp.take_along_axis(
                                table[:, part : part + LANES], spot, axis=1, mode="promise_in_bounds"
                            )
                            picked = found if picked is None else jnp.where(own >= part, found, picked)
                        columns.append(picked)
                    halves.append(jnp.concatenate(columns, axis=1))
                rows = pl.multiple_of((first + top + pair) * width, 2 * width)
                out_ref[pl.ds(rows, 2 * width), :] = jnp.concatenate(halves, axis=0).astype(jnp.bfloat16)
        return carry

    lax.fori_loop(0, subs // group, several, 0)


def decode(ids, book_t):
    subs, width, _ = book_t.shape
    slots = ids[0].shape[1]
    return pl.pallas_call(
        decode_kernel,
        out_shape=jax.ShapeDtypeStruct((subs * width, slots), jnp.bfloat16),
        in_specs=[pl.BlockSpec(memory_space=pltpu.VMEM)] * (len(ids) + 1),
        out_specs=pl.BlockSpec(memory_space=pltpu.VMEM),
        compiler_params=pltpu.CompilerParams(vmem_limit_bytes=8 * 1024 * 1024),
        cost_estimate=pl.CostEstimate(flops=0, bytes_accessed=2 * 1024 * 1024, transcendentals=0),
        name="decode",
    )(*ids, book_t)


def split_in_kernel(x):
    high = x.astype(jnp.bfloat16)
    return high, (x - high.astype(jnp.float32)).astype(jnp.bfloat16)


def vectors_kernel(in_ref, own_ref, other_ref, out_ref, grads_ref, flat_ref):
    rank_dim, tokens = in_ref.shape
    parts, tests, dims = out_ref.shape
    pairs = rank_dim // 2
    tall = dims // LANES
    in_side = in_ref[...]
    test_of = lax.broadcasted_iota(jnp.int32, in_side.shape, 1) // SEQ
    out_side = own_ref[...] + other_ref[...]
    in_high, in_low = split_in_kernel(in_side)
    out_high, out_low = split_in_kernel(out_side)

    def by_test(x):
        zero = jnp.zeros_like(x)
        return jnp.concatenate([jnp.where(test_of == test, x, zero) for test in range(tests)], axis=0)

    def product(x, y):
        return lax.dot_general(
            x, y, (((1,), (1,)), ((), ())), preferred_element_type=jnp.float32
        )

    wide_high = by_test(in_high)
    grads_ref[:, :rank_dim] = product(wide_high, out_high) + (
        product(wide_high, out_low) + product(by_test(in_low), out_high)
    )
    for test in range(tests):
        even = grads_ref[pl.ds(test * rank_dim, pairs, stride=2), :][:, :rank_dim]
        odd = grads_ref[pl.ds(test * rank_dim + 1, pairs, stride=2), :][:, :rank_dim]
        both = jnp.concatenate([even, odd], axis=1)
        squares = jnp.sum(jnp.sum(both * both, axis=0, keepdims=True), axis=1, keepdims=True)
        mean = squares * (1.0 / (rank_dim * rank_dim))
        flat_ref[test * pairs : (test + 1) * pairs, :] = both * (lax.rsqrt(mean + 1e-06) / rank_dim)
    for part in range(parts):
        for row in range(tall):
            out_ref[part, :, row * LANES : (row + 1) * LANES] = flat_ref[
                pl.ds(part * tall + row, tests, stride=pairs), :
            ]


def score_kernel(*refs):
    own_ref, *vector_refs, near_ref, far_ref, out_ref = refs
    tests = own_ref.shape[1]
    core = lax.axis_index("sub")
    own = lax.axis_index("dp")
    total = None
    for part, table_ref in ((core, near_ref), (1 - core, far_ref)):
        vectors = [ref[part] for ref in vector_refs]
        at = GATHER_ORDER.index(0)
        vectors[at] = jnp.where(core == 0, own_ref[part], vectors[at])
        vectors = jnp.concatenate(vectors, axis=0)
        high = vectors.astype(jnp.bfloat16)
        low = (vectors - high.astype(jnp.float32)).astype(jnp.bfloat16)
        both = jnp.dot(
            jnp.concatenate([high, low], axis=0), table_ref[...], preferred_element_type=jnp.float32
        )
        total = both if total is None else total + both
    blocks = len(vector_refs)
    total = total[: blocks * tests] + total[blocks * tests :]
    rows = [None] * blocks
    for at, xor in enumerate(GATHER_ORDER):
        rows[xor] = total[at * tests : (at + 1) * tests]
    step = 1
    while step < blocks:
        rows = [jnp.where((own & step) != 0, rows[at ^ step], rows[at]) for at in range(blocks)]
        step *= 2
    out_ref[...] = jnp.concatenate(rows, axis=0)


def score_blocks(own, blocks, near, far):
    tests = blocks[0].shape[1]
    return pl.pallas_call(
        score_kernel,
        out_shape=jax.ShapeDtypeStruct((len(blocks) * tests, near.shape[1]), jnp.float32),
        in_specs=[pl.BlockSpec(memory_space=pltpu.VMEM)] * (len(blocks) + 3),
        out_specs=pl.BlockSpec(memory_space=pltpu.VMEM),
        compiler_params=pltpu.CompilerParams(vmem_limit_bytes=8 * 1024 * 1024),
        name="score",
    )(own, *blocks, near, far)


def score(vectors, table):
    tests = vectors.shape[0]
    both = jnp.dot(
        jnp.concatenate(split_high_low(vectors), axis=0), table, preferred_element_type=jnp.float32
    )
    return both[:tests] + both[tests:]


def make_vectors(in_side, own, other, dims_local):
    rank_dim, tokens = in_side.shape
    tests = tokens // SEQ
    return pl.pallas_call(
        vectors_kernel,
        out_shape=jax.ShapeDtypeStruct((rank_dim * rank_dim // dims_local, tests, dims_local), jnp.float32),
        in_specs=[pl.BlockSpec(memory_space=pltpu.VMEM)] * 3,
        out_specs=pl.BlockSpec(memory_space=pltpu.VMEM),
        scratch_shapes=[
            pltpu.VMEM((tests * rank_dim, LANES), jnp.float32),
            pltpu.VMEM((tests * rank_dim // 2, LANES), jnp.float32),
        ],
        compiler_params=pltpu.CompilerParams(vmem_limit_bytes=4 * 1024 * 1024),
        name="vectors",
    )(in_side, own, other)


def split_high_low(x):
    high = lax.reduce_precision(x, 8, 7)
    return high.astype(jnp.bfloat16), (x - high).astype(jnp.bfloat16)


def partners(size, step):
    return [(i, i ^ step) for i in range(size)]


def is_power_of_two(n):
    return n & (n - 1) == 0


def sum_over_dp(x, sent, beside):
    size, cores = lax.axis_size("dp"), lax.axis_size("sub")
    beside = list(beside)
    made = []
    if not is_power_of_two(size):
        return lax.psum(x, "dp"), [work() for work in beside]
    steps = [1 << at for at in range(size.bit_length() - 1)]
    for steps_of_core in zip(steps, steps[::-1]):
        pairs = [
            (cores * at + core, cores * (at ^ steps_of_core[1 - core % 2]) + core)
            for at in range(size)
            for core in range(cores)
        ]
        got = lax.ppermute(sent, ("dp", "sub"), pairs)
        if beside:
            got, done = lax.optimization_barrier((got, beside.pop(0)()))
            made.append(done)
        x = x + got.astype(jnp.float32) * (1.0 / LINK_SCALE)
        sent = (x * LINK_SCALE).astype(jnp.float16)
    return x, made + [work() for work in beside]


def gather_over_dp(x):
    size = lax.axis_size("dp")
    if size > 4 or not is_power_of_two(size):
        return lax.all_gather(x, "dp", axis=0)
    own = lax.axis_index("dp")
    got = jnp.zeros((size,) + x.shape, x.dtype)
    got = lax.dynamic_update_index_in_dim(got, x, own, 0)
    for step in reversed(range(1, size)):
        block = lax.ppermute(x, "dp", partners(size, step))
        got = lax.dynamic_update_index_in_dim(got, block, own ^ step, 0)
    return got


def has_two_by_two():
    return lax.axis_size("layer") == 2 and lax.axis_size("sub") == 2


FAR_CODES = [(1, 0), (3, 2), (2, 1), (0, 3)]


def gather_by_core(x):
    size = lax.axis_size("dp")
    blocks = []
    for step in GATHER_ORDER:
        pairs = [
            (4 * at + 2 * layer + core, 4 * (at ^ step) + 2 * (layer ^ core) + core)
            for at in range(size)
            for layer in range(2)
            for core in range(2)
        ]
        if not step:
            pairs = [(i, i ^ 2) for i in range(4 * size)]
        blocks.append(lax.ppermute(x, ("dp", "layer", "sub"), pairs))
    return blocks


def per_device(acts, kv_grad, kv_weight, proj_in, proj_out, codebook, codes, counts):
    rank_dim = proj_in.shape[1]
    sub_local, code_count, sub_width = codebook.shape
    train_local = codes.shape[0]
    dims_local = sub_local * sub_width
    live_rows = jnp.arange(train_local, dtype=jnp.int32) < counts[0]

    rows_local = kv_weight.shape[1]
    own_rows = lax.optimization_barrier(
        lax.dynamic_slice_in_dim(
            jnp.transpose(proj_out), lax.axis_index("dp") * rows_local, rows_local, 1
        )
    )
    folded = jnp.dot(own_rows, kv_weight[0], preferred_element_type=jnp.float32)
    book_t = jnp.transpose(codebook, (0, 2, 1))
    by_core = has_two_by_two() and lax.axis_size("dp") == 4

    sent = (folded * LINK_SCALE).astype(jnp.float16)
    live = jnp.broadcast_to(live_rows, (8, train_local)).astype(jnp.float32)
    live, moved_codes = lax.optimization_barrier((live, codes))
    ids = make_ids(moved_codes)
    if by_core:
        sent, moved_book = lax.optimization_barrier((sent, codebook))
        near_ids = lax.ppermute(ids, "layer", partners(2, 1))
        far_ids = lax.ppermute(ids, ("layer", "sub"), FAR_CODES)
        other_book = lax.ppermute(moved_book, "sub", partners(2, 1))

    def first_side():
        return lax.dot_general(
            proj_in, acts[0], (((0,), (1,)), ((), ())), preferred_element_type=jnp.float32
        )

    def tables():
        if not by_core:
            return (decode([ids], book_t),)
        far = decode([far_ids], jnp.transpose(other_book, (0, 2, 1)))
        far, late_ids = lax.optimization_barrier((far, near_ids))
        return decode([ids, late_ids], book_t), far

    folded, (live, decoded) = sum_over_dp(folded, sent, [lambda: live, tables])
    out_side = lax.dot_general(
        jnp.concatenate(split_high_low(folded), axis=0),
        kv_grad[0],
        (((1,), (1,)), ((), ())),
        preferred_element_type=jnp.float32,
    )
    out_side = out_side[:rank_dim] + out_side[rank_dim:]
    other_side = lax.psum(out_side, "sub") - out_side if lax.axis_size("sub") != 2 else (
        lax.ppermute(out_side, "sub", partners(2, 1))
    )
    other_side, in_side = lax.optimization_barrier((other_side, first_side()))
    vectors = make_vectors(in_side, out_side, other_side, dims_local)
    sent = (vectors * VECTOR_SCALE).astype(jnp.float16)
    core = lax.axis_index("sub")
    if by_core:
        blocks = [
            block.astype(jnp.float32) * (1.0 / VECTOR_SCALE) for block in gather_by_core(sent)
        ]
        total = score_blocks(vectors, blocks, *decoded)
        total = total + lax.ppermute(total, "sub", partners(2, 1))
    else:
        every = gather_over_dp(lax.dynamic_index_in_dim(sent, core, 0, False))
        every = every.reshape(-1, dims_local).astype(jnp.float32) * (1.0 / VECTOR_SCALE)
        total = lax.psum(score(every, decoded[0]), ("layer", "sub"))
    return jnp.transpose(jnp.where(live[:1] > 0.0, total, jnp.float32(0.0)))


def solution(mesh):
    return jax.shard_map(
        per_device,
        mesh=mesh,
        in_specs=(
            P("layer", ("groups", "dp"), None),
            P("layer", ("groups", "dp"), "sub"),
            P("layer", "dp", "sub"),
            P(),
            P(),
            P("sub", None, None),
            P(("groups", "dp"), "layer", "sub"),
            P(("groups", "dp")),
        ),
        out_specs=P(("groups", "dp"), None),
        check_vma=False,
    )
```

```python
import math

import jax
import jax.numpy as jnp
from jax import lax
from jax.experimental import pallas as pl
from jax.experimental.pallas import tpu as pltpu
from jax.sharding import PartitionSpec as P

SEQ = 64
LANES = 128
LINK_SCALE = 1024.0
VECTOR_SCALE = 16384.0
GATHER_ORDER = (1, 2, 0, 3)


def ids_kernel(codes_ref, out_ref):
    slots, _, subs = codes_ref.shape
    for left in range(0, slots, LANES):
        for top in range(0, subs, LANES):
            block = codes_ref[left : left + LANES, 0, top : top + LANES]
            out_ref[top : top + LANES, left : left + LANES] = (
                jnp.transpose(block).astype(jnp.float32).astype(jnp.bfloat16)
            )


def make_ids(codes):
    slots, _, subs = codes.shape
    return pl.pallas_call(
        ids_kernel,
        out_shape=jax.ShapeDtypeStruct((subs, slots), jnp.bfloat16),
        in_specs=[pl.BlockSpec(memory_space=pltpu.VMEM)],
        out_specs=pl.BlockSpec(memory_space=pltpu.VMEM),
        compiler_params=pltpu.CompilerParams(vmem_limit_bytes=4 * 1024 * 1024),
        name="ids",
    )(codes)


def decode_kernel(*refs):
    *ids_refs, book_ref, out_ref = refs
    core = lax.axis_index("sub")
    subs, width, code_count = book_ref.shape
    slots = ids_refs[0].shape[1]
    group = math.gcd(subs, 64)

    def several(step, carry):
        first = pl.multiple_of(step * group, group)
        for top in range(0, group, 16):
            rows = pl.ds(pl.multiple_of(first + top, 16), 16)
            ids = [ref[rows, :].astype(jnp.float32) for ref in ids_refs]
            ids = jnp.where(core == 0, ids[0], ids[-1]).astype(jnp.int32)
            for pair in range(0, 16, 2):
                halves = []
                for sub in (pair, pair + 1):
                    table = book_ref[first + top + sub].astype(jnp.float32)
                    columns = []
                    for left in range(0, slots, LANES):
                        own = jnp.broadcast_to(ids[sub : sub + 1, left : left + LANES], (width, LANES))
                        spot = own & (LANES - 1)
                        picked = None
                        for part in range(0, code_count, LANES):
                            found = jnp.take_along_axis(
                                table[:, part : part + LANES], spot, axis=1, mode="promise_in_bounds"
                            )
                            picked = found if picked is None else jnp.where(own >= part, found, picked)
                        columns.append(picked)
                    halves.append(jnp.concatenate(columns, axis=1))
                rows = pl.multiple_of((first + top + pair) * width, 2 * width)
                out_ref[pl.ds(rows, 2 * width), :] = jnp.concatenate(halves, axis=0).astype(jnp.bfloat16)
        return carry

    lax.fori_loop(0, subs // group, several, 0)


def decode(ids, book_t):
    subs, width, _ = book_t.shape
    slots = ids[0].shape[1]
    return pl.pallas_call(
        decode_kernel,
        out_shape=jax.ShapeDtypeStruct((subs * width, slots), jnp.bfloat16),
        in_specs=[pl.BlockSpec(memory_space=pltpu.VMEM)] * (len(ids) + 1),
        out_specs=pl.BlockSpec(memory_space=pltpu.VMEM),
        compiler_params=pltpu.CompilerParams(vmem_limit_bytes=8 * 1024 * 1024),
        cost_estimate=pl.CostEstimate(flops=0, bytes_accessed=2 * 1024 * 1024, transcendentals=0),
        name="decode",
    )(*ids, book_t)


def split_in_kernel(x):
    high = x.astype(jnp.bfloat16)
    return high, (x - high.astype(jnp.float32)).astype(jnp.bfloat16)


def vectors_kernel(in_ref, own_ref, other_ref, out_ref, grads_ref, flat_ref):
    rank_dim, tokens = in_ref.shape
    parts, tests, dims = out_ref.shape
    pairs = rank_dim // 2
    tall = dims // LANES
    in_side = in_ref[...]
    test_of = lax.broadcasted_iota(jnp.int32, in_side.shape, 1) // SEQ
    out_side = own_ref[...] + other_ref[...]
    in_high, in_low = split_in_kernel(in_side)
    out_high, out_low = split_in_kernel(out_side)

    def by_test(x):
        zero = jnp.zeros_like(x)
        return jnp.concatenate([jnp.where(test_of == test, x, zero) for test in range(tests)], axis=0)

    def product(x, y):
        return lax.dot_general(
            x, y, (((1,), (1,)), ((), ())), preferred_element_type=jnp.float32
        )

    wide_high = by_test(in_high)
    grads_ref[:, :rank_dim] = product(wide_high, out_high) + (
        product(wide_high, out_low) + product(by_test(in_low), out_high)
    )
    for test in range(tests):
        even = grads_ref[pl.ds(test * rank_dim, pairs, stride=2), :][:, :rank_dim]
        odd = grads_ref[pl.ds(test * rank_dim + 1, pairs, stride=2), :][:, :rank_dim]
        both = jnp.concatenate([even, odd], axis=1)
        squares = jnp.sum(jnp.sum(both * both, axis=0, keepdims=True), axis=1, keepdims=True)
        mean = squares * (1.0 / (rank_dim * rank_dim))
        flat_ref[test * pairs : (test + 1) * pairs, :] = both * (lax.rsqrt(mean + 1e-06) / rank_dim)
    for part in range(parts):
        for row in range(tall):
            out_ref[part, :, row * LANES : (row + 1) * LANES] = flat_ref[
                pl.ds(part * tall + row, tests, stride=pairs), :
            ]


def score_kernel(*refs):
    own_ref, *vector_refs, near_ref, far_ref, out_ref = refs
    tests = own_ref.shape[1]
    core = lax.axis_index("sub")
    own = lax.axis_index("dp")
    total = None
    for part, table_ref in ((core, near_ref), (1 - core, far_ref)):
        vectors = [ref[part] for ref in vector_refs]
        at = GATHER_ORDER.index(0)
        vectors[at] = jnp.where(core == 0, own_ref[part], vectors[at])
        vectors = jnp.concatenate(vectors, axis=0)
        high = vectors.astype(jnp.bfloat16)
        low = (vectors - high.astype(jnp.float32)).astype(jnp.bfloat16)
        both = jnp.dot(
            jnp.concatenate([high, low], axis=0), table_ref[...], preferred_element_type=jnp.float32
        )
        total = both if total is None else total + both
    blocks = len(vector_refs)
    total = total[: blocks * tests] + total[blocks * tests :]
    rows = [None] * blocks
    for at, xor in enumerate(GATHER_ORDER):
        rows[xor] = total[at * tests : (at + 1) * tests]
    step = 1
    while step < blocks:
        rows = [jnp.where((own & step) != 0, rows[at ^ step], rows[at]) for at in range(blocks)]
        step *= 2
    out_ref[...] = jnp.concatenate(rows, axis=0)


def score_blocks(own, blocks, near, far):
    tests = blocks[0].shape[1]
    return pl.pallas_call(
        score_kernel,
        out_shape=jax.ShapeDtypeStruct((len(blocks) * tests, near.shape[1]), jnp.float32),
        in_specs=[pl.BlockSpec(memory_space=pltpu.VMEM)] * (len(blocks) + 3),
        out_specs=pl.BlockSpec(memory_space=pltpu.VMEM),
        compiler_params=pltpu.CompilerParams(vmem_limit_bytes=8 * 1024 * 1024),
        name="score",
    )(own, *blocks, near, far)


def score(vectors, table):
    tests = vectors.shape[0]
    both = jnp.dot(
        jnp.concatenate(split_high_low(vectors), axis=0), table, preferred_element_type=jnp.float32
    )
    return both[:tests] + both[tests:]


def make_vectors(in_side, own, other, dims_local):
    rank_dim, tokens = in_side.shape
    tests = tokens // SEQ
    return pl.pallas_call(
        vectors_kernel,
        out_shape=jax.ShapeDtypeStruct((rank_dim * rank_dim // dims_local, tests, dims_local), jnp.float32),
        in_specs=[pl.BlockSpec(memory_space=pltpu.VMEM)] * 3,
        out_specs=pl.BlockSpec(memory_space=pltpu.VMEM),
        scratch_shapes=[
            pltpu.VMEM((tests * rank_dim, LANES), jnp.float32),
            pltpu.VMEM((tests * rank_dim // 2, LANES), jnp.float32),
        ],
        compiler_params=pltpu.CompilerParams(vmem_limit_bytes=4 * 1024 * 1024),
        name="vectors",
    )(in_side, own, other)


def split_high_low(x):
    high = lax.reduce_precision(x, 8, 7)
    return high.astype(jnp.bfloat16), (x - high).astype(jnp.bfloat16)


def partners(size, step):
    return [(i, i ^ step) for i in range(size)]


def is_power_of_two(n):
    return n & (n - 1) == 0


def sum_over_dp(x, sent, beside):
    size, cores = lax.axis_size("dp"), lax.axis_size("sub")
    beside = list(beside)
    made = []
    if not is_power_of_two(size):
        return lax.psum(x, "dp"), [work() for work in beside]
    steps = [1 << at for at in range(size.bit_length() - 1)]
    for steps_of_core in zip(steps, steps[::-1]):
        pairs = [
            (cores * at + core, cores * (at ^ steps_of_core[1 - core % 2]) + core)
            for at in range(size)
            for core in range(cores)
        ]
        got = lax.ppermute(sent, ("dp", "sub"), pairs)
        if beside:
            got, done = lax.optimization_barrier((got, beside.pop(0)()))
            made.append(done)
        x = x + got.astype(jnp.float32) * (1.0 / LINK_SCALE)
        sent = (x * LINK_SCALE).astype(jnp.float16)
    return x, made + [work() for work in beside]


def gather_over_dp(x):
    size = lax.axis_size("dp")
    if size > 4 or not is_power_of_two(size):
        return lax.all_gather(x, "dp", axis=0)
    own = lax.axis_index("dp")
    got = jnp.zeros((size,) + x.shape, x.dtype)
    got = lax.dynamic_update_index_in_dim(got, x, own, 0)
    for step in reversed(range(1, size)):
        block = lax.ppermute(x, "dp", partners(size, step))
        got = lax.dynamic_update_index_in_dim(got, block, own ^ step, 0)
    return got


def has_two_by_two():
    return lax.axis_size("layer") == 2 and lax.axis_size("sub") == 2


FAR_CODES = [(1, 0), (3, 2), (2, 1), (0, 3)]


def gather_by_core(x):
    size = lax.axis_size("dp")
    blocks = []
    for step in GATHER_ORDER:
        pairs = [
            (4 * at + 2 * layer + core, 4 * (at ^ step) + 2 * (layer ^ core) + core)
            for at in range(size)
            for layer in range(2)
            for core in range(2)
        ]
        if not step:
            pairs = [(i, i ^ 2) for i in range(4 * size)]
        blocks.append(lax.ppermute(x, ("dp", "layer", "sub"), pairs))
    return blocks


def per_device(acts, kv_grad, kv_weight, proj_in, proj_out, codebook, codes, counts):
    rank_dim = proj_in.shape[1]
    sub_local, code_count, sub_width = codebook.shape
    train_local = codes.shape[0]
    dims_local = sub_local * sub_width
    live_rows = jnp.arange(train_local, dtype=jnp.int32) < counts[0]

    rows_local = kv_weight.shape[1]
    own_rows = lax.optimization_barrier(
        lax.dynamic_slice_in_dim(
            jnp.transpose(proj_out), lax.axis_index("dp") * rows_local, rows_local, 1
        )
    )
    folded = jnp.dot(own_rows, kv_weight[0], preferred_element_type=jnp.float32)
    book_t = jnp.transpose(codebook, (0, 2, 1))
    by_core = has_two_by_two() and lax.axis_size("dp") == 4

    sent = (folded * LINK_SCALE).astype(jnp.float16)
    live = jnp.broadcast_to(live_rows, (8, train_local)).astype(jnp.float32)
    live, moved_codes = lax.optimization_barrier((live, codes))
    ids = make_ids(moved_codes)
    if by_core:
        sent, moved_book = lax.optimization_barrier((sent, codebook))
        near_moved = lax.ppermute(ids, "layer", partners(2, 1))
        far_ids = lax.ppermute(ids, ("layer", "sub"), FAR_CODES)
        other_book = lax.ppermute(moved_book, "sub", partners(2, 1))

    def first_side():
        return lax.dot_general(
            proj_in, acts[0], (((0,), (1,)), ((), ())), preferred_element_type=jnp.float32
        )

    def far_table():
        if not by_core:
            return decode([ids], book_t), ids
        return decode([far_ids], jnp.transpose(other_book, (0, 2, 1))), near_moved

    folded, (live, (far, near_ids)) = sum_over_dp(folded, sent, [lambda: live, far_table])
    out_side = lax.dot_general(
        jnp.concatenate(split_high_low(folded), axis=0),
        kv_grad[0],
        (((1,), (1,)), ((), ())),
        preferred_element_type=jnp.float32,
    )
    out_side = out_side[:rank_dim] + out_side[rank_dim:]
    other_side = lax.psum(out_side, "sub") - out_side if lax.axis_size("sub") != 2 else (
        lax.ppermute(out_side, "sub", partners(2, 1))
    )
    other_side, in_side = lax.optimization_barrier((other_side, first_side()))
    vectors = make_vectors(in_side, out_side, other_side, dims_local)
    sent = (vectors * VECTOR_SCALE).astype(jnp.float16)
    core = lax.axis_index("sub")
    if by_core:
        blocks = gather_by_core(sent)
        blocks[-1], own_ids, late_ids = lax.optimization_barrier((blocks[-1], ids, near_ids))
        near = decode([own_ids, late_ids], book_t)
        *blocks, near = lax.optimization_barrier((*blocks, near))
        blocks = [block.astype(jnp.float32) * (1.0 / VECTOR_SCALE) for block in blocks]
        total = score_blocks(vectors, blocks, near, far)
        total = total + lax.ppermute(total, "sub", partners(2, 1))
    else:
        every = gather_over_dp(lax.dynamic_index_in_dim(sent, core, 0, False))
        every = every.reshape(-1, dims_local).astype(jnp.float32) * (1.0 / VECTOR_SCALE)
        total = lax.psum(score(every, far), ("layer", "sub"))
    return jnp.transpose(jnp.where(live[:1] > 0.0, total, jnp.float32(0.0)))


def solution(mesh):
    return jax.shard_map(
        per_device,
        mesh=mesh,
        in_specs=(
            P("layer", ("groups", "dp"), None),
            P("layer", ("groups", "dp"), "sub"),
            P("layer", "dp", "sub"),
            P(),
            P(),
            P("sub", None, None),
            P(("groups", "dp"), "layer", "sub"),
            P(("groups", "dp")),
        ),
        out_specs=P(("groups", "dp"), None),
        check_vma=False,
    )
```
